256 devices in a mesh: gx: 16 (over y, z_hi), gy: 4 (over z_lo, core), gz: 4 (over x).
Axes of the slice: x: 4, y: 4, z: 8 (z_hi: 4, z_lo: 2; z = z_hi * 2 + z_lo), core: 2. Of those that a mesh axis runs over, the one named last changes fastest.
Arguments:
- permeability: float32 [3, 128, 32, 512], P(None, 'gx', 'gy', 'gz'), may hold values from 0.001 to 0.1
- well_flags: int32 [128, 32, 512], P('gx', 'gy', 'gz'), may hold values 0 or 1
- support_mask: int32 [8, 128, 32, 512], P(None, 'gx', 'gy', 'gz'), may hold values from 0 to 1, as said below
Outputs:
- prolongation: float32 [8, 128, 32, 512], P(None, 'gx', 'gy', 'gz')
- coarse_matrix: float32 [3, 3, 3, 16, 4, 64], P(None, None, None, 'gx', 'gy', 'gz')
The draws below stay inside these ranges and needn't reach their ends.
Inputs may be any that keep to these rules, and one draw needn't show every extreme that they name: support_mask[s] at a cell is 1 exactly where the cell lies in the support of the coarse block named by slot s at that cell; each block's support is a box that holds the block itself and reaches between 0 and half a block's edge into the neighbouring blocks on each side along each dimension, and is 0 for blocks outside the grid; so a cell's own-block slot is always 1.
All inputs are finite; a program needn't handle non-finite values. No bound on the sum of `well_flags` on one device may be relied on, other than what follows from the above.
Results may differ from the reference program's by a relative error of at most 0.0003.
Values sent between devices are 32-bit elements; how exact they have to be, the bound alone decides.
A program may use at most 128 MiB of HBM per device.

```python
import math
import jax
import jax.numpy as jnp
from jax import lax

BX = 8
BY = 8
BZ = 8
SWEEPS = 4
NX = 128
NY = 32
NZ = 512
NCX = 16
NCY = 4
NCZ = 64


def block_index_drawn(parity, coords, edge):
    owner = coords // edge
    beside = jnp.where(coords % edge < edge // 2, owner - 1, owner + 1)
    return jnp.where(owner % 2 == parity, owner, beside)


def draw_support_mask(key, part):
    edges = (BX, BY, BZ)
    totals = (NX, NY, NZ)
    block_counts = (NX // BX, NY // BY, NZ // BZ)
    reach_shape = (block_counts[0] + 2, block_counts[1] + 2, block_counts[2] + 2, 2)
    reaches = [jax.random.randint(jax.random.fold_in(key, 11 + axis_pos), reach_shape, 0, edges[axis_pos] // 2 + 1) for axis_pos in range(3)]
    shapes = [(totals[0], 1, 1), (1, totals[1], 1), (1, 1, totals[2])]
    slots = []
    for slot in range(8):
        bits = (slot >> 2 & 1, slot >> 1 & 1, slot & 1)
        block_list = []
        distance_list = []
        side_list = []
        valid = jnp.ones((1, 1, 1), dtype=bool)
        for axis_pos in range(3):
            coords = jnp.arange(totals[axis_pos], dtype=jnp.int32)
            edge = edges[axis_pos]
            owner = coords // edge
            block = block_index_drawn(bits[axis_pos], coords, edge)
            distance = jnp.where(owner > block, coords - owner * edge + 1, jnp.where(owner < block, block * edge - coords, 0))
            side = (owner > block).astype(jnp.int32)
            block_list.append(block.reshape(shapes[axis_pos]))
            distance_list.append(distance.reshape(shapes[axis_pos]))
            side_list.append(side.reshape(shapes[axis_pos]))
            valid = valid & ((block >= 0) & (block < block_counts[axis_pos])).reshape(shapes[axis_pos])
        inside = valid
        for axis_pos in range(3):
            reach = reaches[axis_pos][block_list[0] + 1, block_list[1] + 1, block_list[2] + 1, side_list[axis_pos]]
            inside = inside & (distance_list[axis_pos] <= reach)
        slots.append(inside.astype(jnp.int32))
    return jnp.stack(slots)


def set_ends(result, key, smallest, high):
    spot = [jax.random.randint(jax.random.fold_in(key, axis), (), 0, length) for axis, length in enumerate(result.shape)]
    main_axis = result.shape.index(max(result.shape))
    next_to = spot[:main_axis] + [(spot[main_axis] + 1) % result.shape[main_axis]] + spot[main_axis + 1:]
    return result.at[tuple(spot)].set(smallest).at[tuple(next_to)].set(high)


def levels(rng, shape, cuts, least, largest):
    loudness = 1.0
    for position, blocks in cuts:
        heights = jax.random.uniform(jax.random.fold_in(jax.random.fold_in(rng, 6), position), (blocks,), jnp.float32, least / len(cuts), largest / len(cuts))
        loudness = loudness * jnp.repeat(jnp.exp(heights), shape[position] // blocks).reshape((-1,) + (1,) * (len(shape) - 1 - position))
    return loudness


def setup_inputs(seed: int = 0) -> dict:
    key_of = jax.random.split(jax.random.key(seed), 4)
    permeability = jnp.clip(jnp.exp(math.log(0.1) - 4.6051702 * jax.random.uniform(key_of[0], (3, NX, NY, NZ), jnp.float32) ** levels(key_of[0], (3, NX, NY, NZ), ((1, 16), (2, 4), (3, 4)), -0.2, 0.2)), 0.001, 0.1)
    well_flags = set_ends((jax.random.randint(key_of[1], (NX, NY, NZ), 0, 16) < 1).astype(jnp.int32), jax.random.fold_in(key_of[1], 1), 0, 1)
    support_mask = draw_support_mask(jax.random.fold_in(key_of[3], 71), 0)
    return {"permeability": permeability, "well_flags": well_flags, "support_mask": support_mask}


relaxation = 2.0 / 3.0
well_index = 0.05


def block_index(parity, coords, edge):
    owner = coords // edge
    beside = jnp.where(coords % edge < edge // 2, owner - 1, owner + 1)
    return jnp.where(owner % 2 == parity, owner, beside)


def both_blocks(coords, edge):
    return jnp.stack([block_index(0, coords, edge), block_index(1, coords, edge)])


def harmonic(values, inside, axis):
    count = values.shape[axis]
    lower = lax.slice_in_dim(values, 0, count - 1, axis=axis)
    upper = lax.slice_in_dim(values, 1, count, axis=axis)
    both_in = lax.slice_in_dim(inside, 0, count - 1, axis=axis) * lax.slice_in_dim(inside, 1, count, axis=axis)
    return 2.0 * lower * upper * both_in / (lower + upper + 1.0 - both_in)


def prepare(padded_perm, flags, anchor, totals, edges):
    shape_pad = padded_perm.shape[1:]
    coord_list = [anchor[axis_pos] + jnp.arange(shape_pad[axis_pos], dtype=jnp.int32) for axis_pos in range(3)]
    inside_list = [((coord_list[axis_pos] >= 0) & (coord_list[axis_pos] < totals[axis_pos])).astype(jnp.float32) for axis_pos in range(3)]
    inside_box = inside_list[0][:, None, None] * inside_list[1][None, :, None] * inside_list[2][None, None, :]
    trans_x = harmonic(padded_perm[0][:, 1:-1, 1:-1], inside_box[:, 1:-1, 1:-1], 0)
    trans_y = harmonic(padded_perm[1][1:-1, :, 1:-1], inside_box[1:-1, :, 1:-1], 1)
    trans_z = harmonic(padded_perm[2][1:-1, 1:-1, :], inside_box[1:-1, 1:-1, :], 2)
    same_list = []
    for axis_pos in range(3):
        blocks = both_blocks(coord_list[axis_pos], edges[axis_pos])
        same_list.append((blocks[:, :-1] == blocks[:, 1:]).astype(jnp.float32))
    diagonal = trans_x[:-1] + trans_x[1:] + trans_y[:, :-1] + trans_y[:, 1:] + trans_z[:, :, :-1] + trans_z[:, :, 1:]
    diagonal = diagonal + well_index * flags + 1.0 - inside_box[1:-1, 1:-1, 1:-1]
    return (trans_x, trans_y, trans_z), tuple(same_list), diagonal


def operate(padded8, faces, same_list, diagonal):
    padded = padded8.reshape((2, 2, 2) + padded8.shape[1:])
    trans_x, trans_y, trans_z = faces
    weight_x = same_list[0][:, None, None, :, None, None] * trans_x
    weight_y = same_list[1][None, :, None, None, :, None] * trans_y
    weight_z = same_list[2][None, None, :, None, None, :] * trans_z
    center = padded[:, :, :, 1:-1, 1:-1, 1:-1]
    flow = weight_x[:, :, :, :-1] * padded[:, :, :, :-2, 1:-1, 1:-1]
    flow = flow + weight_x[:, :, :, 1:] * padded[:, :, :, 2:, 1:-1, 1:-1]
    flow = flow + weight_y[:, :, :, :, :-1] * padded[:, :, :, 1:-1, :-2, 1:-1]
    flow = flow + weight_y[:, :, :, :, 1:] * padded[:, :, :, 1:-1, 2:, 1:-1]
    flow = flow + weight_z[..., :-1] * padded[:, :, :, 1:-1, 1:-1, :-2]
    flow = flow + weight_z[..., 1:] * padded[:, :, :, 1:-1, 1:-1, 2:]
    return center, diagonal * center - flow


def smooth(padded8, faces, same_list, diagonal, support8):
    center, image = operate(padded8, faces, same_list, diagonal)
    support = support8.reshape(center.shape)
    update = -relaxation * support * image / diagonal
    update_sum = jnp.sum(update, axis=(0, 1, 2), keepdims=True)
    fresh = center + update - center * update_sum
    return fresh.reshape((8,) + fresh.shape[3:])


def initial_basis(anchor, counts, edges):
    hot_list = []
    for axis_pos in range(3):
        coords = anchor[axis_pos] + jnp.arange(counts[axis_pos], dtype=jnp.int32)
        parity = (coords // edges[axis_pos]) % 2
        hot_list.append((parity[None, :] == jnp.arange(2, dtype=jnp.int32)[:, None]).astype(jnp.float32))
    basis = hot_list[0][:, None, None, :, None, None] * hot_list[1][None, :, None, None, :, None] * hot_list[2][None, None, :, None, None, :]
    return basis.reshape((8,) + tuple(counts))


def row_table(coords, edge, base, count):
    blocks = both_blocks(coords, edge)
    offset = blocks[None, :, :] - blocks[:, None, :]
    offset_hit = offset[:, :, None, :] == (jnp.arange(3, dtype=jnp.int32) - 1)[None, None, :, None]
    rows_hit = (blocks[:, :, None] - base) == jnp.arange(count, dtype=jnp.int32)[None, None, :]
    return (offset_hit[..., None] & rows_hit[:, None, None, :, :]).astype(jnp.float32)


def contract(center, image, table_x, table_y, table_z):
    products = center[:, :, :, None, None, None] * image[None, None, None]
    first = jnp.einsum("abcdefijk,cfzkq->abdeijzq", products, table_z, precision=lax.Precision.HIGHEST)
    second = jnp.einsum("abdeijzq,beyjr->adiyrzq", first, table_y, precision=lax.Precision.HIGHEST)
    return jnp.einsum("adiyrzq,adxip->xyzprq", second, table_x, precision=lax.Precision.HIGHEST)


def reference(permeability, well_flags, support_mask):
    totals = (NX, NY, NZ)
    edges = (BX, BY, BZ)
    pad_cells = ((0, 0), (1, 1), (1, 1), (1, 1))
    padded_perm = jnp.pad(permeability, pad_cells)
    faces, same_list, diagonal = prepare(padded_perm, well_flags.astype(jnp.float32), (-1, -1, -1), totals, edges)
    support8 = support_mask.astype(jnp.float32)
    prolongation = initial_basis((0, 0, 0), totals, edges)
    for sweep_index in range(SWEEPS):
        prolongation = smooth(jnp.pad(prolongation, pad_cells), faces, same_list, diagonal, support8)
    center, image = operate(jnp.pad(prolongation, pad_cells), faces, same_list, diagonal)
    table_y = row_table(jnp.arange(NY, dtype=jnp.int32), BY, 0, NCY)
    table_z = row_table(jnp.arange(NZ, dtype=jnp.int32), BZ, 0, NCZ)

    def slab(running, slab_index):
        start = (slab_index * BX).astype(jnp.int32)
        coords = start + jnp.arange(BX, dtype=jnp.int32)
        table_x = row_table(coords, BX, 0, NCX)
        part_center = lax.dynamic_slice_in_dim(center, start, BX, axis=3)
        part_image = lax.dynamic_slice_in_dim(image, start, BX, axis=3)
        return running + contract(part_center, part_image, table_x, table_y, table_z), None

    start_value = jnp.zeros((3, 3, 3, NCX, NCY, NCZ), jnp.float32)
    coarse_matrix, unused = lax.scan(slab, start_value, jnp.arange(NCX, dtype=jnp.int32))
    return prolongation, coarse_matrix
```

```python
import jax
import jax.numpy as jnp
from jax import lax
from jax.experimental import pallas as pl
from jax.experimental.pallas import tpu as pltpu
from jax.sharding import PartitionSpec as P

MESH = pl.DeviceIdType.MESH
AXES = ("gx", "gy", "gz")
COUNT = {"gx": 16, "gy": 4, "gz": 4}
SWEEPS = 4
STEP = 2.0 / 3.0
WELL = 0.05
E = 8
LANES = 128
ROW0 = 8


def harmonic(lower, upper):
    return 2.0 * lower * upper / (lower + upper)


def kernel(
    perm, flags, mask, out_p, out_c,
    kx, ky, kz, kz_send, kz_halo, fl, mk, basis, z_send, z_halo,
    vx, vy, vz, negdiag, part, pz, iz, sums, rows, rows_x, rows_y, rows_d, zr_send, zr_halo,
    load_sem, k_send, k_recv, p_send, p_recv, zr_ssem, zr_rsem, r_send, r_recv, out_sem,
):
    at = {axis: lax.axis_index(axis) for axis in AXES}
    has = {}
    for axis in AXES:
        has[axis, 1] = at[axis] < COUNT[axis] - 1
        has[axis, -1] = at[axis] > 0
    par_x, par_y = lax.rem(at["gx"], 2), lax.rem(at["gy"], 2)
    lane = lax.broadcasted_iota(jnp.int32, (E, LANES), 1)
    row = lax.broadcasted_iota(jnp.int32, (E, LANES), 0)
    even = lax.rem(lane // E, 2) == 0

    loads = [
        pltpu.make_async_copy(perm.at[0], kx.at[pl.ds(1, E)], load_sem.at[0]),
        pltpu.make_async_copy(perm.at[1], ky.at[:, pl.ds(ROW0, E)], load_sem.at[1]),
        pltpu.make_async_copy(perm.at[2], kz, load_sem.at[2]),
        pltpu.make_async_copy(flags, fl, load_sem.at[3]),
        pltpu.make_async_copy(mask, mk, load_sem.at[4]),
    ]
    for load in loads:
        load.start()

    barrier = pltpu.get_barrier_semaphore()
    expected = 0
    for axis in AXES:
        for d in (1, -1):
            @pl.when(has[axis, d])
            def _():
                pl.semaphore_signal(
                    barrier, inc=1, device_id={axis: at[axis] + d}, device_id_type=MESH
                )
            expected = expected + has[axis, d].astype(jnp.int32)

    def shift_to(axis, d):
        size = COUNT[axis]
        return lax.rem(at[axis] + d + size, size)

    class Copy:
        def __init__(self, src, dst, ssem, rsem, moves):
            self.send_if = None
            self.recv_if = None
            target = {}
            for axis, d in moves:
                target[axis] = shift_to(axis, d)
                s, r = has[axis, d], has[axis, -d]
                self.send_if = s if self.send_if is None else self.send_if & s
                self.recv_if = r if self.recv_if is None else self.recv_if & r
            self.copy = pltpu.make_async_remote_copy(
                src_ref=src, dst_ref=dst, send_sem=ssem, recv_sem=rsem,
                device_id=target, device_id_type=MESH,
            )

        def start(self):
            pl.when(self.send_if)(self.copy.start)

        def wait_recv(self):
            pl.when(self.recv_if)(self.copy.wait_recv)

        def wait_send(self):
            pl.when(self.send_if)(self.copy.wait_send)

    started = []

    def start(copies):
        for c in copies:
            c.start()
        started.extend(copies)

    def fill(i, carry):
        s, x = i // 10, lax.rem(i, 10)
        bx, by, bz = s // 4, lax.rem(s // 2, 2), lax.rem(s, 2)
        block_x = jnp.where((x == 0) | (x == 9), 1 - par_x, par_x)
        hot_x = (bx == block_x).astype(jnp.float32)
        own_y = (by == par_y).astype(jnp.float32)
        hot_z = jnp.where(lax.rem(lane // E, 2) == bz, hot_x, 0.0)
        basis[0, s, x, 0:8] = hot_z * (1.0 - own_y)
        basis[0, s, x, 8:16] = hot_z * own_y
        basis[0, s, x, 16:24] = hot_z * (1.0 - own_y)
        return carry

    lax.fori_loop(0, 80, fill, 0)
    slot = lane // E
    hot_xy = (slot // 4 == par_x) & (lax.rem(slot // 2, 2) == par_y)
    for side in range(2):
        z_halo[0, side] = jnp.where(hot_xy & (lax.rem(slot, 2) == 1 - side), 1.0, 0.0)

    zero = jnp.zeros((E, LANES), jnp.float32)
    for d, k_plane in ((-1, 0), (1, 9)):
        side = (d + 1) // 2

        @pl.when(jnp.logical_not(has["gx", d]))
        def _():
            kx[k_plane] = zero
            for k in range(1, SWEEPS + 1):
                basis[k, :, k_plane, 8:16] = jnp.zeros((8, E, LANES), jnp.float32)
            rows_x[side] = jnp.zeros((2, E, LANES), jnp.float32)

        @pl.when(jnp.logical_not(has["gy", d]))
        def _():
            y_row = 7 if d < 0 else 16
            ky[:, y_row:y_row + 1] = jnp.zeros((E, 1, LANES), jnp.float32)

            def clear(i, carry):
                basis[1 + i // 8, lax.rem(i, 8), 1:9, y_row:y_row + 1] = jnp.zeros(
                    (E, 1, LANES), jnp.float32
                )
                return carry

            lax.fori_loop(0, 8 * SWEEPS, clear, 0)
            rows_y[side] = jnp.zeros((2, E, LANES), jnp.float32)

        @pl.when(jnp.logical_not(has["gz", d]))
        def _():
            kz_halo[side] = zero
            for k in range(1, SWEEPS + 1):
                z_halo[k, side] = zero
            zr_halo[side] = zero

        for e in (1, -1):
            @pl.when(jnp.logical_not(has["gx", d] & has["gy", e]))
            def _():
                rows_d[side, (e + 1) // 2] = zero

    for load in loads[:3]:
        load.wait()
    for side in range(2):
        tile = zero
        for x in range(E):
            shift = (x - 127) % LANES if side == 0 else x
            moved = pltpu.roll(kz[x], shift, 1) if shift else kz[x]
            tile = jnp.where(lane == x, moved, tile)
        kz_send[side] = tile
    pl.semaphore_wait(barrier, expected)
    k_x = [
        Copy(kx.at[8], kx.at[0], k_send.at[0], k_recv.at[0], (("gx", 1),)),
        Copy(kx.at[1], kx.at[9], k_send.at[1], k_recv.at[1], (("gx", -1),)),
    ]
    k_yz = [
        Copy(ky.at[:, pl.ds(15, 1)], ky.at[:, pl.ds(7, 1)], k_send.at[2], k_recv.at[2], (("gy", 1),)),
        Copy(ky.at[:, pl.ds(8, 1)], ky.at[:, pl.ds(16, 1)], k_send.at[3], k_recv.at[3], (("gy", -1),)),
        Copy(kz_send.at[0], kz_halo.at[0], k_send.at[4], k_recv.at[4], (("gz", 1),)),
        Copy(kz_send.at[1], kz_halo.at[1], k_send.at[5], k_recv.at[5], (("gz", -1),)),
    ]
    start(k_x)
    start(k_yz)

    def weights(x):
        here = kx[x + 1]
        t_x = (harmonic(kx[x], here), harmonic(here, kx[x + 2]))
        here = ky[x, 8:16]
        t_y = (harmonic(ky[x, 7:15], here), harmonic(here, ky[x, 9:17]))
        here = kz[x]
        before = jnp.where(
            lane == 0, pltpu.roll(kz_halo[0], LANES - x, 1), pltpu.roll(here, 1, 1)
        )
        after = jnp.where(
            lane == 127, pltpu.roll(kz_halo[1], 127 - x, 1), pltpu.roll(here, 127, 1)
        )
        t_z = (harmonic(before, here), harmonic(here, after))
        diagonal = t_x[0] + t_x[1] + t_y[0] + t_y[1] + t_z[0] + t_z[1]
        diagonal = diagonal + WELL * fl[x].astype(jnp.float32)
        negdiag[x] = -1.5 * diagonal
        scale = STEP / diagonal
        for b in range(2):
            keep_x = (par_x == b).astype(jnp.float32)
            keep_y = (par_y == b).astype(jnp.float32)
            own_z = even if b == 0 else jnp.logical_not(even)
            for side in range(2):
                inner = 4 - side
                vx[b, side, x] = t_x[side] * scale * jnp.where(x == inner, keep_x, 1.0)
                vy[b, side, x] = t_y[side] * scale * jnp.where(row == inner, keep_y, 1.0)
                cut = (lax.rem(lane, E) == inner) & jnp.logical_not(own_z)
                vz[b, side, x] = jnp.where(cut, 0.0, t_z[side] * scale)

    def center_of(k, x):
        return basis[k, :, x + 1, 8:16].reshape(2, 2, 2, E, LANES)

    def flow_x(k, x, side):
        near = basis[k, :, x + 2 * side, 8:16].reshape(2, 2, 2, E, LANES)
        return vx[:, side, x][:, None, None] * near

    def flow_yz(k, x):
        center = basis[k, :, x + 1, 8:16]
        total = -STEP * center.reshape(2, 2, 2, E, LANES)
        for side in range(2):
            near = basis[k, :, x + 1, 7 + 2 * side:15 + 2 * side].reshape(2, 2, 2, E, LANES)
            total = total + vy[:, side, x][None, :, None] * near
            edge = lane == (0, 127)[side]
            halo = z_halo[k, side]
            moved = []
            for s in range(8):
                place = s * 8 + x
                shift = LANES - place if side == 0 else 127 - place
                moved.append(
                    jnp.where(
                        edge,
                        pltpu.roll(halo, shift, 1),
                        pltpu.roll(center[s], (1, 127)[side], 1),
                    )
                )
            near = jnp.stack(moved).reshape(2, 2, 2, E, LANES)
            total = total + vz[:, side, x][None, None] * near
        return total

    def update(k, x, flow):
        center = center_of(k, x)
        support = mk[:, x].astype(jnp.float32).reshape(2, 2, 2, E, LANES)
        change = support * flow
        change_sum = jnp.sum(change, axis=(0, 1, 2))
        fresh = center + change - center * change_sum
        basis[k + 1, :, x + 1, 8:16] = fresh.reshape(8, E, LANES)

    def pack_z(k, x, tiles):
        up, down = tiles
        for s in range(8):
            place = s * 8 + x
            value = basis[k, s, x + 1, 8:16]
            up = jnp.where(lane == place, pltpu.roll(value, place + 1, 1), up)
            down = jnp.where(lane == place, pltpu.roll(value, place, 1), down)
        return up, down

    def copies(k):
        ref = basis.at[k]
        own = pl.ds(8, E)
        planes = pl.ds(1, E)
        sems = [(p_send.at[k, i], p_recv.at[k, i]) for i in range(6)]
        x = [
            Copy(ref.at[:, 8, own], ref.at[:, 0, own], *sems[0], (("gx", 1),)),
            Copy(ref.at[:, 1, own], ref.at[:, 9, own], *sems[1], (("gx", -1),)),
        ]
        yz = [
            Copy(ref.at[:, planes, pl.ds(15, 1)], ref.at[:, planes, pl.ds(7, 1)], *sems[2], (("gy", 1),)),
            Copy(ref.at[:, planes, pl.ds(8, 1)], ref.at[:, planes, pl.ds(16, 1)], *sems[3], (("gy", -1),)),
            Copy(z_send.at[k, 0], z_halo.at[k, 0], *sems[4], (("gz", 1),)),
            Copy(z_send.at[k, 1], z_halo.at[k, 1], *sems[5], (("gz", -1),)),
        ]
        return x, yz

    def inner_flow(k, x):
        return flow_yz(k, x) + flow_x(k, x, 0) + flow_x(k, x, 1)

    arriving_x, arriving_yz = k_x, k_yz
    for k in range(SWEEPS):
        for c in arriving_yz:
            c.wait_recv()
        if k == 0:
            for load in loads[3:]:
                load.wait()

            def prepare(x, carry):
                weights(x)
                return carry

            lax.fori_loop(1, 7, prepare, 0)

        def inner(x, tiles):
            update(k, x, inner_flow(k, x))
            return pack_z(k + 1, x, tiles)

        tiles = lax.fori_loop(1, 7, inner, (zero, zero))
        if k > 0:
            for x, side in ((0, 1), (7, 0)):
                part[1 - side] = (flow_yz(k, x) + flow_x(k, x, side)).reshape(8, E, LANES)
        for c in arriving_x:
            c.wait_recv()
        arriving_x, arriving_yz = copies(k + 1)
        for x, side in ((0, 0), (7, 1)):
            if k == 0:
                weights(x)
                flow = inner_flow(k, x)
            else:
                flow = part[side].reshape(2, 2, 2, E, LANES) + flow_x(k, x, side)
            update(k, x, flow)
        start(arriving_x)
        for x in (0, 7):
            tiles = pack_z(k + 1, x, tiles)
        z_send[k + 1, 0], z_send[k + 1, 1] = tiles
        start(arriving_yz)

    out = pltpu.make_async_copy(
        basis.at[SWEEPS, :, pl.ds(1, E), pl.ds(8, E)], out_p, out_sem.at[0]
    )
    out.start()

    def split_z(values):
        pair = values.reshape(4, 2, E, LANES)
        return (
            jnp.where(even, pair[:, 0], pair[:, 1]),
            jnp.where(even, pair[:, 1], pair[:, 0]),
        )

    def image(x, flow):
        own, beside = split_z(flow * negdiag[x])
        iz[:, 0, x] = own
        iz[:, 1, x] = beside

    def split_basis(x, carry):
        own, beside = split_z(center_of(SWEEPS, x))
        pz[:, 0, x] = own
        pz[:, 1, x] = beside
        return carry

    lax.fori_loop(0, E, split_basis, 0)
    for c in arriving_yz:
        c.wait_recv()

    def inner_image(x, carry):
        image(x, inner_flow(SWEEPS, x))
        return carry

    lax.fori_loop(1, 7, inner_image, 0)
    for x, side in ((0, 1), (7, 0)):
        part[1 - side] = (flow_yz(SWEEPS, x) + flow_x(SWEEPS, x, side)).reshape(8, E, LANES)

    def contract(first):
        def body(i, carry):
            half, a_x, a_y = i // 4, lax.rem(i // 2, 2), lax.rem(i, 2)
            s_xy = lax.rem(a_x + par_x, 2) * 2 + lax.rem(a_y + par_y, 2)
            planes = [1 + 3 * half + j for j in range(3)] if first else [7 * half]
            for a_z in range(2):
                for e_x in range(2):
                    for e_y in range(2):
                        u_xy = lax.rem(a_x + e_x + par_x, 2) * 2 + lax.rem(a_y + e_y + par_y, 2)
                        for e_z in range(2):
                            e = e_x * 4 + e_y * 2 + e_z
                            base = pl.multiple_of((i * 2 + a_z) * 64, 64) + e * 8
                            total = None if first else sums[pl.ds(base, E)]
                            for x in planes:
                                term = pz[s_xy, a_z, x] * iz[u_xy, (a_z + e_z) % 2, x]
                                total = term if total is None else total + term
                            sums[pl.ds(base, E)] = total
            return carry

        lax.fori_loop(0, 8, body, 0)

    contract(True)
    for c in arriving_x:
        c.wait_recv()
    for x, side in ((0, 0), (7, 1)):
        image(x, part[side].reshape(2, 2, 2, E, LANES) + flow_x(SWEEPS, x, side))
    contract(False)

    quarter = []
    for y_half in range(2):
        total = sums[pl.ds(4 * y_half, LANES, stride=8)]
        for y in range(1, 4):
            total = total + sums[pl.ds(4 * y_half + y, LANES, stride=8)]
        total = total.reshape(16, E, LANES)
        total = total + pltpu.roll(total, 127, 2)
        total = total + pltpu.roll(total, 126, 2)
        quarter.append(total.reshape(8, 2, E, LANES))
    up, down = zero, zero
    for i in range(8):
        for y_half in range(2):
            place = i * 2 + y_half
            beside = quarter[y_half][i, 1]
            up = jnp.where(lane == place, pltpu.roll(beside, place + 4, 1), up)
            moved = pltpu.roll(beside, place, 1) if place else beside
            down = jnp.where(lane == place, moved, down)
    zr_send[0], zr_send[1] = up, down
    zr = [
        Copy(zr_send.at[0], zr_halo.at[0], zr_ssem.at[0], zr_rsem.at[0], (("gz", 1),)),
        Copy(zr_send.at[1], zr_halo.at[1], zr_ssem.at[1], zr_rsem.at[1], (("gz", -1),)),
    ]
    start(zr)
    low = (lax.rem(lane, E) == 0) & (lane != 0)
    high = (lax.rem(lane, E) == 4) & (lane != 124)
    merged = []
    for y_half in range(2):
        own, beside = quarter[y_half][:, 0], quarter[y_half][:, 1]
        own = own + jnp.where(low, pltpu.roll(beside, 4, 2), 0.0)
        merged.append(own + jnp.where(high, pltpu.roll(beside, 124, 2), 0.0))
    for c in zr:
        c.wait_recv()
    from_below, from_above = zr_halo[0], zr_halo[1]
    for i in range(8):
        for y_half in range(2):
            place = i * 2 + y_half
            moved = pltpu.roll(from_below, LANES - place, 1) if place else from_below
            total = merged[y_half][i] + jnp.where(lane == 0, moved, 0.0)
            total = total + jnp.where(lane == 124, pltpu.roll(from_above, 124 - place, 1), 0.0)
            rows[i // 2 % 2, i % 2, i // 4, y_half] = total

    row_copies = []
    for side, d in ((0, 1), (1, -1)):
        half = 1 - side
        row_copies.append(Copy(rows.at[1, 0, half], rows_x.at[side], r_send.at[side], r_recv.at[side], (("gx", d),)))
        row_copies.append(Copy(rows.at[0, 1, :, half], rows_y.at[side], r_send.at[2 + side], r_recv.at[2 + side], (("gy", d),)))
        for side_y, d_y in ((0, 1), (1, -1)):
            n = 4 + side * 2 + side_y
            row_copies.append(Copy(
                rows.at[1, 1, half, 1 - side_y], rows_d.at[side, side_y], r_send.at[n], r_recv.at[n],
                (("gx", d), ("gy", d_y)),
            ))
    start(row_copies)
    for c in row_copies:
        c.wait_recv()
    whole = [
        [rows[0, 0, h, y] + rows_x[h, y] + rows_y[y, h] + rows_d[h, y] for y in range(2)] for h in range(2)
    ]
    tiles = jnp.stack([whole[0][0], whole[0][1], whole[1][0], whole[1][1]])
    lows, highs = tiles, pltpu.roll(tiles, 124, 2)
    for b in range(4):
        inside = lax.rem(lane, 2 ** (b + 4))
        takes = (inside >= 2**b) & (inside < 2 ** (b + 1))
        lows = jnp.where(takes, pltpu.roll(lows, LANES - 7 * 2**b, 2), lows)
        highs = jnp.where(takes, pltpu.roll(highs, LANES - 7 * 2**b, 2), highs)
    picks = {0: ((0,), 1), 1: ((0, 1), 0), 2: ((1,), 1)}
    for d_x in range(3):
        for d_y in range(3):
            (halves_x, e_x), (halves_y, e_y) = picks[d_x], picks[d_y]
            low_tile, high_tile = None, None
            for h in halves_x:
                for y in halves_y:
                    n = h * 2 + y
                    low_tile = lows[n] if low_tile is None else low_tile + lows[n]
                    high_tile = highs[n] if high_tile is None else high_tile + highs[n]
            e = e_x * 4 + e_y * 2
            out_row = (d_x * 3 + d_y) * 3
            out_c[out_row:out_row + 1, :] = low_tile[e + 1:e + 2, :16]
            out_c[out_row + 1:out_row + 2, :] = low_tile[e:e + 1, :16] + high_tile[e:e + 1, :16]
            out_c[out_row + 2:out_row + 3, :] = high_tile[e + 1:e + 2, :16]
    out.wait()
    for c in started:
        c.wait_send()


def shards(permeability, well_flags, support_mask):
    f32 = jnp.float32
    vmem = pltpu.VMEM
    dma = pltpu.SemaphoreType.DMA
    any_spec = pl.BlockSpec(memory_space=pltpu.HBM)
    prolongation, coarse = pl.pallas_call(
        kernel,
        out_shape=(
            jax.ShapeDtypeStruct((8, E, E, LANES), f32),
            jax.ShapeDtypeStruct((27, 16), f32),
        ),
        in_specs=[any_spec] * 3,
        out_specs=(any_spec, pl.BlockSpec(memory_space=pltpu.VMEM)),
        scratch_shapes=[
            vmem((10, E, LANES), f32),
            vmem((E, 24, LANES), f32),
            vmem((E, E, LANES), f32),
            vmem((2, E, LANES), f32),
            vmem((2, E, LANES), f32),
            vmem((E, E, LANES), jnp.int32),
            vmem((8, E, E, LANES), jnp.int32),
            vmem((SWEEPS + 1, 8, 10, 24, LANES), f32),
            vmem((SWEEPS + 1, 2, E, LANES), f32),
            vmem((SWEEPS + 1, 2, E, LANES), f32),
            vmem((2, 2, E, E, LANES), f32),
            vmem((2, 2, E, E, LANES), f32),
            vmem((2, 2, E, E, LANES), f32),
            vmem((E, E, LANES), f32),
            vmem((2, 8, E, LANES), f32),
            vmem((4, 2, E, E, LANES), f32),
            vmem((4, 2, E, E, LANES), f32),
            vmem((1024, LANES), f32),
            vmem((2, 2, 2, 2, E, LANES), f32),
            vmem((2, 2, E, LANES), f32),
            vmem((2, 2, E, LANES), f32),
            vmem((2, 2, E, LANES), f32),
            vmem((2, E, LANES), f32),
            vmem((2, E, LANES), f32),
            dma((5,)),
            dma((6,)),
            dma((6,)),
            dma((SWEEPS + 1, 6)),
            dma((SWEEPS + 1, 6)),
            dma((2,)),
            dma((2,)),
            dma((8,)),
            dma((8,)),
            dma((1,)),
        ],
        compiler_params=pltpu.CompilerParams(
            collective_id=0, has_side_effects=True, vmem_limit_bytes=60 * 1024 * 1024
        ),
        name="smooth_and_contract",
    )(permeability, well_flags, support_mask)
    return prolongation, coarse.reshape(3, 3, 3, 1, 1, 16)


def solution(mesh):
    placed = (P(None, "gx", "gy", "gz"), P("gx", "gy", "gz"), P(None, "gx", "gy", "gz"))
    return jax.shard_map(
        shards,
        mesh=mesh,
        in_specs=placed,
        out_specs=(P(None, "gx", "gy", "gz"), P(None, None, None, "gx", "gy", "gz")),
        check_vma=False,
    )
```

```python
import jax
import jax.numpy as jnp
from jax import lax
from jax.experimental import pallas as pl
from jax.experimental.pallas import tpu as pltpu
from jax.sharding import PartitionSpec as P

MESH = pl.DeviceIdType.MESH
AXES = ("gx", "gy", "gz")
COUNT = {"gx": 16, "gy": 4, "gz": 4}
SWEEPS = 4
STEP = 2.0 / 3.0
WELL = 0.05
E = 8
LANES = 128
ROW0 = 8


def harmonic(lower, upper):
    return 2.0 * lower * upper / (lower + upper)


def kernel(
    perm, flags, mask, out_p, out_c,
    kx, ky, kz, kz_send, kz_halo, fl, mk, basis, z_send, z_halo,
    vx, vy, vz, negdiag, part, pz, iz, sums, rows, rows_x, rows_y, rows_d, zr_send, zr_halo,
    load_sem, k_send, k_recv, p_send, p_recv, zr_ssem, zr_rsem, r_send, r_recv, out_sem,
):
    at = {axis: lax.axis_index(axis) for axis in AXES}
    has = {}
    for axis in AXES:
        has[axis, 1] = at[axis] < COUNT[axis] - 1
        has[axis, -1] = at[axis] > 0
    par_x, par_y = lax.rem(at["gx"], 2), lax.rem(at["gy"], 2)
    lane = lax.broadcasted_iota(jnp.int32, (E, LANES), 1)
    row = lax.broadcasted_iota(jnp.int32, (E, LANES), 0)
    even = lax.rem(lane // E, 2) == 0

    loads = [
        pltpu.make_async_copy(perm.at[0], kx.at[pl.ds(1, E)], load_sem.at[0]),
        pltpu.make_async_copy(perm.at[1], ky.at[:, pl.ds(ROW0, E)], load_sem.at[1]),
        pltpu.make_async_copy(perm.at[2], kz, load_sem.at[2]),
        pltpu.make_async_copy(flags, fl, load_sem.at[3]),
        pltpu.make_async_copy(mask, mk, load_sem.at[4]),
    ]
    for load in loads:
        load.start()

    barrier = pltpu.get_barrier_semaphore()
    expected = 0
    for axis in AXES:
        for d in (1, -1):
            @pl.when(has[axis, d])
            def _():
                pl.semaphore_signal(
                    barrier, inc=1, device_id={axis: at[axis] + d}, device_id_type=MESH
                )
            expected = expected + has[axis, d].astype(jnp.int32)

    def shift_to(axis, d):
        size = COUNT[axis]
        return lax.rem(at[axis] + d + size, size)

    class Copy:
        def __init__(self, src, dst, ssem, rsem, moves):
            self.send_if = None
            self.recv_if = None
            target = {}
            for axis, d in moves:
                target[axis] = shift_to(axis, d)
                s, r = has[axis, d], has[axis, -d]
                self.send_if = s if self.send_if is None else self.send_if & s
                self.recv_if = r if self.recv_if is None else self.recv_if & r
            self.copy = pltpu.make_async_remote_copy(
                src_ref=src, dst_ref=dst, send_sem=ssem, recv_sem=rsem,
                device_id=target, device_id_type=MESH,
            )

        def start(self):
            pl.when(self.send_if)(self.copy.start)

        def wait_recv(self):
            pl.when(self.recv_if)(self.copy.wait_recv)

        def wait_send(self):
            pl.when(self.send_if)(self.copy.wait_send)

    started = []

    def start(copies):
        for c in copies:
            c.start()
        started.extend(copies)

    def fill(i, carry):
        s, x = i // 10, lax.rem(i, 10)
        bx, by, bz = s // 4, lax.rem(s // 2, 2), lax.rem(s, 2)
        block_x = jnp.where((x == 0) | (x == 9), 1 - par_x, par_x)
        hot_x = (bx == block_x).astype(jnp.float32)
        own_y = (by == par_y).astype(jnp.float32)
        hot_z = jnp.where(lax.rem(lane // E, 2) == bz, hot_x, 0.0)
        basis[0, s, x, 0:8] = hot_z * (1.0 - own_y)
        basis[0, s, x, 8:16] = hot_z * own_y
        basis[0, s, x, 16:24] = hot_z * (1.0 - own_y)
        return carry

    lax.fori_loop(0, 80, fill, 0)
    slot = lane // E
    hot_xy = (slot // 4 == par_x) & (lax.rem(slot // 2, 2) == par_y)
    for side in range(2):
        z_halo[0, side] = jnp.where(hot_xy & (lax.rem(slot, 2) == 1 - side), 1.0, 0.0)

    zero = jnp.zeros((E, LANES), jnp.float32)
    for d, k_plane in ((-1, 0), (1, 9)):
        side = (d + 1) // 2

        @pl.when(jnp.logical_not(has["gx", d]))
        def _():
            kx[k_plane] = zero
            for k in range(1, SWEEPS + 1):
                basis[k, :, k_plane, 8:16] = jnp.zeros((8, E, LANES), jnp.float32)
            rows_x[side] = jnp.zeros((2, E, LANES), jnp.float32)

        @pl.when(jnp.logical_not(has["gy", d]))
        def _():
            y_row = 7 if d < 0 else 16
            ky[:, y_row:y_row + 1] = jnp.zeros((E, 1, LANES), jnp.float32)

            def clear(i, carry):
                basis[1 + i // 8, lax.rem(i, 8), 1:9, y_row:y_row + 1] = jnp.zeros(
                    (E, 1, LANES), jnp.float32
                )
                return carry

            lax.fori_loop(0, 8 * SWEEPS, clear, 0)
            rows_y[side] = jnp.zeros((2, E, LANES), jnp.float32)

        @pl.when(jnp.logical_not(has["gz", d]))
        def _():
            kz_halo[side] = zero
            for k in range(1, SWEEPS + 1):
                z_halo[k, side] = zero
            zr_halo[side] = zero

        for e in (1, -1):
            @pl.when(jnp.logical_not(has["gx", d] & has["gy", e]))
            def _():
                rows_d[side, (e + 1) // 2] = zero

    for load in loads[:3]:
        load.wait()
    for side in range(2):
        tile = zero
        for x in range(E):
            shift = (x - 127) % LANES if side == 0 else x
            moved = pltpu.roll(kz[x], shift, 1) if shift else kz[x]
            tile = jnp.where(lane == x, moved, tile)
        kz_send[side] = tile
    pl.semaphore_wait(barrier, expected)
    k_x = [
        Copy(kx.at[8], kx.at[0], k_send.at[0], k_recv.at[0], (("gx", 1),)),
        Copy(kx.at[1], kx.at[9], k_send.at[1], k_recv.at[1], (("gx", -1),)),
    ]
    k_yz = [
        Copy(ky.at[:, pl.ds(15, 1)], ky.at[:, pl.ds(7, 1)], k_send.at[2], k_recv.at[2], (("gy", 1),)),
        Copy(ky.at[:, pl.ds(8, 1)], ky.at[:, pl.ds(16, 1)], k_send.at[3], k_recv.at[3], (("gy", -1),)),
        Copy(kz_send.at[0], kz_halo.at[0], k_send.at[4], k_recv.at[4], (("gz", 1),)),
        Copy(kz_send.at[1], kz_halo.at[1], k_send.at[5], k_recv.at[5], (("gz", -1),)),
    ]
    start(k_x)
    start(k_yz)

    def weights(x):
        here = kx[x + 1]
        t_x = (harmonic(kx[x], here), harmonic(here, kx[x + 2]))
        here = ky[x, 8:16]
        t_y = (harmonic(ky[x, 7:15], here), harmonic(here, ky[x, 9:17]))
        here = kz[x]
        before = jnp.where(
            lane == 0, pltpu.roll(kz_halo[0], LANES - x, 1), pltpu.roll(here, 1, 1)
        )
        after = jnp.where(
            lane == 127, pltpu.roll(kz_halo[1], 127 - x, 1), pltpu.roll(here, 127, 1)
        )
        t_z = (harmonic(before, here), harmonic(here, after))
        diagonal = t_x[0] + t_x[1] + t_y[0] + t_y[1] + t_z[0] + t_z[1]
        diagonal = diagonal + WELL * fl[x].astype(jnp.float32)
        negdiag[x] = -1.5 * diagonal
        scale = STEP / diagonal
        for b in range(2):
            keep_x = (par_x == b).astype(jnp.float32)
            keep_y = (par_y == b).astype(jnp.float32)
            own_z = even if b == 0 else jnp.logical_not(even)
            for side in range(2):
                inner = 4 - side
                vx[b, side, x] = t_x[side] * scale * jnp.where(x == inner, keep_x, 1.0)
                vy[b, side, x] = t_y[side] * scale * jnp.where(row == inner, keep_y, 1.0)
                cut = (lax.rem(lane, E) == inner) & jnp.logical_not(own_z)
                vz[b, side, x] = jnp.where(cut, 0.0, t_z[side] * scale)

    def center_of(k, x):
        return basis[k, :, x + 1, 8:16].reshape(2, 2, 2, E, LANES)

    def flow_x(k, x, side):
        near = basis[k, :, x + 2 * side, 8:16].reshape(2, 2, 2, E, LANES)
        return vx[:, side, x][:, None, None] * near

    def flow_yz(k, x):
        center = basis[k, :, x + 1, 8:16]
        total = -STEP * center.reshape(2, 2, 2, E, LANES)
        for side in range(2):
            near = basis[k, :, x + 1, 7 + 2 * side:15 + 2 * side].reshape(2, 2, 2, E, LANES)
            total = total + vy[:, side, x][None, :, None] * near
            edge = lane == (0, 127)[side]
            halo = z_halo[k, side]
            moved = []
            for s in range(8):
                place = s * 8 + x
                shift = LANES - place if side == 0 else 127 - place
                moved.append(
                    jnp.where(
                        edge,
                        pltpu.roll(halo, shift, 1),
                        pltpu.roll(center[s], (1, 127)[side], 1),
                    )
                )
            near = jnp.stack(moved).reshape(2, 2, 2, E, LANES)
            total = total + vz[:, side, x][None, None] * near
        return total

    def update(k, x, flow):
        center = center_of(k, x)
        support = mk[:, x].astype(jnp.float32).reshape(2, 2, 2, E, LANES)
        change = support * flow
        change_sum = jnp.sum(change, axis=(0, 1, 2))
        fresh = center + change - center * change_sum
        basis[k + 1, :, x + 1, 8:16] = fresh.reshape(8, E, LANES)

    def pack_z(k, x, tiles):
        up, down = tiles
        for s in range(8):
            place = s * 8 + x
            value = basis[k, s, x + 1, 8:16]
            up = jnp.where(lane == place, pltpu.roll(value, place + 1, 1), up)
            down = jnp.where(lane == place, pltpu.roll(value, place, 1), down)
        return up, down

    def copies(k):
        ref = basis.at[k]
        own = pl.ds(8, E)
        planes = pl.ds(1, E)
        sems = [(p_send.at[k, i], p_recv.at[k, i]) for i in range(6)]
        x = [
            Copy(ref.at[:, 8, own], ref.at[:, 0, own], *sems[0], (("gx", 1),)),
            Copy(ref.at[:, 1, own], ref.at[:, 9, own], *sems[1], (("gx", -1),)),
        ]
        yz = [
            Copy(ref.at[:, planes, pl.ds(15, 1)], ref.at[:, planes, pl.ds(7, 1)], *sems[2], (("gy", 1),)),
            Copy(ref.at[:, planes, pl.ds(8, 1)], ref.at[:, planes, pl.ds(16, 1)], *sems[3], (("gy", -1),)),
            Copy(z_send.at[k, 0], z_halo.at[k, 0], *sems[4], (("gz", 1),)),
            Copy(z_send.at[k, 1], z_halo.at[k, 1], *sems[5], (("gz", -1),)),
        ]
        return x, yz

    def inner_flow(k, x):
        return flow_yz(k, x) + flow_x(k, x, 0) + flow_x(k, x, 1)

    arriving_x, arriving_yz = k_x, k_yz
    for k in range(SWEEPS):
        for c in arriving_yz:
            c.wait_recv()
        if k == 0:
            for load in loads[3:]:
                load.wait()

            def prepare(x, carry):
                weights(x)
                return carry

            lax.fori_loop(1, 7, prepare, 0, unroll=True)

        def inner(x, tiles):
            update(k, x, inner_flow(k, x))
            return pack_z(k + 1, x, tiles)

        tiles = lax.fori_loop(1, 7, inner, (zero, zero), unroll=True)
        if k > 0:
            for x, side in ((0, 1), (7, 0)):
                part[1 - side] = (flow_yz(k, x) + flow_x(k, x, side)).reshape(8, E, LANES)
        for c in arriving_x:
            c.wait_recv()
        arriving_x, arriving_yz = copies(k + 1)
        for x, side in ((0, 0), (7, 1)):
            if k == 0:
                weights(x)
                flow = inner_flow(k, x)
            else:
                flow = part[side].reshape(2, 2, 2, E, LANES) + flow_x(k, x, side)
            update(k, x, flow)
        start(arriving_x)
        for x in (0, 7):
            tiles = pack_z(k + 1, x, tiles)
        z_send[k + 1, 0], z_send[k + 1, 1] = tiles
        start(arriving_yz)

    out = pltpu.make_async_copy(
        basis.at[SWEEPS, :, pl.ds(1, E), pl.ds(8, E)], out_p, out_sem.at[0]
    )
    out.start()

    def split_z(values):
        pair = values.reshape(4, 2, E, LANES)
        return (
            jnp.where(even, pair[:, 0], pair[:, 1]),
            jnp.where(even, pair[:, 1], pair[:, 0]),
        )

    def image(x, flow):
        own, beside = split_z(flow * negdiag[x])
        iz[:, 0, x] = own
        iz[:, 1, x] = beside

    def split_basis(x, carry):
        own, beside = split_z(center_of(SWEEPS, x))
        pz[:, 0, x] = own
        pz[:, 1, x] = beside
        return carry

    lax.fori_loop(0, E, split_basis, 0, unroll=True)
    for c in arriving_yz:
        c.wait_recv()

    def inner_image(x, carry):
        image(x, inner_flow(SWEEPS, x))
        return carry

    lax.fori_loop(1, 7, inner_image, 0, unroll=True)
    for x, side in ((0, 1), (7, 0)):
        part[1 - side] = (flow_yz(SWEEPS, x) + flow_x(SWEEPS, x, side)).reshape(8, E, LANES)

    def contract(first):
        def body(i, carry):
            half, a_x, a_y = i // 4, lax.rem(i // 2, 2), lax.rem(i, 2)
            s_xy = lax.rem(a_x + par_x, 2) * 2 + lax.rem(a_y + par_y, 2)
            planes = [1 + 3 * half + j for j in range(3)] if first else [7 * half]
            for a_z in range(2):
                for e_x in range(2):
                    for e_y in range(2):
                        u_xy = lax.rem(a_x + e_x + par_x, 2) * 2 + lax.rem(a_y + e_y + par_y, 2)
                        for e_z in range(2):
                            e = e_x * 4 + e_y * 2 + e_z
                            base = pl.multiple_of((i * 2 + a_z) * 64, 64) + e * 8
                            total = None if first else sums[pl.ds(base, E)]
                            for x in planes:
                                term = pz[s_xy, a_z, x] * iz[u_xy, (a_z + e_z) % 2, x]
                                total = term if total is None else total + term
                            sums[pl.ds(base, E)] = total
            return carry

        lax.fori_loop(0, 8, body, 0, unroll=2)

    contract(True)
    for c in arriving_x:
        c.wait_recv()
    for x, side in ((0, 0), (7, 1)):
        image(x, part[side].reshape(2, 2, 2, E, LANES) + flow_x(SWEEPS, x, side))
    contract(False)

    quarter = []
    for y_half in range(2):
        total = sums[pl.ds(4 * y_half, LANES, stride=8)]
        for y in range(1, 4):
            total = total + sums[pl.ds(4 * y_half + y, LANES, stride=8)]
        total = total.reshape(16, E, LANES)
        total = total + pltpu.roll(total, 127, 2)
        total = total + pltpu.roll(total, 126, 2)
        quarter.append(total.reshape(8, 2, E, LANES))
    up, down = zero, zero
    for i in range(8):
        for y_half in range(2):
            place = i * 2 + y_half
            beside = quarter[y_half][i, 1]
            up = jnp.where(lane == place, pltpu.roll(beside, place + 4, 1), up)
            moved = pltpu.roll(beside, place, 1) if place else beside
            down = jnp.where(lane == place, moved, down)
    zr_send[0], zr_send[1] = up, down
    zr = [
        Copy(zr_send.at[0], zr_halo.at[0], zr_ssem.at[0], zr_rsem.at[0], (("gz", 1),)),
        Copy(zr_send.at[1], zr_halo.at[1], zr_ssem.at[1], zr_rsem.at[1], (("gz", -1),)),
    ]
    start(zr)
    low = (lax.rem(lane, E) == 0) & (lane != 0)
    high = (lax.rem(lane, E) == 4) & (lane != 124)
    merged = []
    for y_half in range(2):
        own, beside = quarter[y_half][:, 0], quarter[y_half][:, 1]
        own = own + jnp.where(low, pltpu.roll(beside, 4, 2), 0.0)
        merged.append(own + jnp.where(high, pltpu.roll(beside, 124, 2), 0.0))
    for c in zr:
        c.wait_recv()
    from_below, from_above = zr_halo[0], zr_halo[1]
    for i in range(8):
        for y_half in range(2):
            place = i * 2 + y_half
            moved = pltpu.roll(from_below, LANES - place, 1) if place else from_below
            total = merged[y_half][i] + jnp.where(lane == 0, moved, 0.0)
            total = total + jnp.where(lane == 124, pltpu.roll(from_above, 124 - place, 1), 0.0)
            rows[i // 2 % 2, i % 2, i // 4, y_half] = total

    row_copies = []
    for side, d in ((0, 1), (1, -1)):
        half = 1 - side
        row_copies.append(Copy(rows.at[1, 0, half], rows_x.at[side], r_send.at[side], r_recv.at[side], (("gx", d),)))
        row_copies.append(Copy(rows.at[0, 1, :, half], rows_y.at[side], r_send.at[2 + side], r_recv.at[2 + side], (("gy", d),)))
        for side_y, d_y in ((0, 1), (1, -1)):
            n = 4 + side * 2 + side_y
            row_copies.append(Copy(
                rows.at[1, 1, half, 1 - side_y], rows_d.at[side, side_y], r_send.at[n], r_recv.at[n],
                (("gx", d), ("gy", d_y)),
            ))
    start(row_copies)
    for c in row_copies:
        c.wait_recv()
    whole = [
        [rows[0, 0, h, y] + rows_x[h, y] + rows_y[y, h] + rows_d[h, y] for y in range(2)] for h in range(2)
    ]
    tiles = jnp.stack([whole[0][0], whole[0][1], whole[1][0], whole[1][1]])
    lows, highs = tiles, pltpu.roll(tiles, 124, 2)
    for b in range(4):
        inside = lax.rem(lane, 2 ** (b + 4))
        takes = (inside >= 2**b) & (inside < 2 ** (b + 1))
        lows = jnp.where(takes, pltpu.roll(lows, LANES - 7 * 2**b, 2), lows)
        highs = jnp.where(takes, pltpu.roll(highs, LANES - 7 * 2**b, 2), highs)
    picks = {0: ((0,), 1), 1: ((0, 1), 0), 2: ((1,), 1)}
    for d_x in range(3):
        for d_y in range(3):
            (halves_x, e_x), (halves_y, e_y) = picks[d_x], picks[d_y]
            low_tile, high_tile = None, None
            for h in halves_x:
                for y in halves_y:
                    n = h * 2 + y
                    low_tile = lows[n] if low_tile is None else low_tile + lows[n]
                    high_tile = highs[n] if high_tile is None else high_tile + highs[n]
            e = e_x * 4 + e_y * 2
            out_row = (d_x * 3 + d_y) * 3
            out_c[out_row:out_row + 1, :] = low_tile[e + 1:e + 2, :16]
            out_c[out_row + 1:out_row + 2, :] = low_tile[e:e + 1, :16] + high_tile[e:e + 1, :16]
            out_c[out_row + 2:out_row + 3, :] = high_tile[e + 1:e + 2, :16]
    out.wait()
    for c in started:
        c.wait_send()


def shards(permeability, well_flags, support_mask):
    f32 = jnp.float32
    vmem = pltpu.VMEM
    dma = pltpu.SemaphoreType.DMA
    any_spec = pl.BlockSpec(memory_space=pltpu.HBM)
    prolongation, coarse = pl.pallas_call(
        kernel,
        out_shape=(
            pltpu.VMEM((8, E, E, LANES), f32),
            pltpu.VMEM((27, 16), f32),
        ),
        in_specs=[any_spec] * 3,
        out_specs=(pl.BlockSpec(memory_space=pltpu.VMEM), pl.BlockSpec(memory_space=pltpu.VMEM)),
        scratch_shapes=[
            vmem((10, E, LANES), f32),
            vmem((E, 24, LANES), f32),
            vmem((E, E, LANES), f32),
            vmem((2, E, LANES), f32),
            vmem((2, E, LANES), f32),
            vmem((E, E, LANES), jnp.int32),
            vmem((8, E, E, LANES), jnp.int32),
            vmem((SWEEPS + 1, 8, 10, 24, LANES), f32),
            vmem((SWEEPS + 1, 2, E, LANES), f32),
            vmem((SWEEPS + 1, 2, E, LANES), f32),
            vmem((2, 2, E, E, LANES), f32),
            vmem((2, 2, E, E, LANES), f32),
            vmem((2, 2, E, E, LANES), f32),
            vmem((E, E, LANES), f32),
            vmem((2, 8, E, LANES), f32),
            vmem((4, 2, E, E, LANES), f32),
            vmem((4, 2, E, E, LANES), f32),
            vmem((1024, LANES), f32),
            vmem((2, 2, 2, 2, E, LANES), f32),
            vmem((2, 2, E, LANES), f32),
            vmem((2, 2, E, LANES), f32),
            vmem((2, 2, E, LANES), f32),
            vmem((2, E, LANES), f32),
            vmem((2, E, LANES), f32),
            dma((5,)),
            dma((6,)),
            dma((6,)),
            dma((SWEEPS + 1, 6)),
            dma((SWEEPS + 1, 6)),
            dma((2,)),
            dma((2,)),
            dma((8,)),
            dma((8,)),
            dma((1,)),
        ],
        compiler_params=pltpu.CompilerParams(
            collective_id=0, has_side_effects=True, vmem_limit_bytes=60 * 1024 * 1024
        ),
        name="smooth_and_contract",
    )(permeability, well_flags, support_mask)
    return prolongation, coarse.reshape(3, 3, 3, 1, 1, 16)


def solution(mesh):
    placed = (P(None, "gx", "gy", "gz"), P("gx", "gy", "gz"), P(None, "gx", "gy", "gz"))
    return jax.shard_map(
        shards,
        mesh=mesh,
        in_specs=placed,
        out_specs=(P(None, "gx", "gy", "gz"), P(None, None, None, "gx", "gy", "gz")),
        check_vma=False,
    )
```

```python
import jax
import jax.numpy as jnp
from jax import lax
from jax.experimental import pallas as pl
from jax.experimental.pallas import tpu as pltpu
from jax.sharding import PartitionSpec as P

MESH = pl.DeviceIdType.MESH
AXES = ("gx", "gy", "gz")
COUNT = {"gx": 16, "gy": 4, "gz": 4}
SWEEPS = 4
STEP = 2.0 / 3.0
WELL = 0.05
E = 8
LANES = 128
ROW0 = 8


def harmonic(lower, upper):
    return 2.0 * lower * upper / (lower + upper)


def kernel(
    perm, flags, mask, out_p, out_c,
    kx, ky, kz, kz_send, kz_halo, fl, mk, basis, z_send, z_halo,
    vx, vy, vz, negdiag, part, pz, iz, sums, rows, rows_x, rows_y, rows_d, zr_send, zr_halo,
    faces, face_sums, face_rows, face_rows_y, zf_send, zf_halo,
    load_sem, k_send, k_recv, p_send, p_recv, r_send, r_recv, out_sem,
):
    at = {axis: lax.axis_index(axis) for axis in AXES}
    has = {}
    for axis in AXES:
        has[axis, 1] = at[axis] < COUNT[axis] - 1
        has[axis, -1] = at[axis] > 0
    par_x, par_y = lax.rem(at["gx"], 2), lax.rem(at["gy"], 2)
    lane = lax.broadcasted_iota(jnp.int32, (E, LANES), 1)
    row = lax.broadcasted_iota(jnp.int32, (E, LANES), 0)
    even = lax.rem(lane // E, 2) == 0

    loads = [
        pltpu.make_async_copy(perm.at[0], kx.at[pl.ds(1, E)], load_sem.at[0]),
        pltpu.make_async_copy(perm.at[1], ky.at[:, pl.ds(ROW0, E)], load_sem.at[1]),
        pltpu.make_async_copy(perm.at[2], kz, load_sem.at[2]),
        pltpu.make_async_copy(flags, fl, load_sem.at[3]),
        pltpu.make_async_copy(mask, mk, load_sem.at[4]),
    ]
    for load in loads:
        load.start()

    barrier = pltpu.get_barrier_semaphore()
    expected = 0
    for axis in AXES:
        for d in (1, -1):
            @pl.when(has[axis, d])
            def _():
                pl.semaphore_signal(
                    barrier, inc=1, device_id={axis: at[axis] + d}, device_id_type=MESH
                )
            expected = expected + has[axis, d].astype(jnp.int32)

    def shift_to(axis, d):
        size = COUNT[axis]
        return lax.rem(at[axis] + d + size, size)

    class Copy:
        def __init__(self, src, dst, ssem, rsem, moves):
            self.send_if = None
            self.recv_if = None
            target = {}
            for axis, d in moves:
                target[axis] = shift_to(axis, d)
                s, r = has[axis, d], has[axis, -d]
                self.send_if = s if self.send_if is None else self.send_if & s
                self.recv_if = r if self.recv_if is None else self.recv_if & r
            self.copy = pltpu.make_async_remote_copy(
                src_ref=src, dst_ref=dst, send_sem=ssem, recv_sem=rsem,
                device_id=target, device_id_type=MESH,
            )

        def start(self):
            pl.when(self.send_if)(self.copy.start)

        def wait_recv(self):
            pl.when(self.recv_if)(self.copy.wait_recv)

        def wait_send(self):
            pl.when(self.send_if)(self.copy.wait_send)

    started = []

    def start(copies):
        for c in copies:
            c.start()
        started.extend(copies)

    def fill(i, carry):
        s, x = i // 10, lax.rem(i, 10)
        bx, by, bz = s // 4, lax.rem(s // 2, 2), lax.rem(s, 2)
        block_x = jnp.where((x == 0) | (x == 9), 1 - par_x, par_x)
        hot_x = (bx == block_x).astype(jnp.float32)
        own_y = (by == par_y).astype(jnp.float32)
        hot_z = jnp.where(lax.rem(lane // E, 2) == bz, hot_x, 0.0)
        basis[0, s, x, 0:8] = hot_z * (1.0 - own_y)
        basis[0, s, x, 8:16] = hot_z * own_y
        basis[0, s, x, 16:24] = hot_z * (1.0 - own_y)
        return carry

    lax.fori_loop(0, 80, fill, 0)
    slot = lane // E
    hot_xy = (slot // 4 == par_x) & (lax.rem(slot // 2, 2) == par_y)
    for side in range(2):
        z_halo[0, side] = jnp.where(hot_xy & (lax.rem(slot, 2) == 1 - side), 1.0, 0.0)

    zero = jnp.zeros((E, LANES), jnp.float32)
    for d, k_plane in ((-1, 0), (1, 9)):
        side = (d + 1) // 2

        @pl.when(jnp.logical_not(has["gx", d]))
        def _():
            kx[k_plane] = zero
            for k in range(1, SWEEPS + 1):
                basis[k, :, k_plane, 8:16] = jnp.zeros((8, E, LANES), jnp.float32)
            rows_x[side] = jnp.zeros((2, E, LANES), jnp.float32)

        @pl.when(jnp.logical_not(has["gy", d]))
        def _():
            y_row = 7 if d < 0 else 16
            ky[:, y_row:y_row + 1] = jnp.zeros((E, 1, LANES), jnp.float32)

            def clear(i, carry):
                basis[1 + i // 8, lax.rem(i, 8), 1:9, y_row:y_row + 1] = jnp.zeros(
                    (E, 1, LANES), jnp.float32
                )
                return carry

            lax.fori_loop(0, 8 * SWEEPS, clear, 0)
            rows_y[side] = jnp.zeros((2, E, LANES), jnp.float32)
            face_rows_y[side] = jnp.zeros((2, E, LANES), jnp.float32)

        @pl.when(jnp.logical_not(has["gz", d]))
        def _():
            kz_halo[side] = zero
            for k in range(1, SWEEPS + 1):
                z_halo[k, side] = zero

        for e in (1, -1):
            @pl.when(jnp.logical_not(has["gx", d] & has["gy", e]))
            def _():
                rows_d[side, (e + 1) // 2] = zero

    for m_z in (1, -1):
        side = (1 - m_z) // 2
        for m_y in (1, 0, -1):
            near = has["gz", -m_z]
            if m_y:
                near = near & has["gy", -m_y]

            @pl.when(jnp.logical_not(near))
            def _():
                zf_halo[side, m_y + 1] = zero

            for m_x in (1, 0, -1):
                there = near & has["gx", -m_x] if m_x else near

                @pl.when(jnp.logical_not(there))
                def _():
                    zr_halo[side, m_x + 1, m_y + 1] = zero

    for load in loads[:3]:
        load.wait()
    for side in range(2):
        tile = zero
        for x in range(E):
            shift = (x - 127) % LANES if side == 0 else x
            moved = pltpu.roll(kz[x], shift, 1) if shift else kz[x]
            tile = jnp.where(lane == x, moved, tile)
        kz_send[side] = tile
    pl.semaphore_wait(barrier, expected)
    k_x = [
        Copy(kx.at[8], kx.at[0], k_send.at[0], k_recv.at[0], (("gx", 1),)),
        Copy(kx.at[1], kx.at[9], k_send.at[1], k_recv.at[1], (("gx", -1),)),
    ]
    k_yz = [
        Copy(ky.at[:, pl.ds(15, 1)], ky.at[:, pl.ds(7, 1)], k_send.at[2], k_recv.at[2], (("gy", 1),)),
        Copy(ky.at[:, pl.ds(8, 1)], ky.at[:, pl.ds(16, 1)], k_send.at[3], k_recv.at[3], (("gy", -1),)),
        Copy(kz_send.at[0], kz_halo.at[0], k_send.at[4], k_recv.at[4], (("gz", 1),)),
        Copy(kz_send.at[1], kz_halo.at[1], k_send.at[5], k_recv.at[5], (("gz", -1),)),
    ]
    start(k_x)
    start(k_yz)

    def weights(x):
        here = kx[x + 1]
        t_x = (harmonic(kx[x], here), harmonic(here, kx[x + 2]))
        here = ky[x, 8:16]
        t_y = (harmonic(ky[x, 7:15], here), harmonic(here, ky[x, 9:17]))
        here = kz[x]
        before = jnp.where(
            lane == 0, pltpu.roll(kz_halo[0], LANES - x, 1), pltpu.roll(here, 1, 1)
        )
        after = jnp.where(
            lane == 127, pltpu.roll(kz_halo[1], 127 - x, 1), pltpu.roll(here, 127, 1)
        )
        t_z = (harmonic(before, here), harmonic(here, after))
        diagonal = t_x[0] + t_x[1] + t_y[0] + t_y[1] + t_z[0] + t_z[1]
        diagonal = diagonal + WELL * fl[x].astype(jnp.float32)
        negdiag[x] = -1.5 * diagonal
        scale = STEP / diagonal
        for b in range(2):
            keep_x = (par_x == b).astype(jnp.float32)
            keep_y = (par_y == b).astype(jnp.float32)
            own_z = even if b == 0 else jnp.logical_not(even)
            for side in range(2):
                inner = 4 - side
                vx[b, side, x] = t_x[side] * scale * jnp.where(x == inner, keep_x, 1.0)
                vy[b, side, x] = t_y[side] * scale * jnp.where(row == inner, keep_y, 1.0)
                cut = (lax.rem(lane, E) == inner) & jnp.logical_not(own_z)
                vz[b, side, x] = jnp.where(cut, 0.0, t_z[side] * scale)

    def center_of(k, x):
        return basis[k, :, x + 1, 8:16].reshape(2, 2, 2, E, LANES)

    def flow_x(k, x, side):
        near = basis[k, :, x + 2 * side, 8:16].reshape(2, 2, 2, E, LANES)
        return vx[:, side, x][:, None, None] * near

    def flow_yz(k, x):
        center = basis[k, :, x + 1, 8:16]
        total = -STEP * center.reshape(2, 2, 2, E, LANES)
        for side in range(2):
            near = basis[k, :, x + 1, 7 + 2 * side:15 + 2 * side].reshape(2, 2, 2, E, LANES)
            total = total + vy[:, side, x][None, :, None] * near
            edge = lane == (0, 127)[side]
            halo = z_halo[k, side]
            moved = []
            for s in range(8):
                place = s * 8 + x
                shift = LANES - place if side == 0 else 127 - place
                moved.append(
                    jnp.where(
                        edge,
                        pltpu.roll(halo, shift, 1),
                        pltpu.roll(center[s], (1, 127)[side], 1),
                    )
                )
            near = jnp.stack(moved).reshape(2, 2, 2, E, LANES)
            total = total + vz[:, side, x][None, None] * near
        return total

    def update(k, x, flow):
        center = center_of(k, x)
        support = mk[:, x].astype(jnp.float32).reshape(2, 2, 2, E, LANES)
        change = support * flow
        change_sum = jnp.sum(change, axis=(0, 1, 2))
        fresh = center + change - center * change_sum
        basis[k + 1, :, x + 1, 8:16] = fresh.reshape(8, E, LANES)

    def pack_z(k, x, tiles):
        up, down = tiles
        for s in range(8):
            place = s * 8 + x
            value = basis[k, s, x + 1, 8:16]
            up = jnp.where(lane == place, pltpu.roll(value, place + 1, 1), up)
            down = jnp.where(lane == place, pltpu.roll(value, place, 1), down)
        return up, down

    def copies(k):
        ref = basis.at[k]
        own = pl.ds(8, E)
        planes = pl.ds(1, E)
        sems = [(p_send.at[k, i], p_recv.at[k, i]) for i in range(6)]
        x = [
            Copy(ref.at[:, 8, own], ref.at[:, 0, own], *sems[0], (("gx", 1),)),
            Copy(ref.at[:, 1, own], ref.at[:, 9, own], *sems[1], (("gx", -1),)),
        ]
        yz = [
            Copy(ref.at[:, planes, pl.ds(15, 1)], ref.at[:, planes, pl.ds(7, 1)], *sems[2], (("gy", 1),)),
            Copy(ref.at[:, planes, pl.ds(8, 1)], ref.at[:, planes, pl.ds(16, 1)], *sems[3], (("gy", -1),)),
            Copy(z_send.at[k, 0], z_halo.at[k, 0], *sems[4], (("gz", 1),)),
            Copy(z_send.at[k, 1], z_halo.at[k, 1], *sems[5], (("gz", -1),)),
        ]
        return x, yz

    def inner_flow(k, x):
        return flow_yz(k, x) + flow_x(k, x, 0) + flow_x(k, x, 1)

    arriving_x, arriving_yz = k_x, k_yz
    for k in range(SWEEPS):
        for c in arriving_yz:
            c.wait_recv()
        if k == 0:
            for load in loads[3:]:
                load.wait()

            def prepare(x, carry):
                weights(x)
                return carry

            lax.fori_loop(1, 7, prepare, 0, unroll=True)

        def inner(x, tiles):
            update(k, x, inner_flow(k, x))
            return pack_z(k + 1, x, tiles)

        tiles = lax.fori_loop(1, 7, inner, (zero, zero), unroll=True)
        if k > 0:
            for x, side in ((0, 1), (7, 0)):
                part[1 - side] = (flow_yz(k, x) + flow_x(k, x, side)).reshape(8, E, LANES)
        for c in arriving_x:
            c.wait_recv()
        arriving_x, arriving_yz = copies(k + 1)
        for x, side in ((0, 0), (7, 1)):
            if k == 0:
                weights(x)
                flow = inner_flow(k, x)
            else:
                flow = part[side].reshape(2, 2, 2, E, LANES) + flow_x(k, x, side)
            update(k, x, flow)
        start(arriving_x)
        for x in (0, 7):
            tiles = pack_z(k + 1, x, tiles)
        z_send[k + 1, 0], z_send[k + 1, 1] = tiles
        start(arriving_yz)

    out = pltpu.make_async_copy(
        basis.at[SWEEPS, :, pl.ds(1, E), pl.ds(8, E)], out_p, out_sem.at[0]
    )
    out.start()

    def split_z(values):
        pair = values.reshape(4, 2, E, LANES)
        return (
            jnp.where(even, pair[:, 0], pair[:, 1]),
            jnp.where(even, pair[:, 1], pair[:, 0]),
        )

    def split_basis(x, carry):
        own, beside = split_z(center_of(SWEEPS, x))
        pz[:, 0, x] = own
        pz[:, 1, x] = beside
        return carry

    lax.fori_loop(0, E, split_basis, 0, unroll=True)
    for c in arriving_yz:
        c.wait_recv()

    def image(x, flow):
        own, beside = split_z(flow * negdiag[x])
        iz[:, 0, x] = own
        iz[:, 1, x] = beside

    def inner_image(x, carry):
        image(x, inner_flow(SWEEPS, x))
        return carry

    lax.fori_loop(1, 7, inner_image, 0, unroll=True)
    for x, side in ((0, 1), (7, 0)):
        image(x, flow_yz(SWEEPS, x) + flow_x(SWEEPS, x, side))

    def pair_of(a_x, a_y):
        return lax.rem(a_x + par_x, 2) * 2 + lax.rem(a_y + par_y, 2)

    def contract(i, carry):
        half, a_x, a_y = i // 4, lax.rem(i // 2, 2), lax.rem(i, 2)
        for a_z in range(2):
            for e in range(8):
                u_xy = pair_of(a_x + e // 4, a_y + e // 2 % 2)
                total = None
                for j in range(4):
                    x = 4 * half + j
                    term = pz[pair_of(a_x, a_y), a_z, x] * iz[u_xy, (a_z + e) % 2, x]
                    total = term if total is None else total + term
                sums[pl.ds(pl.multiple_of((i * 2 + a_z) * 64, 64) + e * 8, E)] = total
        return carry

    lax.fori_loop(0, 8, contract, 0, unroll=2)

    def halves(ref, count):
        results = []
        for y_half in range(2):
            total = ref[pl.ds(4 * y_half, count * 8, stride=8)]
            for y in range(1, 4):
                total = total + ref[pl.ds(4 * y_half + y, count * 8, stride=8)]
            total = total.reshape(count, E, LANES)
            total = total + pltpu.roll(total, 127, 2)
            total = total + pltpu.roll(total, 126, 2)
            results.append(total.reshape(count // 2, 2, E, LANES))
        return results

    low = (lax.rem(lane, E) == 0) & (lane != 0)
    high = (lax.rem(lane, E) == 4) & (lane != 124)

    def merge_z(pair):
        own, beside = pair[:, 0], pair[:, 1]
        own = own + jnp.where(low, pltpu.roll(beside, 4, 2), 0.0)
        return own + jnp.where(high, pltpu.roll(beside, 124, 2), 0.0)

    def pack_rows(entries):
        up, down = zero, zero
        for place, beside in entries:
            up = jnp.where(lane == place, pltpu.roll(beside, place + 4, 1), up)
            moved = pltpu.roll(beside, place, 1) if place else beside
            down = jnp.where(lane == place, moved, down)
        return up, down

    row_copies = []

    def move_rows(src, dst, moves):
        n = len(row_copies)
        row_copies.append(Copy(src, dst, r_send.at[n], r_recv.at[n], tuple(m for m in moves if m[1])))

    quarter = halves(sums, 16)
    entries = []
    for i in range(8):
        half, a_x, a_y = i // 4, i // 2 % 2, i % 2
        for y_half in range(2):
            place = (a_x * 2 + a_y) * 32 + (half ^ a_x) * 2 + (y_half ^ a_y)
            entries.append((place, quarter[y_half][i, 1]))
    zr_send[0], zr_send[1] = pack_rows(entries)
    order = [(m_x, m_y) for m_x in (1, -1, 0) for m_y in (1, -1, 0)]
    for side, m_z in ((0, 1), (1, -1)):
        for m_x, m_y in order:
            move_rows(
                zr_send.at[side], zr_halo.at[side, m_x + 1, m_y + 1],
                (("gx", m_x), ("gy", m_y), ("gz", m_z)),
            )
    start(row_copies)
    for y_half in range(2):
        merged = merge_z(quarter[y_half])
        for i in range(8):
            rows[i // 2 % 2, i % 2, i // 4, y_half] = merged[i]
    first = len(row_copies)
    for side, d in ((0, 1), (1, -1)):
        for side_y, d_y in ((0, 1), (1, -1)):
            move_rows(
                rows.at[1, 1, 1 - side, 1 - side_y], rows_d.at[side, side_y], (("gx", d), ("gy", d_y))
            )
    for side, d in ((0, 1), (1, -1)):
        move_rows(rows.at[1, 0, 1 - side], rows_x.at[side], (("gx", d),))
        move_rows(rows.at[0, 1, :, 1 - side], rows_y.at[side], (("gy", d),))
    start(row_copies[first:])
    first = len(row_copies)

    for c in arriving_x:
        c.wait_recv()
    for side in range(2):
        x = 7 * side
        weight = vx[0, side, x] * negdiag[x]
        for n, plane in enumerate((x + 1, 9 * side)):
            own, beside = split_z(basis[SWEEPS, :, plane, 8:16])
            faces[side, n, 0, :, 0] = own
            faces[side, n, 0, :, 1] = beside
            faces[side, n, 1, :, 0] = own * weight
            faces[side, n, 1, :, 1] = beside * weight

    def contract_faces(i, carry):
        side, a_y = i // 2, lax.rem(i, 2)
        s_xy = pair_of(0, a_y)
        for a_z in range(2):
            for e in range(8):
                u_xy = pair_of(e // 4, a_y + e // 2 % 2)
                u_z = (a_z + e) % 2
                total = faces[side, 0, 0, s_xy, a_z] * faces[side, 1, 1, u_xy, u_z]
                total = total + faces[side, 1, 0, s_xy, a_z] * faces[side, 0, 1, u_xy, u_z]
                face_sums[pl.ds(pl.multiple_of((i * 2 + a_z) * 64, 64) + e * 8, E)] = total
        return carry

    lax.fori_loop(0, 4, contract_faces, 0, unroll=True)
    quarter = halves(face_sums, 8)
    entries = []
    for i in range(4):
        half, a_y = i // 2, i % 2
        for y_half in range(2):
            entries.append((a_y * 32 + half * 2 + (y_half ^ a_y), quarter[y_half][i, 1]))
    zf_send[0], zf_send[1] = pack_rows(entries)
    for side, m_z in ((0, 1), (1, -1)):
        for m_y in (1, -1, 0):
            move_rows(zf_send.at[side], zf_halo.at[side, m_y + 1], (("gy", m_y), ("gz", m_z)))
    start(row_copies[first:])
    first = len(row_copies)
    face_own = []
    for y_half in range(2):
        merged = merge_z(quarter[y_half])
        face_own.append((merged[0], merged[2]))
        face_rows[y_half, 0], face_rows[y_half, 1] = merged[1], merged[3]
    for side, d in ((0, 1), (1, -1)):
        move_rows(face_rows.at[1 - side], face_rows_y.at[side], (("gy", d),))
    start(row_copies[first:])

    for c in row_copies:
        c.wait_recv()
    whole = [
        [
            rows[0, 0, h, y] + rows_x[h, y] + rows_y[y, h] + rows_d[h, y] + face_own[y][h] + face_rows_y[y, h]
            for y in range(2)
        ]
        for h in range(2)
    ]
    for side in range(2):
        packed = zero
        for m_x, m_y in order:
            inside = lane - 32 * (2 * abs(m_x) + abs(m_y))
            takes = (inside >= 0) & (inside < 4)
            if m_x:
                takes = takes & (inside // 2 == (1 - m_x) // 2)
            if m_y:
                takes = takes & (lax.rem(inside, 2) == (1 - m_y) // 2)
            value = zr_halo[side, m_x + 1, m_y + 1]
            if m_x == 0:
                value = value + zf_halo[side, m_y + 1]
            packed = packed + jnp.where(takes, value, 0.0)
        packed = packed + pltpu.roll(packed, 64, 1)
        packed = packed + pltpu.roll(packed, 32, 1)
        target = 124 * side
        for h in range(2):
            for y in range(2):
                shift = (target - (h * 2 + y)) % LANES
                moved = pltpu.roll(packed, shift, 1) if shift else packed
                whole[h][y] = whole[h][y] + jnp.where(lane == target, moved, 0.0)
    tiles = jnp.stack([whole[0][0], whole[0][1], whole[1][0], whole[1][1]])
    lows, highs = tiles, pltpu.roll(tiles, 124, 2)
    for b in range(4):
        inside = lax.rem(lane, 2 ** (b + 4))
        takes = (inside >= 2**b) & (inside < 2 ** (b + 1))
        lows = jnp.where(takes, pltpu.roll(lows, LANES - 7 * 2**b, 2), lows)
        highs = jnp.where(takes, pltpu.roll(highs, LANES - 7 * 2**b, 2), highs)
    picks = {0: ((0,), 1), 1: ((0, 1), 0), 2: ((1,), 1)}
    for d_x in range(3):
        for d_y in range(3):
            (halves_x, e_x), (halves_y, e_y) = picks[d_x], picks[d_y]
            low_tile, high_tile = None, None
            for h in halves_x:
                for y in halves_y:
                    n = h * 2 + y
                    low_tile = lows[n] if low_tile is None else low_tile + lows[n]
                    high_tile = highs[n] if high_tile is None else high_tile + highs[n]
            e = e_x * 4 + e_y * 2
            out_row = (d_x * 3 + d_y) * 3
            out_c[out_row:out_row + 1, :] = low_tile[e + 1:e + 2, :16]
            out_c[out_row + 1:out_row + 2, :] = low_tile[e:e + 1, :16] + high_tile[e:e + 1, :16]
            out_c[out_row + 2:out_row + 3, :] = high_tile[e + 1:e + 2, :16]
    out.wait()
    for c in started:
        c.wait_send()


def shards(permeability, well_flags, support_mask):
    f32 = jnp.float32
    vmem = pltpu.VMEM
    dma = pltpu.SemaphoreType.DMA
    any_spec = pl.BlockSpec(memory_space=pltpu.HBM)
    prolongation, coarse = pl.pallas_call(
        kernel,
        out_shape=(
            pltpu.VMEM((8, E, E, LANES), f32),
            pltpu.VMEM((27, 16), f32),
        ),
        in_specs=[any_spec] * 3,
        out_specs=(pl.BlockSpec(memory_space=pltpu.VMEM), pl.BlockSpec(memory_space=pltpu.VMEM)),
        scratch_shapes=[
            vmem((10, E, LANES), f32),
            vmem((E, 24, LANES), f32),
            vmem((E, E, LANES), f32),
            vmem((2, E, LANES), f32),
            vmem((2, E, LANES), f32),
            vmem((E, E, LANES), jnp.int32),
            vmem((8, E, E, LANES), jnp.int32),
            vmem((SWEEPS + 1, 8, 10, 24, LANES), f32),
            vmem((SWEEPS + 1, 2, E, LANES), f32),
            vmem((SWEEPS + 1, 2, E, LANES), f32),
            vmem((2, 2, E, E, LANES), f32),
            vmem((2, 2, E, E, LANES), f32),
            vmem((2, 2, E, E, LANES), f32),
            vmem((E, E, LANES), f32),
            vmem((2, 8, E, LANES), f32),
            vmem((4, 2, E, E, LANES), f32),
            vmem((4, 2, E, E, LANES), f32),
            vmem((1024, LANES), f32),
            vmem((2, 2, 2, 2, E, LANES), f32),
            vmem((2, 2, E, LANES), f32),
            vmem((2, 2, E, LANES), f32),
            vmem((2, 2, E, LANES), f32),
            vmem((2, E, LANES), f32),
            vmem((2, 3, 3, E, LANES), f32),
            vmem((2, 2, 2, 4, 2, E, LANES), f32),
            vmem((512, LANES), f32),
            vmem((2, 2, E, LANES), f32),
            vmem((2, 2, E, LANES), f32),
            vmem((2, E, LANES), f32),
            vmem((2, 3, E, LANES), f32),
            dma((5,)),
            dma((6,)),
            dma((6,)),
            dma((SWEEPS + 1, 6)),
            dma((SWEEPS + 1, 6)),
            dma((34,)),
            dma((34,)),
            dma((1,)),
        ],
        compiler_params=pltpu.CompilerParams(
            collective_id=0, has_side_effects=True, vmem_limit_bytes=60 * 1024 * 1024
        ),
        name="smooth_and_contract",
    )(permeability, well_flags, support_mask)
    return prolongation, coarse.reshape(3, 3, 3, 1, 1, 16)


def solution(mesh):
    placed = (P(None, "gx", "gy", "gz"), P("gx", "gy", "gz"), P(None, "gx", "gy", "gz"))
    return jax.shard_map(
        shards,
        mesh=mesh,
        in_specs=placed,
        out_specs=(P(None, "gx", "gy", "gz"), P(None, None, None, "gx", "gy", "gz")),
        check_vma=False,
    )
```

```python
import jax
import jax.numpy as jnp
from jax import lax
from jax.experimental import pallas as pl
from jax.experimental.pallas import tpu as pltpu
from jax.sharding import PartitionSpec as P

MESH = pl.DeviceIdType.MESH
AXES = ("gx", "gy", "gz")
COUNT = {"gx": 16, "gy": 4, "gz": 4}
SWEEPS = 4
STEP = 2.0 / 3.0
WELL = 0.05
E = 8
LANES = 128
ROW0 = 8


def harmonic(lower, upper):
    return 2.0 * lower * upper / (lower + upper)


def kernel(
    perm, flags, mask, out_p, out_c,
    kx, ky, kz, kz_send, kz_halo, fl, mk, basis, z_send, z_halo,
    vx, vy, vz, negdiag, part, pz, iz, sums, rows, rows_x, rows_y, rows_d, zr_send, zr_halo,
    faces, face_sums, face_rows, face_rows_y, zf_send, zf_halo, a_send, a_halo, mask_halo, part_halo, halo_vx,
    load_sem, k_send, k_recv, p_send, p_recv, r_send, r_recv, h_send, h_recv, out_sem,
):
    at = {axis: lax.axis_index(axis) for axis in AXES}
    has = {}
    for axis in AXES:
        has[axis, 1] = at[axis] < COUNT[axis] - 1
        has[axis, -1] = at[axis] > 0
    par_x, par_y = lax.rem(at["gx"], 2), lax.rem(at["gy"], 2)
    lane = lax.broadcasted_iota(jnp.int32, (E, LANES), 1)
    row = lax.broadcasted_iota(jnp.int32, (E, LANES), 0)
    even = lax.rem(lane // E, 2) == 0

    loads = [
        pltpu.make_async_copy(perm.at[0], kx.at[pl.ds(1, E)], load_sem.at[0]),
        pltpu.make_async_copy(perm.at[1], ky.at[:, pl.ds(ROW0, E)], load_sem.at[1]),
        pltpu.make_async_copy(perm.at[2], kz, load_sem.at[2]),
        pltpu.make_async_copy(flags, fl, load_sem.at[3]),
        pltpu.make_async_copy(mask, mk, load_sem.at[4]),
    ]
    for load in loads:
        load.start()

    barrier = pltpu.get_barrier_semaphore()
    expected = 0
    for axis in AXES:
        for d in (1, -1):
            @pl.when(has[axis, d])
            def _():
                pl.semaphore_signal(
                    barrier, inc=1, device_id={axis: at[axis] + d}, device_id_type=MESH
                )
            expected = expected + has[axis, d].astype(jnp.int32)

    def shift_to(axis, d):
        size = COUNT[axis]
        return lax.rem(at[axis] + d + size, size)

    class Copy:
        def __init__(self, src, dst, ssem, rsem, moves):
            self.send_if = None
            self.recv_if = None
            target = {}
            for axis, d in moves:
                target[axis] = shift_to(axis, d)
                s, r = has[axis, d], has[axis, -d]
                self.send_if = s if self.send_if is None else self.send_if & s
                self.recv_if = r if self.recv_if is None else self.recv_if & r
            self.copy = pltpu.make_async_remote_copy(
                src_ref=src, dst_ref=dst, send_sem=ssem, recv_sem=rsem,
                device_id=target, device_id_type=MESH,
            )

        def start(self):
            pl.when(self.send_if)(self.copy.start)

        def wait_recv(self):
            pl.when(self.recv_if)(self.copy.wait_recv)

        def wait_send(self):
            pl.when(self.send_if)(self.copy.wait_send)

    started = []

    def start(copies):
        for c in copies:
            c.start()
        started.extend(copies)

    def fill(i, carry):
        s, x = i // 10, lax.rem(i, 10)
        bx, by, bz = s // 4, lax.rem(s // 2, 2), lax.rem(s, 2)
        block_x = jnp.where((x == 0) | (x == 9), 1 - par_x, par_x)
        hot_x = (bx == block_x).astype(jnp.float32)
        own_y = (by == par_y).astype(jnp.float32)
        hot_z = jnp.where(lax.rem(lane // E, 2) == bz, hot_x, 0.0)
        basis[0, s, x, 0:8] = hot_z * (1.0 - own_y)
        basis[0, s, x, 8:16] = hot_z * own_y
        basis[0, s, x, 16:24] = hot_z * (1.0 - own_y)
        return carry

    lax.fori_loop(0, 80, fill, 0)
    slot = lane // E
    hot_xy = (slot // 4 == par_x) & (lax.rem(slot // 2, 2) == par_y)
    for side in range(2):
        for group in range(2):
            z_halo[0, group, side] = jnp.where(hot_xy & (lax.rem(slot, 2) == 1 - side), 1.0, 0.0)

    zero = jnp.zeros((E, LANES), jnp.float32)
    for d, k_plane in ((-1, 0), (1, 9)):
        side = (d + 1) // 2

        @pl.when(jnp.logical_not(has["gx", d]))
        def _():
            kx[k_plane] = zero
            a_halo[side] = jnp.ones((3, E, LANES), jnp.float32)
            mask_halo[side] = jnp.zeros((8, E, LANES), jnp.int32)
            part_halo[side] = jnp.zeros((8, E, LANES), jnp.float32)
            for k in range(1, SWEEPS + 1):
                basis[k, :, k_plane, 8:16] = jnp.zeros((8, E, LANES), jnp.float32)
            rows_x[side] = jnp.zeros((2, E, LANES), jnp.float32)

        @pl.when(jnp.logical_not(has["gy", d]))
        def _():
            y_row = 7 if d < 0 else 16
            ky[:, y_row:y_row + 1] = jnp.zeros((E, 1, LANES), jnp.float32)

            def clear(i, carry):
                basis[1 + i // 8, lax.rem(i, 8), 1:9, y_row:y_row + 1] = jnp.zeros(
                    (E, 1, LANES), jnp.float32
                )
                return carry

            lax.fori_loop(0, 8 * SWEEPS, clear, 0)
            rows_y[side] = jnp.zeros((2, E, LANES), jnp.float32)
            face_rows_y[side] = jnp.zeros((2, E, LANES), jnp.float32)

        @pl.when(jnp.logical_not(has["gz", d]))
        def _():
            kz_halo[side] = zero
            for k in range(1, SWEEPS + 1):
                z_halo[k, 0, side] = zero
                z_halo[k, 1, side] = zero

        for e in (1, -1):
            @pl.when(jnp.logical_not(has["gx", d] & has["gy", e]))
            def _():
                rows_d[side, (e + 1) // 2] = zero

    for m_z in (1, -1):
        side = (1 - m_z) // 2
        for m_y in (1, 0, -1):
            near = has["gz", -m_z]
            if m_y:
                near = near & has["gy", -m_y]

            @pl.when(jnp.logical_not(near))
            def _():
                zf_halo[side, m_y + 1] = zero

            for m_x in (1, 0, -1):
                there = near & has["gx", -m_x] if m_x else near

                @pl.when(jnp.logical_not(there))
                def _():
                    zr_halo[side, m_x + 1, m_y + 1] = zero

    for load in loads[:3]:
        load.wait()
    for side in range(2):
        tile = zero
        for x in range(E):
            shift = (x - 127) % LANES if side == 0 else x
            moved = pltpu.roll(kz[x], shift, 1) if shift else kz[x]
            tile = jnp.where(lane == x, moved, tile)
        kz_send[side] = tile
    pl.semaphore_wait(barrier, expected)
    k_x = [
        Copy(kx.at[8], kx.at[0], k_send.at[0], k_recv.at[0], (("gx", 1),)),
        Copy(kx.at[1], kx.at[9], k_send.at[1], k_recv.at[1], (("gx", -1),)),
    ]
    k_yz = [
        Copy(ky.at[:, pl.ds(15, 1)], ky.at[:, pl.ds(7, 1)], k_send.at[2], k_recv.at[2], (("gy", 1),)),
        Copy(ky.at[:, pl.ds(8, 1)], ky.at[:, pl.ds(16, 1)], k_send.at[3], k_recv.at[3], (("gy", -1),)),
        Copy(kz_send.at[0], kz_halo.at[0], k_send.at[4], k_recv.at[4], (("gz", 1),)),
        Copy(kz_send.at[1], kz_halo.at[1], k_send.at[5], k_recv.at[5], (("gz", -1),)),
    ]
    start(k_x)
    start(k_yz)
    for load in loads[3:]:
        load.wait()
    h_copies = []
    for src, dst in ((mk, mask_halo), (a_send, a_halo), (part, part_halo)):
        for side, d in ((0, -1), (1, 1)):
            n = len(h_copies)
            if src is mk:
                block = mk.at[:, 7 * side]
            else:
                block = src.at[2, side] if src is part else src.at[side]
            h_copies.append(Copy(block, dst.at[1 - side], h_send.at[n], h_recv.at[n], (("gx", d),)))
    start(h_copies[:2])

    def faces_yz(x):
        here = ky[x, 8:16]
        t_y = (harmonic(ky[x, 7:15], here), harmonic(here, ky[x, 9:17]))
        here = kz[x]
        before = jnp.where(
            lane == 0, pltpu.roll(kz_halo[0], LANES - x, 1), pltpu.roll(here, 1, 1)
        )
        after = jnp.where(
            lane == 127, pltpu.roll(kz_halo[1], 127 - x, 1), pltpu.roll(here, 127, 1)
        )
        return t_y, (harmonic(before, here), harmonic(here, after))

    def outer_plane(side):
        x = 7 * side
        t_x = harmonic(kx[x + 1 - side], kx[x + 2 - side])
        t_y, t_z = faces_yz(x)
        total = t_x + t_y[0] + t_y[1] + t_z[0] + t_z[1]
        a_send[side, 0] = total + WELL * fl[x].astype(jnp.float32)
        a_send[side, 1] = jnp.where(row == 0, t_y[0], jnp.where(row == 7, t_y[1], 0.0))
        place = lax.rem(lane, E)
        a_send[side, 2] = jnp.where(place == 0, t_z[0], jnp.where(place == 7, t_z[1], 0.0))

    def first_halo(side):
        plane, away = 9 * side, 1 - par_x
        t_x = harmonic(kx[8 * side], kx[8 * side + 1])
        scale = STEP / (a_halo[side, 0] + t_x)
        halo_vx[side] = t_x * scale

        def support(b_x, b_y, own):
            n = 4 * b_x + 2 * b_y
            low, high = mask_halo[side, n], mask_halo[side, n + 1]
            pair = (low, high) if own else (high, low)
            return jnp.where(even, *pair).astype(jnp.float32)

        u_x = support(par_x, par_y, True) * (t_x * scale)
        u_y = support(away, 1 - par_y, True) * (a_halo[side, 1] * scale)
        u_z = support(away, par_y, False) * (a_halo[side, 2] * scale)
        own = 1.0 - (u_x + u_y + u_z)

        def put(b_x, b_y, own_z, beside_z):
            n = 4 * b_x + 2 * b_y
            basis[1, n, plane, 8:16] = jnp.where(even, own_z, beside_z)
            basis[1, n + 1, plane, 8:16] = jnp.where(even, beside_z, own_z)

        put(away, par_y, own, u_z)
        put(par_x, par_y, u_x, zero)
        put(away, 1 - par_y, u_y, zero)
        put(par_x, 1 - par_y, zero, zero)

    def third_halo(side):
        plane = 9 * side
        flow = part_halo[side] + halo_vx[side] * basis[2, :, 1 + 7 * side, 8:16]
        center = basis[2, :, plane, 8:16]
        change = mask_halo[side].astype(jnp.float32) * flow
        basis[3, :, plane, 8:16] = center + change - center * jnp.sum(change, axis=0)

    def weights(x):
        here = kx[x + 1]
        t_x = (harmonic(kx[x], here), harmonic(here, kx[x + 2]))
        t_y, t_z = faces_yz(x)
        diagonal = t_x[0] + t_x[1] + t_y[0] + t_y[1] + t_z[0] + t_z[1]
        diagonal = diagonal + WELL * fl[x].astype(jnp.float32)
        negdiag[x] = -1.5 * diagonal
        scale = STEP / diagonal
        for b in range(2):
            keep_x = (par_x == b).astype(jnp.float32)
            keep_y = (par_y == b).astype(jnp.float32)
            own_z = even if b == 0 else jnp.logical_not(even)
            for side in range(2):
                inner = 4 - side
                vx[b, side, x] = t_x[side] * scale * jnp.where(x == inner, keep_x, 1.0)
                vy[b, side, x] = t_y[side] * scale * jnp.where(row == inner, keep_y, 1.0)
                cut = (lax.rem(lane, E) == inner) & jnp.logical_not(own_z)
                vz[b, side, x] = jnp.where(cut, 0.0, t_z[side] * scale)

    def center_of(k, x):
        return basis[k, :, x + 1, 8:16].reshape(2, 2, 2, E, LANES)

    def flow_x(k, x, side):
        near = basis[k, :, x + 2 * side, 8:16].reshape(2, 2, 2, E, LANES)
        return vx[:, side, x][:, None, None] * near

    def flow_yz(k, x, group):
        center = basis[k, :, x + 1, 8:16]
        total = -STEP * center.reshape(2, 2, 2, E, LANES)
        for side in range(2):
            near = basis[k, :, x + 1, 7 + 2 * side:15 + 2 * side].reshape(2, 2, 2, E, LANES)
            total = total + vy[:, side, x][None, :, None] * near
            edge = lane == (0, 127)[side]
            halo = z_halo[k, group, side]
            moved = []
            for s in range(8):
                place = s * 8 + x
                shift = LANES - place if side == 0 else 127 - place
                moved.append(
                    jnp.where(
                        edge,
                        pltpu.roll(halo, shift, 1),
                        pltpu.roll(center[s], (1, 127)[side], 1),
                    )
                )
            near = jnp.stack(moved).reshape(2, 2, 2, E, LANES)
            total = total + vz[:, side, x][None, None] * near
        return total

    def update(k, x, flow):
        center = center_of(k, x)
        support = mk[:, x].astype(jnp.float32).reshape(2, 2, 2, E, LANES)
        change = support * flow
        change_sum = jnp.sum(change, axis=(0, 1, 2))
        fresh = center + change - center * change_sum
        basis[k + 1, :, x + 1, 8:16] = fresh.reshape(8, E, LANES)

    def pack_z(k, x, tiles):
        up, down = tiles
        for s in range(8):
            place = s * 8 + x
            value = basis[k, s, x + 1, 8:16]
            up = jnp.where(lane == place, pltpu.roll(value, place + 1, 1), up)
            down = jnp.where(lane == place, pltpu.roll(value, place, 1), down)
        return up, down

    def copies(k):
        ref = basis.at[k]
        own = pl.ds(8, E)
        sems = [(p_send.at[k, i], p_recv.at[k, i]) for i in range(12)]
        x = [
            Copy(ref.at[:, 8, own], ref.at[:, 0, own], *sems[0], (("gx", 1),)),
            Copy(ref.at[:, 1, own], ref.at[:, 9, own], *sems[1], (("gx", -1),)),
        ] if k % 2 == 0 else []
        yz = []
        for group in range(2):
            part_yz = []
            for n, planes in enumerate((pl.ds(2, 6),) if group == 0 else (pl.ds(1, 1), pl.ds(8, 1))):
                at_sem = 2 + 2 * group + 2 * n
                for side, (a, b, d) in enumerate(((15, 7, 1), (8, 16, -1))):
                    part_yz.append(Copy(
                        ref.at[:, planes, pl.ds(a, 1)], ref.at[:, planes, pl.ds(b, 1)],
                        *sems[at_sem + side], (("gy", d),),
                    ))
            for side, d in ((0, 1), (1, -1)):
                part_yz.append(Copy(
                    z_send.at[k, group, side], z_halo.at[k, group, side],
                    *sems[8 + 2 * group + side], (("gz", d),),
                ))
            yz.append(part_yz)
        return x, yz[0], yz[1]

    def inner_flow(k, x, group=0):
        return flow_yz(k, x, group) + flow_x(k, x, 0) + flow_x(k, x, 1)

    arriving_x = []
    for k in range(SWEEPS):
        next_x, next_inner, next_outer = copies(k + 1)
        if k == 0:
            for c in k_yz:
                c.wait_recv()
            for side in range(2):
                outer_plane(side)
            start(h_copies[2:4])

            def prepare(x, carry):
                weights(x)
                return carry

            lax.fori_loop(1, 7, prepare, 0, unroll=True)
        else:
            for c in arriving_inner:
                c.wait_recv()

        def inner(x, tiles):
            update(k, x, inner_flow(k, x))
            return pack_z(k + 1, x, tiles)

        tiles = lax.fori_loop(1, 7, inner, (zero, zero), unroll=True)
        z_send[k + 1, 0, 0], z_send[k + 1, 0, 1] = tiles
        start(next_inner)
        if k > 0:
            for c in arriving_outer:
                c.wait_recv()
            for x, side in ((0, 1), (7, 0)):
                part[k, 1 - side] = (flow_yz(k, x, 1) + flow_x(k, x, side)).reshape(8, E, LANES)
            if k == 2:
                start(h_copies[4:])
        for c in (k_x, h_copies[:4], arriving_x, h_copies[4:])[k]:
            c.wait_recv()
        for side in range(2):
            if k == 1:
                first_halo(side)
            if k == 3:
                third_halo(side)
        for x, side in ((0, 0), (7, 1)):
            if k == 0:
                weights(x)
                flow = inner_flow(k, x, 1)
            else:
                flow = part[k, side].reshape(2, 2, 2, E, LANES) + flow_x(k, x, side)
            update(k, x, flow)
        if k % 2:
            start(next_x)
        tiles = (zero, zero)
        for x in (0, 7):
            tiles = pack_z(k + 1, x, tiles)
        z_send[k + 1, 1, 0], z_send[k + 1, 1, 1] = tiles
        start(next_outer)
        arriving_x, arriving_inner, arriving_outer = next_x, next_inner, next_outer

    out = pltpu.make_async_copy(
        basis.at[SWEEPS, :, pl.ds(1, E), pl.ds(8, E)], out_p, out_sem.at[0]
    )
    out.start()

    def split_z(values):
        pair = values.reshape(4, 2, E, LANES)
        return (
            jnp.where(even, pair[:, 0], pair[:, 1]),
            jnp.where(even, pair[:, 1], pair[:, 0]),
        )

    def split_basis(x, carry):
        own, beside = split_z(center_of(SWEEPS, x))
        pz[:, 0, x] = own
        pz[:, 1, x] = beside
        return carry

    lax.fori_loop(0, E, split_basis, 0, unroll=True)
    for c in arriving_inner + arriving_outer:
        c.wait_recv()

    def image(x, flow):
        own, beside = split_z(flow * negdiag[x])
        iz[:, 0, x] = own
        iz[:, 1, x] = beside

    def inner_image(x, carry):
        image(x, inner_flow(SWEEPS, x))
        return carry

    lax.fori_loop(1, 7, inner_image, 0, unroll=True)
    for x, side in ((0, 1), (7, 0)):
        image(x, flow_yz(SWEEPS, x, 1) + flow_x(SWEEPS, x, side))

    def pair_of(a_x, a_y):
        return lax.rem(a_x + par_x, 2) * 2 + lax.rem(a_y + par_y, 2)

    def contract(i, carry):
        half, a_x, a_y = i // 4, lax.rem(i // 2, 2), lax.rem(i, 2)
        for a_z in range(2):
            for e in range(8):
                u_xy = pair_of(a_x + e // 4, a_y + e // 2 % 2)
                total = None
                for j in range(4):
                    x = 4 * half + j
                    term = pz[pair_of(a_x, a_y), a_z, x] * iz[u_xy, (a_z + e) % 2, x]
                    total = term if total is None else total + term
                sums[pl.ds(pl.multiple_of((i * 2 + a_z) * 64, 64) + e * 8, E)] = total
        return carry

    lax.fori_loop(0, 8, contract, 0, unroll=2)

    def halves(ref, count):
        results = []
        for y_half in range(2):
            total = ref[pl.ds(4 * y_half, count * 8, stride=8)]
            for y in range(1, 4):
                total = total + ref[pl.ds(4 * y_half + y, count * 8, stride=8)]
            total = total.reshape(count, E, LANES)
            total = total + pltpu.roll(total, 127, 2)
            total = total + pltpu.roll(total, 126, 2)
            results.append(total.reshape(count // 2, 2, E, LANES))
        return results

    low = (lax.rem(lane, E) == 0) & (lane != 0)
    high = (lax.rem(lane, E) == 4) & (lane != 124)

    def merge_z(pair):
        own, beside = pair[:, 0], pair[:, 1]
        own = own + jnp.where(low, pltpu.roll(beside, 4, 2), 0.0)
        return own + jnp.where(high, pltpu.roll(beside, 124, 2), 0.0)

    def pack_rows(entries):
        up, down = zero, zero
        for place, beside in entries:
            up = jnp.where(lane == place, pltpu.roll(beside, place + 4, 1), up)
            moved = pltpu.roll(beside, place, 1) if place else beside
            down = jnp.where(lane == place, moved, down)
        return up, down

    row_copies = []

    def move_rows(src, dst, moves):
        n = len(row_copies)
        row_copies.append(Copy(src, dst, r_send.at[n], r_recv.at[n], tuple(m for m in moves if m[1])))

    quarter = halves(sums, 16)
    entries = []
    for i in range(8):
        half, a_x, a_y = i // 4, i // 2 % 2, i % 2
        for y_half in range(2):
            place = (a_x * 2 + a_y) * 32 + (half ^ a_x) * 2 + (y_half ^ a_y)
            entries.append((place, quarter[y_half][i, 1]))
    zr_send[0], zr_send[1] = pack_rows(entries)
    order = [(m_x, m_y) for m_x in (1, -1, 0) for m_y in (1, -1, 0)]
    for side, m_z in ((0, 1), (1, -1)):
        for m_x, m_y in order:
            move_rows(
                zr_send.at[side], zr_halo.at[side, m_x + 1, m_y + 1],
                (("gx", m_x), ("gy", m_y), ("gz", m_z)),
            )
    start(row_copies)
    for y_half in range(2):
        merged = merge_z(quarter[y_half])
        for i in range(8):
            rows[i // 2 % 2, i % 2, i // 4, y_half] = merged[i]
    first = len(row_copies)
    for side, d in ((0, 1), (1, -1)):
        for side_y, d_y in ((0, 1), (1, -1)):
            move_rows(
                rows.at[1, 1, 1 - side, 1 - side_y], rows_d.at[side, side_y], (("gx", d), ("gy", d_y))
            )
    for side, d in ((0, 1), (1, -1)):
        move_rows(rows.at[1, 0, 1 - side], rows_x.at[side], (("gx", d),))
        move_rows(rows.at[0, 1, :, 1 - side], rows_y.at[side], (("gy", d),))
    start(row_copies[first:])
    first = len(row_copies)

    for c in arriving_x:
        c.wait_recv()
    for side in range(2):
        x = 7 * side
        weight = vx[0, side, x] * negdiag[x]
        for n, plane in enumerate((x + 1, 9 * side)):
            own, beside = split_z(basis[SWEEPS, :, plane, 8:16])
            faces[side, n, 0, :, 0] = own
            faces[side, n, 0, :, 1] = beside
            faces[side, n, 1, :, 0] = own * weight
            faces[side, n, 1, :, 1] = beside * weight

    def contract_faces(i, carry):
        side, a_y = i // 2, lax.rem(i, 2)
        s_xy = pair_of(0, a_y)
        for a_z in range(2):
            for e in range(8):
                u_xy = pair_of(e // 4, a_y + e // 2 % 2)
                u_z = (a_z + e) % 2
                total = faces[side, 0, 0, s_xy, a_z] * faces[side, 1, 1, u_xy, u_z]
                total = total + faces[side, 1, 0, s_xy, a_z] * faces[side, 0, 1, u_xy, u_z]
                face_sums[pl.ds(pl.multiple_of((i * 2 + a_z) * 64, 64) + e * 8, E)] = total
        return carry

    lax.fori_loop(0, 4, contract_faces, 0, unroll=True)
    quarter = halves(face_sums, 8)
    entries = []
    for i in range(4):
        half, a_y = i // 2, i % 2
        for y_half in range(2):
            entries.append((a_y * 32 + half * 2 + (y_half ^ a_y), quarter[y_half][i, 1]))
    zf_send[0], zf_send[1] = pack_rows(entries)
    for side, m_z in ((0, 1), (1, -1)):
        for m_y in (1, -1, 0):
            move_rows(zf_send.at[side], zf_halo.at[side, m_y + 1], (("gy", m_y), ("gz", m_z)))
    start(row_copies[first:])
    first = len(row_copies)
    face_own = []
    for y_half in range(2):
        merged = merge_z(quarter[y_half])
        face_own.append((merged[0], merged[2]))
        face_rows[y_half, 0], face_rows[y_half, 1] = merged[1], merged[3]
    for side, d in ((0, 1), (1, -1)):
        move_rows(face_rows.at[1 - side], face_rows_y.at[side], (("gy", d),))
    start(row_copies[first:])

    for c in row_copies:
        c.wait_recv()
    whole = [
        [
            rows[0, 0, h, y] + rows_x[h, y] + rows_y[y, h] + rows_d[h, y] + face_own[y][h] + face_rows_y[y, h]
            for y in range(2)
        ]
        for h in range(2)
    ]
    for side in range(2):
        packed = zero
        for m_x, m_y in order:
            inside = lane - 32 * (2 * abs(m_x) + abs(m_y))
            takes = (inside >= 0) & (inside < 4)
            if m_x:
                takes = takes & (inside // 2 == (1 - m_x) // 2)
            if m_y:
                takes = takes & (lax.rem(inside, 2) == (1 - m_y) // 2)
            value = zr_halo[side, m_x + 1, m_y + 1]
            if m_x == 0:
                value = value + zf_halo[side, m_y + 1]
            packed = packed + jnp.where(takes, value, 0.0)
        packed = packed + pltpu.roll(packed, 64, 1)
        packed = packed + pltpu.roll(packed, 32, 1)
        target = 124 * side
        for h in range(2):
            for y in range(2):
                shift = (target - (h * 2 + y)) % LANES
                moved = pltpu.roll(packed, shift, 1) if shift else packed
                whole[h][y] = whole[h][y] + jnp.where(lane == target, moved, 0.0)
    tiles = jnp.stack([whole[0][0], whole[0][1], whole[1][0], whole[1][1]])
    lows, highs = tiles, pltpu.roll(tiles, 124, 2)
    for b in range(4):
        inside = lax.rem(lane, 2 ** (b + 4))
        takes = (inside >= 2**b) & (inside < 2 ** (b + 1))
        lows = jnp.where(takes, pltpu.roll(lows, LANES - 7 * 2**b, 2), lows)
        highs = jnp.where(takes, pltpu.roll(highs, LANES - 7 * 2**b, 2), highs)
    picks = {0: ((0,), 1), 1: ((0, 1), 0), 2: ((1,), 1)}
    for d_x in range(3):
        for d_y in range(3):
            (halves_x, e_x), (halves_y, e_y) = picks[d_x], picks[d_y]
            low_tile, high_tile = None, None
            for h in halves_x:
                for y in halves_y:
                    n = h * 2 + y
                    low_tile = lows[n] if low_tile is None else low_tile + lows[n]
                    high_tile = highs[n] if high_tile is None else high_tile + highs[n]
            e = e_x * 4 + e_y * 2
            out_row = (d_x * 3 + d_y) * 3
            out_c[out_row:out_row + 1, :] = low_tile[e + 1:e + 2, :16]
            out_c[out_row + 1:out_row + 2, :] = low_tile[e:e + 1, :16] + high_tile[e:e + 1, :16]
            out_c[out_row + 2:out_row + 3, :] = high_tile[e + 1:e + 2, :16]
    out.wait()
    for c in started:
        c.wait_send()


def shards(permeability, well_flags, support_mask):
    f32 = jnp.float32
    vmem = pltpu.VMEM
    dma = pltpu.SemaphoreType.DMA
    any_spec = pl.BlockSpec(memory_space=pltpu.HBM)
    prolongation, coarse = pl.pallas_call(
        kernel,
        out_shape=(
            pltpu.VMEM((8, E, E, LANES), f32),
            pltpu.VMEM((27, 16), f32),
        ),
        in_specs=[any_spec] * 3,
        out_specs=(pl.BlockSpec(memory_space=pltpu.VMEM), pl.BlockSpec(memory_space=pltpu.VMEM)),
        scratch_shapes=[
            vmem((10, E, LANES), f32),
            vmem((E, 24, LANES), f32),
            vmem((E, E, LANES), f32),
            vmem((2, E, LANES), f32),
            vmem((2, E, LANES), f32),
            vmem((E, E, LANES), jnp.int32),
            vmem((8, E, E, LANES), jnp.int32),
            vmem((SWEEPS + 1, 8, 10, 24, LANES), f32),
            vmem((SWEEPS + 1, 2, 2, E, LANES), f32),
            vmem((SWEEPS + 1, 2, 2, E, LANES), f32),
            vmem((2, 2, E, E, LANES), f32),
            vmem((2, 2, E, E, LANES), f32),
            vmem((2, 2, E, E, LANES), f32),
            vmem((E, E, LANES), f32),
            vmem((SWEEPS, 2, 8, E, LANES), f32),
            vmem((4, 2, E, E, LANES), f32),
            vmem((4, 2, E, E, LANES), f32),
            vmem((1024, LANES), f32),
            vmem((2, 2, 2, 2, E, LANES), f32),
            vmem((2, 2, E, LANES), f32),
            vmem((2, 2, E, LANES), f32),
            vmem((2, 2, E, LANES), f32),
            vmem((2, E, LANES), f32),
            vmem((2, 3, 3, E, LANES), f32),
            vmem((2, 2, 2, 4, 2, E, LANES), f32),
            vmem((512, LANES), f32),
            vmem((2, 2, E, LANES), f32),
            vmem((2, 2, E, LANES), f32),
            vmem((2, E, LANES), f32),
            vmem((2, 3, E, LANES), f32),
            vmem((2, 3, E, LANES), f32),
            vmem((2, 3, E, LANES), f32),
            vmem((2, 8, E, LANES), jnp.int32),
            vmem((2, 8, E, LANES), f32),
            vmem((2, E, LANES), f32),
            dma((5,)),
            dma((6,)),
            dma((6,)),
            dma((SWEEPS + 1, 12)),
            dma((SWEEPS + 1, 12)),
            dma((34,)),
            dma((34,)),
            dma((6,)),
            dma((6,)),
            dma((1,)),
        ],
        compiler_params=pltpu.CompilerParams(
            collective_id=0, has_side_effects=True, vmem_limit_bytes=60 * 1024 * 1024
        ),
        name="smooth_and_contract",
    )(permeability, well_flags, support_mask)
    return prolongation, coarse.reshape(3, 3, 3, 1, 1, 16)


def solution(mesh):
    placed = (P(None, "gx", "gy", "gz"), P("gx", "gy", "gz"), P(None, "gx", "gy", "gz"))
    return jax.shard_map(
        shards,
        mesh=mesh,
        in_specs=placed,
        out_specs=(P(None, "gx", "gy", "gz"), P(None, None, None, "gx", "gy", "gz")),
        check_vma=False,
    )
```

```python
import jax
import jax.numpy as jnp
from jax import lax
from jax.experimental import pallas as pl
from jax.experimental.pallas import tpu as pltpu
from jax.sharding import PartitionSpec as P

MESH = pl.DeviceIdType.MESH
AXES = ("gx", "gy", "gz")
COUNT = {"gx": 16, "gy": 4, "gz": 4}
SWEEPS = 4
STEP = 2.0 / 3.0
WELL = 0.05
E = 8
LANES = 128
ROW0 = 8


def harmonic(lower, upper):
    return 2.0 * lower * upper / (lower + upper)


def kernel(
    perm, flags, mask, out_p, out_c,
    kx, ky, kz, kz_send, kz_halo, fl, mk, basis, z_send, z_halo,
    vx, vy, vz, negdiag, part, pz, iz, sums, rows, rows_x, rows_y, rows_d, zr_send, zr_halo,
    faces, face_sums, face_rows, face_rows_y, zf_send, zf_halo, a_send, a_halo, mask_halo, part_halo, halo_vx, t_yz, near_sum,
    load_sem, k_send, k_recv, p_send, p_recv, r_send, r_recv, h_send, h_recv, out_sem,
):
    at = {axis: lax.axis_index(axis) for axis in AXES}
    has = {}
    for axis in AXES:
        has[axis, 1] = at[axis] < COUNT[axis] - 1
        has[axis, -1] = at[axis] > 0
    par_x, par_y = lax.rem(at["gx"], 2), lax.rem(at["gy"], 2)
    lane = lax.broadcasted_iota(jnp.int32, (E, LANES), 1)
    row = lax.broadcasted_iota(jnp.int32, (E, LANES), 0)
    even = lax.rem(lane // E, 2) == 0

    loads = [
        pltpu.make_async_copy(perm.at[0], kx.at[pl.ds(1, E)], load_sem.at[0]),
        pltpu.make_async_copy(perm.at[1], ky.at[:, pl.ds(ROW0, E)], load_sem.at[1]),
        pltpu.make_async_copy(perm.at[2], kz, load_sem.at[2]),
        pltpu.make_async_copy(flags, fl, load_sem.at[3]),
        pltpu.make_async_copy(mask, mk, load_sem.at[4]),
    ]
    for load in loads:
        load.start()

    barrier = pltpu.get_barrier_semaphore()
    expected = 0
    for axis in AXES:
        for d in (1, -1):
            @pl.when(has[axis, d])
            def _():
                pl.semaphore_signal(
                    barrier, inc=1, device_id={axis: at[axis] + d}, device_id_type=MESH
                )
            expected = expected + has[axis, d].astype(jnp.int32)

    def shift_to(axis, d):
        size = COUNT[axis]
        return lax.rem(at[axis] + d + size, size)

    class Copy:
        def __init__(self, src, dst, ssem, rsem, moves):
            self.send_if = None
            self.recv_if = None
            target = {}
            for axis, d in moves:
                target[axis] = shift_to(axis, d)
                s, r = has[axis, d], has[axis, -d]
                self.send_if = s if self.send_if is None else self.send_if & s
                self.recv_if = r if self.recv_if is None else self.recv_if & r
            self.copy = pltpu.make_async_remote_copy(
                src_ref=src, dst_ref=dst, send_sem=ssem, recv_sem=rsem,
                device_id=target, device_id_type=MESH,
            )

        def start(self):
            pl.when(self.send_if)(self.copy.start)

        def wait_recv(self):
            pl.when(self.recv_if)(self.copy.wait_recv)

        def wait_send(self):
            pl.when(self.send_if)(self.copy.wait_send)

    started = []

    def start(copies):
        for c in copies:
            c.start()
        started.extend(copies)

    zero = jnp.zeros((E, LANES), jnp.float32)
    for d, k_plane in ((-1, 0), (1, 9)):
        side = (d + 1) // 2

        @pl.when(jnp.logical_not(has["gx", d]))
        def _():
            kx[k_plane] = zero
            a_halo[side] = jnp.ones((3, E, LANES), jnp.float32)
            mask_halo[side] = jnp.zeros((8, E, LANES), jnp.int32)
            part_halo[side] = jnp.zeros((8, E, LANES), jnp.float32)
            for k in range(1, SWEEPS + 1):
                basis[k, :, k_plane, 8:16] = jnp.zeros((8, E, LANES), jnp.float32)
            rows_x[side] = jnp.zeros((2, E, LANES), jnp.float32)

        @pl.when(jnp.logical_not(has["gy", d]))
        def _():
            y_row = 7 if d < 0 else 16
            ky[:, y_row:y_row + 1] = jnp.zeros((E, 1, LANES), jnp.float32)

            def clear(i, carry):
                basis[1 + i // 8, lax.rem(i, 8), 1:9, y_row:y_row + 1] = jnp.zeros(
                    (E, 1, LANES), jnp.float32
                )
                return carry

            lax.fori_loop(0, 8 * SWEEPS, clear, 0)
            rows_y[side] = jnp.zeros((2, E, LANES), jnp.float32)
            face_rows_y[side] = jnp.zeros((2, E, LANES), jnp.float32)

        @pl.when(jnp.logical_not(has["gz", d]))
        def _():
            kz_halo[side] = zero
            for k in range(1, SWEEPS + 1):
                z_halo[k, 0, side] = zero
                z_halo[k, 1, side] = zero

        for e in (1, -1):
            @pl.when(jnp.logical_not(has["gx", d] & has["gy", e]))
            def _():
                rows_d[side, (e + 1) // 2] = zero

    for m_z in (1, -1):
        side = (1 - m_z) // 2
        for m_y in (1, 0, -1):
            near = has["gz", -m_z]
            if m_y:
                near = near & has["gy", -m_y]

            @pl.when(jnp.logical_not(near))
            def _():
                zf_halo[side, m_y + 1] = zero

            for m_x in (1, 0, -1):
                there = near & has["gx", -m_x] if m_x else near

                @pl.when(jnp.logical_not(there))
                def _():
                    zr_halo[side, m_x + 1, m_y + 1] = zero

    for load in loads[:3]:
        load.wait()
    for side in range(2):
        tile = zero
        for x in range(E):
            shift = (x - 127) % LANES if side == 0 else x
            moved = pltpu.roll(kz[x], shift, 1) if shift else kz[x]
            tile = jnp.where(lane == x, moved, tile)
        kz_send[side] = tile
    pl.semaphore_wait(barrier, expected)
    k_x = [
        Copy(kx.at[8], kx.at[0], k_send.at[0], k_recv.at[0], (("gx", 1),)),
        Copy(kx.at[1], kx.at[9], k_send.at[1], k_recv.at[1], (("gx", -1),)),
    ]
    k_yz = [
        Copy(ky.at[:, pl.ds(15, 1)], ky.at[:, pl.ds(7, 1)], k_send.at[2], k_recv.at[2], (("gy", 1),)),
        Copy(ky.at[:, pl.ds(8, 1)], ky.at[:, pl.ds(16, 1)], k_send.at[3], k_recv.at[3], (("gy", -1),)),
        Copy(kz_send.at[0], kz_halo.at[0], k_send.at[4], k_recv.at[4], (("gz", 1),)),
        Copy(kz_send.at[1], kz_halo.at[1], k_send.at[5], k_recv.at[5], (("gz", -1),)),
    ]
    start(k_x)
    start(k_yz)
    for load in loads[3:]:
        load.wait()
    h_copies = []
    for src, dst in ((mk, mask_halo), (a_send, a_halo), (part, part_halo)):
        for side, d in ((0, -1), (1, 1)):
            n = len(h_copies)
            if src is mk:
                block = mk.at[:, 7 * side]
            else:
                block = src.at[2, side] if src is part else src.at[side]
            h_copies.append(Copy(block, dst.at[1 - side], h_send.at[n], h_recv.at[n], (("gx", d),)))
    start(h_copies[:2])

    def faces_yz(x):
        here = ky[x, 8:16]
        t_y = (harmonic(ky[x, 7:15], here), harmonic(here, ky[x, 9:17]))
        here = kz[x]
        before = jnp.where(
            lane == 0, pltpu.roll(kz_halo[0], LANES - x, 1), pltpu.roll(here, 1, 1)
        )
        after = jnp.where(
            lane == 127, pltpu.roll(kz_halo[1], 127 - x, 1), pltpu.roll(here, 127, 1)
        )
        return t_y, (harmonic(before, here), harmonic(here, after))

    def prepare(x, inner_x):
        t_y, t_z = faces_yz(x)
        for n in range(2):
            t_yz[x, n] = t_y[n]
            t_yz[x, 2 + n] = t_z[n]
        total = t_y[0] + t_y[1] + t_z[0] + t_z[1]
        for n in inner_x:
            total = total + harmonic(kx[x + n], kx[x + n + 1])
        total = total + WELL * fl[x].astype(jnp.float32)
        near_sum[x] = total
        place = lax.rem(lane, E)
        cross_y = jnp.where(row == 0, t_y[0], jnp.where(row == 7, t_y[1], 0.0))
        cross_z = jnp.where(place == 0, t_z[0], jnp.where(place == 7, t_z[1], 0.0))
        return total, cross_y, cross_z

    def first_values(masks, plane, own_x, scale, t_x, t_y, t_z):
        def support(b_x, b_y, own):
            n = 4 * b_x + 2 * b_y
            pair = (masks(n), masks(n + 1)) if own else (masks(n + 1), masks(n))
            return jnp.where(even, *pair).astype(jnp.float32)

        u_y = support(own_x, 1 - par_y, True) * (t_y * scale)
        u_z = support(own_x, par_y, False) * (t_z * scale)
        u_x = zero if t_x is None else support(1 - own_x, par_y, True) * (t_x * scale)

        def put(b_x, b_y, own_z, beside_z):
            n = 4 * b_x + 2 * b_y
            basis[1, n, plane, 8:16] = jnp.where(even, own_z, beside_z)
            basis[1, n + 1, plane, 8:16] = jnp.where(even, beside_z, own_z)

        put(own_x, par_y, 1.0 - (u_x + u_y + u_z), u_z)
        put(1 - own_x, par_y, u_x, zero)
        put(own_x, 1 - par_y, u_y, zero)
        put(1 - own_x, 1 - par_y, zero, zero)

    def first_halo(side):
        t_x = harmonic(kx[8 * side], kx[8 * side + 1])
        scale = STEP / (a_halo[side, 0] + t_x)
        halo_vx[side] = t_x * scale
        first_values(
            lambda n: mask_halo[side, n], 9 * side, 1 - par_x, scale, t_x, a_halo[side, 1], a_halo[side, 2]
        )

    def third_halo(side):
        plane = 9 * side
        flow = part_halo[side] + halo_vx[side] * basis[2, :, 1 + 7 * side, 8:16]
        center = basis[2, :, plane, 8:16]
        change = mask_halo[side].astype(jnp.float32) * flow
        basis[3, :, plane, 8:16] = center + change - center * jnp.sum(change, axis=0)

    def weights(x):
        here = kx[x + 1]
        t_x = (harmonic(kx[x], here), harmonic(here, kx[x + 2]))
        t_y, t_z = (t_yz[x, 0], t_yz[x, 1]), (t_yz[x, 2], t_yz[x, 3])
        diagonal = near_sum[x]
        negdiag[x] = -1.5 * diagonal
        scale = STEP / diagonal
        for b in range(2):
            keep_x = (par_x == b).astype(jnp.float32)
            keep_y = (par_y == b).astype(jnp.float32)
            own_z = even if b == 0 else jnp.logical_not(even)
            for side in range(2):
                inner = 4 - side
                vx[b, side, x] = t_x[side] * scale * jnp.where(x == inner, keep_x, 1.0)
                vy[b, side, x] = t_y[side] * scale * jnp.where(row == inner, keep_y, 1.0)
                cut = (lax.rem(lane, E) == inner) & jnp.logical_not(own_z)
                vz[b, side, x] = jnp.where(cut, 0.0, t_z[side] * scale)

    def center_of(k, x):
        return basis[k, :, x + 1, 8:16].reshape(2, 2, 2, E, LANES)

    def flow_x(k, x, side):
        near = basis[k, :, x + 2 * side, 8:16].reshape(2, 2, 2, E, LANES)
        return vx[:, side, x][:, None, None] * near

    def flow_yz(k, x, group):
        center = basis[k, :, x + 1, 8:16]
        total = -STEP * center.reshape(2, 2, 2, E, LANES)
        halo = jnp.where(lax.rem(lane, 2) == 0, z_halo[k, group, 0], z_halo[k, group, 1])
        ends = [pltpu.roll(halo, LANES - 2 * (n * 8 + x), 1) if n else
                pltpu.roll(halo, lax.rem(LANES - 2 * x, LANES), 1) for n in range(8)]
        for side in range(2):
            near = basis[k, :, x + 1, 7 + 2 * side:15 + 2 * side].reshape(2, 2, 2, E, LANES)
            total = total + vy[:, side, x][None, :, None] * near
            edge = lane == (0, 127)[side]
            moved = [
                jnp.where(edge, ends[n], pltpu.roll(center[n], (1, 127)[side], 1)) for n in range(8)
            ]
            near = jnp.stack(moved).reshape(2, 2, 2, E, LANES)
            total = total + vz[:, side, x][None, None] * near
        return total

    def update(k, x, flow):
        center = center_of(k, x)
        support = mk[:, x].astype(jnp.float32).reshape(2, 2, 2, E, LANES)
        change = support * flow
        change_sum = jnp.sum(change, axis=(0, 1, 2))
        fresh = center + change - center * change_sum
        basis[k + 1, :, x + 1, 8:16] = fresh.reshape(8, E, LANES)

    def pack_z(k, x, tiles):
        up, down = tiles
        for s in range(8):
            place = 2 * (s * 8 + x)
            before = lax.rem(place + 127, LANES)
            value = basis[k, s, x + 1, 8:16]
            up = jnp.where(lane == place, pltpu.roll(value, place + 1, 1), up)
            down = jnp.where(lane == before, pltpu.roll(value, before, 1), down)
        return up, down

    def copies(k):
        ref = basis.at[k]
        own = pl.ds(8, E)
        sems = [(p_send.at[k, i], p_recv.at[k, i]) for i in range(12)]
        x = [
            Copy(ref.at[:, 8, own], ref.at[:, 0, own], *sems[0], (("gx", 1),)),
            Copy(ref.at[:, 1, own], ref.at[:, 9, own], *sems[1], (("gx", -1),)),
        ] if k % 2 == 0 else []
        yz = []
        for group in range(2):
            part_yz = []
            for n, planes in enumerate((pl.ds(2, 6),) if group == 0 else (pl.ds(1, 1), pl.ds(8, 1))):
                at_sem = 2 + 2 * group + 2 * n
                for side, (a, b, d) in enumerate(((15, 7, 1), (8, 16, -1))):
                    part_yz.append(Copy(
                        ref.at[:, planes, pl.ds(a, 1)], ref.at[:, planes, pl.ds(b, 1)],
                        *sems[at_sem + side], (("gy", d),),
                    ))
            for side, d in ((0, 1), (1, -1)):
                part_yz.append(Copy(
                    z_send.at[k, group, side], z_halo.at[k, group, side],
                    *sems[8 + 2 * group + side], (("gz", d),),
                ))
            yz.append(part_yz)
        return x, yz[0], yz[1]

    def inner_flow(k, x, group=0):
        return flow_yz(k, x, group) + flow_x(k, x, 0) + flow_x(k, x, 1)

    def pack_outer(k):
        tiles = (zero, zero)
        for x in (0, 7):
            tiles = pack_z(k, x, tiles)
        z_send[k, 1, 0], z_send[k, 1, 1] = tiles

    arriving_x, arriving_inner, arriving_outer = copies(1)
    for c in k_yz:
        c.wait_recv()
    for side in range(2):
        for n, tile in enumerate(prepare(7 * side, (1 - side,))):
            a_send[side, n] = tile
    start(h_copies[2:4])

    def first_inner(x, tiles):
        total, t_y, t_z = prepare(x, (0, 1))
        first_values(lambda n: mk[n, x], x + 1, par_x, STEP / total, None, t_y, t_z)
        return pack_z(1, x, tiles)

    tiles = lax.fori_loop(1, 7, first_inner, (zero, zero), unroll=True)
    z_send[1, 0, 0], z_send[1, 0, 1] = tiles
    start(arriving_inner)
    for c in k_x:
        c.wait_recv()
    for side in range(2):
        x = 7 * side
        t_x = harmonic(kx[8 * side], kx[8 * side + 1])
        near_sum[x] = a_send[side, 0] + t_x
        first_values(
            lambda n: mk[n, x], x + 1, par_x, STEP / near_sum[x], t_x, a_send[side, 1], a_send[side, 2]
        )
    pack_outer(1)
    start(arriving_outer)

    def weigh(x, carry):
        weights(x)
        return carry

    lax.fori_loop(0, E, weigh, 0, unroll=True)
    for k in range(1, SWEEPS):
        next_x, next_inner, next_outer = copies(k + 1)
        for c in arriving_inner:
            c.wait_recv()

        def inner(x, tiles):
            update(k, x, inner_flow(k, x))
            return pack_z(k + 1, x, tiles)

        tiles = lax.fori_loop(1, 7, inner, (zero, zero), unroll=True)
        z_send[k + 1, 0, 0], z_send[k + 1, 0, 1] = tiles
        start(next_inner)
        for c in arriving_outer:
            c.wait_recv()
        for x, side in ((0, 1), (7, 0)):
            part[k, 1 - side] = (flow_yz(k, x, 1) + flow_x(k, x, side)).reshape(8, E, LANES)
        if k == 2:
            start(h_copies[4:])
        for c in (h_copies[:4], arriving_x, h_copies[4:])[k - 1]:
            c.wait_recv()
        for side in range(2):
            if k == 1:
                first_halo(side)
            if k == 3:
                third_halo(side)
        for x, side in ((0, 0), (7, 1)):
            update(k, x, part[k, side].reshape(2, 2, 2, E, LANES) + flow_x(k, x, side))
        if k % 2:
            start(next_x)
        pack_outer(k + 1)
        start(next_outer)
        arriving_x, arriving_inner, arriving_outer = next_x, next_inner, next_outer

    out = pltpu.make_async_copy(
        basis.at[SWEEPS, :, pl.ds(1, E), pl.ds(8, E)], out_p, out_sem.at[0]
    )
    out.start()

    def split_z(values):
        pair = values.reshape(4, 2, E, LANES)
        return (
            jnp.where(even, pair[:, 0], pair[:, 1]),
            jnp.where(even, pair[:, 1], pair[:, 0]),
        )

    def split_basis(x, carry):
        own, beside = split_z(center_of(SWEEPS, x))
        pz[:, 0, x] = own
        pz[:, 1, x] = beside
        return carry

    lax.fori_loop(0, E, split_basis, 0, unroll=True)
    for c in arriving_inner + arriving_outer:
        c.wait_recv()

    def image(x, flow):
        own, beside = split_z(flow * negdiag[x])
        iz[:, 0, x] = own
        iz[:, 1, x] = beside

    def inner_image(x, carry):
        image(x, inner_flow(SWEEPS, x))
        return carry

    lax.fori_loop(1, 7, inner_image, 0, unroll=True)
    for x, side in ((0, 1), (7, 0)):
        image(x, flow_yz(SWEEPS, x, 1) + flow_x(SWEEPS, x, side))

    def pair_of(a_x, a_y):
        return lax.rem(a_x + par_x, 2) * 2 + lax.rem(a_y + par_y, 2)

    def contract(i, carry):
        half, a_x, a_y = i // 4, lax.rem(i // 2, 2), lax.rem(i, 2)
        for a_z in range(2):
            for e in range(8):
                u_xy = pair_of(a_x + e // 4, a_y + e // 2 % 2)
                total = None
                for j in range(4):
                    x = 4 * half + j
                    term = pz[pair_of(a_x, a_y), a_z, x] * iz[u_xy, (a_z + e) % 2, x]
                    total = term if total is None else total + term
                sums[pl.ds(pl.multiple_of((i * 2 + a_z) * 64, 64) + e * 8, E)] = total
        return carry

    lax.fori_loop(0, 8, contract, 0, unroll=2)

    def halves(ref, count):
        results = []
        for y_half in range(2):
            total = ref[pl.ds(4 * y_half, count * 8, stride=8)]
            for y in range(1, 4):
                total = total + ref[pl.ds(4 * y_half + y, count * 8, stride=8)]
            total = total.reshape(count, E, LANES)
            total = total + pltpu.roll(total, 127, 2)
            total = total + pltpu.roll(total, 126, 2)
            results.append(total.reshape(count // 2, 2, E, LANES))
        return results

    low = (lax.rem(lane, E) == 0) & (lane != 0)
    high = (lax.rem(lane, E) == 4) & (lane != 124)

    def merge_z(pair):
        own, beside = pair[:, 0], pair[:, 1]
        own = own + jnp.where(low, pltpu.roll(beside, 4, 2), 0.0)
        return own + jnp.where(high, pltpu.roll(beside, 124, 2), 0.0)

    def pack_rows(entries):
        up, down = zero, zero
        for place, beside in entries:
            up = jnp.where(lane == place, pltpu.roll(beside, place + 4, 1), up)
            moved = pltpu.roll(beside, place, 1) if place else beside
            down = jnp.where(lane == place, moved, down)
        return up, down

    row_copies = []

    def move_rows(src, dst, moves):
        n = len(row_copies)
        row_copies.append(Copy(src, dst, r_send.at[n], r_recv.at[n], tuple(m for m in moves if m[1])))

    quarter = halves(sums, 16)
    entries = []
    for i in range(8):
        half, a_x, a_y = i // 4, i // 2 % 2, i % 2
        for y_half in range(2):
            place = (a_x * 2 + a_y) * 32 + (half ^ a_x) * 2 + (y_half ^ a_y)
            entries.append((place, quarter[y_half][i, 1]))
    zr_send[0], zr_send[1] = pack_rows(entries)
    order = [(m_x, m_y) for m_x in (1, -1, 0) for m_y in (1, -1, 0)]
    for side, m_z in ((0, 1), (1, -1)):
        for m_x, m_y in order:
            move_rows(
                zr_send.at[side], zr_halo.at[side, m_x + 1, m_y + 1],
                (("gx", m_x), ("gy", m_y), ("gz", m_z)),
            )
    start(row_copies)
    for y_half in range(2):
        merged = merge_z(quarter[y_half])
        for i in range(8):
            rows[i // 2 % 2, i % 2, i // 4, y_half] = merged[i]
    first = len(row_copies)
    for side, d in ((0, 1), (1, -1)):
        for side_y, d_y in ((0, 1), (1, -1)):
            move_rows(
                rows.at[1, 1, 1 - side, 1 - side_y], rows_d.at[side, side_y], (("gx", d), ("gy", d_y))
            )
    for side, d in ((0, 1), (1, -1)):
        move_rows(rows.at[1, 0, 1 - side], rows_x.at[side], (("gx", d),))
        move_rows(rows.at[0, 1, :, 1 - side], rows_y.at[side], (("gy", d),))
    start(row_copies[first:])
    first = len(row_copies)

    for c in arriving_x:
        c.wait_recv()
    for side in range(2):
        x = 7 * side
        weight = vx[0, side, x] * negdiag[x]
        for n, plane in enumerate((x + 1, 9 * side)):
            own, beside = split_z(basis[SWEEPS, :, plane, 8:16])
            faces[side, n, 0, :, 0] = own
            faces[side, n, 0, :, 1] = beside
            faces[side, n, 1, :, 0] = own * weight
            faces[side, n, 1, :, 1] = beside * weight

    def contract_faces(i, carry):
        side, a_y = i // 2, lax.rem(i, 2)
        s_xy = pair_of(0, a_y)
        for a_z in range(2):
            for e in range(8):
                u_xy = pair_of(e // 4, a_y + e // 2 % 2)
                u_z = (a_z + e) % 2
                total = faces[side, 0, 0, s_xy, a_z] * faces[side, 1, 1, u_xy, u_z]
                total = total + faces[side, 1, 0, s_xy, a_z] * faces[side, 0, 1, u_xy, u_z]
                face_sums[pl.ds(pl.multiple_of((i * 2 + a_z) * 64, 64) + e * 8, E)] = total
        return carry

    lax.fori_loop(0, 4, contract_faces, 0, unroll=True)
    quarter = halves(face_sums, 8)
    entries = []
    for i in range(4):
        half, a_y = i // 2, i % 2
        for y_half in range(2):
            entries.append((a_y * 32 + half * 2 + (y_half ^ a_y), quarter[y_half][i, 1]))
    zf_send[0], zf_send[1] = pack_rows(entries)
    for side, m_z in ((0, 1), (1, -1)):
        for m_y in (1, -1, 0):
            move_rows(zf_send.at[side], zf_halo.at[side, m_y + 1], (("gy", m_y), ("gz", m_z)))
    start(row_copies[first:])
    first = len(row_copies)
    face_own = []
    for y_half in range(2):
        merged = merge_z(quarter[y_half])
        face_own.append((merged[0], merged[2]))
        face_rows[y_half, 0], face_rows[y_half, 1] = merged[1], merged[3]
    for side, d in ((0, 1), (1, -1)):
        move_rows(face_rows.at[1 - side], face_rows_y.at[side], (("gy", d),))
    start(row_copies[first:])

    for c in row_copies:
        c.wait_recv()
    whole = [
        [
            rows[0, 0, h, y] + rows_x[h, y] + rows_y[y, h] + rows_d[h, y] + face_own[y][h] + face_rows_y[y, h]
            for y in range(2)
        ]
        for h in range(2)
    ]
    for side in range(2):
        packed = zero
        for m_x, m_y in order:
            inside = lane - 32 * (2 * abs(m_x) + abs(m_y))
            takes = (inside >= 0) & (inside < 4)
            if m_x:
                takes = takes & (inside // 2 == (1 - m_x) // 2)
            if m_y:
                takes = takes & (lax.rem(inside, 2) == (1 - m_y) // 2)
            value = zr_halo[side, m_x + 1, m_y + 1]
            if m_x == 0:
                value = value + zf_halo[side, m_y + 1]
            packed = packed + jnp.where(takes, value, 0.0)
        target = 124 * side
        for h in range(2):
            for y in range(2):
                total = None
                for group in range(4):
                    shift = (target - group * 32 - (h * 2 + y)) % LANES
                    moved = pltpu.roll(packed, shift, 1) if shift else packed
                    total = moved if total is None else total + moved
                whole[h][y] = whole[h][y] + jnp.where(lane == target, total, 0.0)
    tiles = jnp.stack([whole[0][0], whole[0][1], whole[1][0], whole[1][1]])

    def gather(offset):
        values = tiles
        for step, (spread, size) in enumerate(((7, 1), (28, 4))):
            result = None
            for n in range(4):
                shift = (LANES - spread * n - (0 if step else offset)) % LANES
                moved = pltpu.roll(values, shift, 2) if shift else values
                here = lax.rem(lane, 32) == n if step == 0 else lane // 4 == n
                result = moved if result is None else jnp.where(here, moved, result)
            values = result
        return values

    lows, highs = gather(0), gather(4)
    picks = {0: ((0,), 1), 1: ((0, 1), 0), 2: ((1,), 1)}
    for d_x in range(3):
        for d_y in range(3):
            (halves_x, e_x), (halves_y, e_y) = picks[d_x], picks[d_y]
            low_tile, high_tile = None, None
            for h in halves_x:
                for y in halves_y:
                    n = h * 2 + y
                    low_tile = lows[n] if low_tile is None else low_tile + lows[n]
                    high_tile = highs[n] if high_tile is None else high_tile + highs[n]
            e = e_x * 4 + e_y * 2
            out_row = (d_x * 3 + d_y) * 3
            out_c[out_row:out_row + 1, :] = low_tile[e + 1:e + 2, :16]
            out_c[out_row + 1:out_row + 2, :] = low_tile[e:e + 1, :16] + high_tile[e:e + 1, :16]
            out_c[out_row + 2:out_row + 3, :] = high_tile[e + 1:e + 2, :16]
    out.wait()
    for c in started:
        c.wait_send()


def shards(permeability, well_flags, support_mask):
    f32 = jnp.float32
    vmem = pltpu.VMEM
    dma = pltpu.SemaphoreType.DMA
    any_spec = pl.BlockSpec(memory_space=pltpu.HBM)
    prolongation, coarse = pl.pallas_call(
        kernel,
        out_shape=(
            pltpu.VMEM((8, E, E, LANES), f32),
            pltpu.VMEM((27, 16), f32),
        ),
        in_specs=[any_spec] * 3,
        out_specs=(pl.BlockSpec(memory_space=pltpu.VMEM), pl.BlockSpec(memory_space=pltpu.VMEM)),
        scratch_shapes=[
            vmem((10, E, LANES), f32),
            vmem((E, 24, LANES), f32),
            vmem((E, E, LANES), f32),
            vmem((2, E, LANES), f32),
            vmem((2, E, LANES), f32),
            vmem((E, E, LANES), jnp.int32),
            vmem((8, E, E, LANES), jnp.int32),
            vmem((SWEEPS + 1, 8, 10, 24, LANES), f32),
            vmem((SWEEPS + 1, 2, 2, E, LANES), f32),
            vmem((SWEEPS + 1, 2, 2, E, LANES), f32),
            vmem((2, 2, E, E, LANES), f32),
            vmem((2, 2, E, E, LANES), f32),
            vmem((2, 2, E, E, LANES), f32),
            vmem((E, E, LANES), f32),
            vmem((SWEEPS, 2, 8, E, LANES), f32),
            vmem((4, 2, E, E, LANES), f32),
            vmem((4, 2, E, E, LANES), f32),
            vmem((1024, LANES), f32),
            vmem((2, 2, 2, 2, E, LANES), f32),
            vmem((2, 2, E, LANES), f32),
            vmem((2, 2, E, LANES), f32),
            vmem((2, 2, E, LANES), f32),
            vmem((2, E, LANES), f32),
            vmem((2, 3, 3, E, LANES), f32),
            vmem((2, 2, 2, 4, 2, E, LANES), f32),
            vmem((512, LANES), f32),
            vmem((2, 2, E, LANES), f32),
            vmem((2, 2, E, LANES), f32),
            vmem((2, E, LANES), f32),
            vmem((2, 3, E, LANES), f32),
            vmem((2, 3, E, LANES), f32),
            vmem((2, 3, E, LANES), f32),
            vmem((2, 8, E, LANES), jnp.int32),
            vmem((2, 8, E, LANES), f32),
            vmem((2, E, LANES), f32),
            vmem((E, 4, E, LANES), f32),
            vmem((E, E, LANES), f32),
            dma((5,)),
            dma((6,)),
            dma((6,)),
            dma((SWEEPS + 1, 12)),
            dma((SWEEPS + 1, 12)),
            dma((34,)),
            dma((34,)),
            dma((6,)),
            dma((6,)),
            dma((1,)),
        ],
        compiler_params=pltpu.CompilerParams(
            collective_id=0, has_side_effects=True, vmem_limit_bytes=60 * 1024 * 1024
        ),
        name="smooth_and_contract",
    )(permeability, well_flags, support_mask)
    return prolongation, coarse.reshape(3, 3, 3, 1, 1, 16)


def solution(mesh):
    placed = (P(None, "gx", "gy", "gz"), P("gx", "gy", "gz"), P(None, "gx", "gy", "gz"))
    return jax.shard_map(
        shards,
        mesh=mesh,
        in_specs=placed,
        out_specs=(P(None, "gx", "gy", "gz"), P(None, None, None, "gx", "gy", "gz")),
        check_vma=False,
    )
```

```python
import functools

import jax
import jax.numpy as jnp
from jax import lax
from jax.experimental import pallas as pl
from jax.experimental.pallas import tpu as pltpu
from jax.sharding import PartitionSpec as P

MESH = pl.DeviceIdType.MESH
AXES = ("gx", "gy", "gz")
COUNT = {"gx": 16, "gy": 4, "gz": 4}
SWEEPS = 4
STEP = 2.0 / 3.0
WELL = 0.05
E = 8
LANES = 128
ROW0 = 8


def harmonic(lower, upper):
    return 2.0 * lower * upper / (lower + upper)


def kernel(
    perm, flags, mask, out_p, out_c,
    kx, ky, kz, kz_send, kz_halo, fl, mk, basis, z_send, z_halo,
    vx, vy, vz, negdiag, part, pz, iz, sums, rows, rows_x, rows_y, rows_d, zr_send, zr_halo,
    faces, face_sums, face_rows, face_rows_y, zf_send, zf_halo, a_send, a_halo, mask_halo, part_halo, halo_vx, t_yz, near_sum,
    y_faces, y_sums, z_near, z_near_w, z_own_w, z_sums, rows2, rows2_x, rows2_y, rows2_d, zg_send, zg_halo,
    load_sem, k_send, k_recv, p_send, p_recv, r_send, r_recv, h_send, h_recv, out_sem,
):
    at = {axis: lax.axis_index(axis) for axis in AXES}
    has = {}
    for axis in AXES:
        has[axis, 1] = at[axis] < COUNT[axis] - 1
        has[axis, -1] = at[axis] > 0
    par_x, par_y = lax.rem(at["gx"], 2), lax.rem(at["gy"], 2)
    lane = lax.broadcasted_iota(jnp.int32, (E, LANES), 1)
    row = lax.broadcasted_iota(jnp.int32, (E, LANES), 0)
    even = lax.rem(lane // E, 2) == 0

    loads = [
        pltpu.make_async_copy(perm.at[0], kx.at[pl.ds(1, E)], load_sem.at[0]),
        pltpu.make_async_copy(perm.at[1], ky.at[:, pl.ds(ROW0, E)], load_sem.at[1]),
        pltpu.make_async_copy(perm.at[2], kz, load_sem.at[2]),
        pltpu.make_async_copy(flags, fl, load_sem.at[3]),
        pltpu.make_async_copy(mask, mk, load_sem.at[4]),
    ]
    for load in loads:
        load.start()

    barrier = pltpu.get_barrier_semaphore()
    expected = 0
    for axis in AXES:
        for d in (1, -1):
            @pl.when(has[axis, d])
            def _():
                pl.semaphore_signal(
                    barrier, inc=1, device_id={axis: at[axis] + d}, device_id_type=MESH
                )
            expected = expected + has[axis, d].astype(jnp.int32)

    def shift_to(axis, d):
        size = COUNT[axis]
        return lax.rem(at[axis] + d + size, size)

    class Copy:
        def __init__(self, src, dst, ssem, rsem, moves):
            self.send_if = None
            self.recv_if = None
            target = {}
            for axis, d in moves:
                target[axis] = shift_to(axis, d)
                s, r = has[axis, d], has[axis, -d]
                self.send_if = s if self.send_if is None else self.send_if & s
                self.recv_if = r if self.recv_if is None else self.recv_if & r
            self.copy = pltpu.make_async_remote_copy(
                src_ref=src, dst_ref=dst, send_sem=ssem, recv_sem=rsem,
                device_id=target, device_id_type=MESH,
            )

        def start(self):
            pl.when(self.send_if)(self.copy.start)

        def wait_recv(self):
            pl.when(self.recv_if)(self.copy.wait_recv)

        def wait_send(self):
            pl.when(self.send_if)(self.copy.wait_send)

    started = []

    def start(copies):
        for c in copies:
            c.start()
        started.extend(copies)

    zero = jnp.zeros((E, LANES), jnp.float32)
    for d, k_plane in ((-1, 0), (1, 9)):
        side = (d + 1) // 2

        @pl.when(jnp.logical_not(has["gx", d]))
        def _():
            kx[k_plane] = zero
            a_halo[side] = jnp.ones((3, E, LANES), jnp.float32)
            mask_halo[side] = jnp.zeros((8, E, LANES), jnp.int32)
            for n in range(2):
                part_halo[n, side] = jnp.zeros((8, E, LANES), jnp.float32)
            for k in range(1, SWEEPS + 1):
                basis[k, :, k_plane, 8:16] = jnp.zeros((8, E, LANES), jnp.float32)
            rows_x[side] = jnp.zeros((2, E, LANES), jnp.float32)
            rows2_x[side] = jnp.zeros((2, E, LANES), jnp.float32)

        @pl.when(jnp.logical_not(has["gy", d]))
        def _():
            y_row = 7 if d < 0 else 16
            ky[:, y_row:y_row + 1] = jnp.zeros((E, 1, LANES), jnp.float32)

            def clear(i, carry):
                basis[i // 8, lax.rem(i, 8), 1:9, y_row:y_row + 1] = jnp.zeros(
                    (E, 1, LANES), jnp.float32
                )
                return carry

            lax.fori_loop(0, 8 * SWEEPS, clear, 0)
            rows_y[side] = jnp.zeros((2, E, LANES), jnp.float32)
            rows2_y[side] = jnp.zeros((2, E, LANES), jnp.float32)
            face_rows_y[side] = jnp.zeros((2, E, LANES), jnp.float32)

        @pl.when(jnp.logical_not(has["gz", d]))
        def _():
            kz_halo[side] = zero
            for k in range(1, SWEEPS + 1):
                z_halo[k, 0, side] = zero
                z_halo[k, 1, side] = zero

        for e in (1, -1):
            @pl.when(jnp.logical_not(has["gx", d] & has["gy", e]))
            def _():
                rows_d[side, (e + 1) // 2] = zero
                rows2_d[side, (e + 1) // 2] = zero

    for m_z in (1, -1):
        side = (1 - m_z) // 2
        for m_y in (1, 0, -1):
            near = has["gz", -m_z]
            if m_y:
                near = near & has["gy", -m_y]

            @pl.when(jnp.logical_not(near))
            def _():
                zf_halo[side, m_y + 1] = zero

            for m_x in (1, 0, -1):
                there = near & has["gx", -m_x] if m_x else near

                @pl.when(jnp.logical_not(there))
                def _():
                    zr_halo[side, m_x + 1, m_y + 1] = zero

        for m_x in (1, 0, -1):
            there = has["gz", -m_z]
            if m_x:
                there = there & has["gx", -m_x]

            @pl.when(jnp.logical_not(there))
            def _():
                zg_halo[side, m_x + 1] = zero

    def close(i, carry):
        basis[SWEEPS, i, 1:9, 7:8] = jnp.zeros((E, 1, LANES), jnp.float32)
        basis[SWEEPS, i, 1:9, 16:17] = jnp.zeros((E, 1, LANES), jnp.float32)
        return carry

    lax.fori_loop(0, 8, close, 0)

    for load in loads[:3]:
        load.wait()
    for side in range(2):
        tile = zero
        for x in range(E):
            shift = (x - 127) % LANES if side == 0 else x
            moved = pltpu.roll(kz[x], shift, 1) if shift else kz[x]
            tile = jnp.where(lane == x, moved, tile)
        kz_send[side] = tile
    pl.semaphore_wait(barrier, expected)
    k_x = [
        Copy(kx.at[8], kx.at[0], k_send.at[0], k_recv.at[0], (("gx", 1),)),
        Copy(kx.at[1], kx.at[9], k_send.at[1], k_recv.at[1], (("gx", -1),)),
    ]
    k_yz = [
        Copy(ky.at[:, pl.ds(15, 1)], ky.at[:, pl.ds(7, 1)], k_send.at[2], k_recv.at[2], (("gy", 1),)),
        Copy(ky.at[:, pl.ds(8, 1)], ky.at[:, pl.ds(16, 1)], k_send.at[3], k_recv.at[3], (("gy", -1),)),
        Copy(kz_send.at[0], kz_halo.at[0], k_send.at[4], k_recv.at[4], (("gz", 1),)),
        Copy(kz_send.at[1], kz_halo.at[1], k_send.at[5], k_recv.at[5], (("gz", -1),)),
    ]
    start(k_x)
    start(k_yz)
    for load in loads[3:]:
        load.wait()
    h_copies = []
    for src, dst in (
        (lambda side: mk.at[:, 7 * side], mask_halo),
        (lambda side: a_send.at[side], a_halo),
        (lambda side: part.at[2, side], part_halo.at[0]),
        (lambda side: part.at[3, side], part_halo.at[1]),
    ):
        for side, d in ((0, -1), (1, 1)):
            n = len(h_copies)
            h_copies.append(Copy(src(side), dst.at[1 - side], h_send.at[n], h_recv.at[n], (("gx", d),)))
    start(h_copies[:2])

    def faces_yz(x):
        here = ky[x, 8:16]
        t_y = (harmonic(ky[x, 7:15], here), harmonic(here, ky[x, 9:17]))
        here = kz[x]
        before = jnp.where(
            lane == 0, pltpu.roll(kz_halo[0], LANES - x, 1), pltpu.roll(here, 1, 1)
        )
        after = jnp.where(
            lane == 127, pltpu.roll(kz_halo[1], 127 - x, 1), pltpu.roll(here, 127, 1)
        )
        return t_y, (harmonic(before, here), harmonic(here, after))

    def prepare(x, inner_x):
        t_y, t_z = faces_yz(x)
        for n in range(2):
            t_yz[x, n] = t_y[n]
            t_yz[x, 2 + n] = t_z[n]
        total = t_y[0] + t_y[1] + t_z[0] + t_z[1]
        for n in inner_x:
            total = total + harmonic(kx[x + n], kx[x + n + 1])
        total = total + WELL * fl[x].astype(jnp.float32)
        near_sum[x] = total
        place = lax.rem(lane, E)
        cross_y = jnp.where(row == 0, t_y[0], jnp.where(row == 7, t_y[1], 0.0))
        cross_z = jnp.where(place == 0, t_z[0], jnp.where(place == 7, t_z[1], 0.0))
        return total, cross_y, cross_z

    def first_values(masks, plane, own_x, scale, t_x, t_y, t_z):
        def support(b_x, b_y, own):
            n = 4 * b_x + 2 * b_y
            pair = (masks(n), masks(n + 1)) if own else (masks(n + 1), masks(n))
            return jnp.where(even, *pair).astype(jnp.float32)

        u_y = support(own_x, 1 - par_y, True) * (t_y * scale)
        u_z = support(own_x, par_y, False) * (t_z * scale)
        u_x = zero if t_x is None else support(1 - own_x, par_y, True) * (t_x * scale)

        def put(b_x, b_y, own_z, beside_z):
            n = 4 * b_x + 2 * b_y
            basis[1, n, plane, 8:16] = jnp.where(even, own_z, beside_z)
            basis[1, n + 1, plane, 8:16] = jnp.where(even, beside_z, own_z)

        put(own_x, par_y, 1.0 - (u_x + u_y + u_z), u_z)
        put(1 - own_x, par_y, u_x, zero)
        put(own_x, 1 - par_y, u_y, zero)
        put(1 - own_x, 1 - par_y, zero, zero)

    def first_halo(side):
        t_x = harmonic(kx[8 * side], kx[8 * side + 1])
        scale = STEP / (a_halo[side, 0] + t_x)
        halo_vx[side] = t_x * scale
        first_values(
            lambda n: mask_halo[side, n], 9 * side, 1 - par_x, scale, t_x, a_halo[side, 1], a_halo[side, 2]
        )

    def next_halo(k, side):
        plane = 9 * side
        flow = part_halo[k - 2, side] + halo_vx[side] * basis[k, :, 1 + 7 * side, 8:16]
        center = basis[k, :, plane, 8:16]
        change = mask_halo[side].astype(jnp.float32) * flow
        basis[k + 1, :, plane, 8:16] = center + change - center * jnp.sum(change, axis=0)

    def weights(x):
        here = kx[x + 1]
        t_x = (harmonic(kx[x], here), harmonic(here, kx[x + 2]))
        t_y, t_z = (t_yz[x, 0], t_yz[x, 1]), (t_yz[x, 2], t_yz[x, 3])
        diagonal = near_sum[x]
        negdiag[x] = -1.5 * diagonal
        scale = STEP / diagonal
        for b in range(2):
            keep_x = (par_x == b).astype(jnp.float32)
            keep_y = (par_y == b).astype(jnp.float32)
            own_z = even if b == 0 else jnp.logical_not(even)
            for side in range(2):
                inner = 4 - side
                vx[b, side, x] = t_x[side] * scale * jnp.where(x == inner, keep_x, 1.0)
                vy[b, side, x] = t_y[side] * scale * jnp.where(row == inner, keep_y, 1.0)
                cut = (lax.rem(lane, E) == inner) & jnp.logical_not(own_z)
                vz[b, side, x] = jnp.where(cut, 0.0, t_z[side] * scale)

    def center_of(k, x):
        return basis[k, :, x + 1, 8:16].reshape(2, 2, 2, E, LANES)

    def flow_x(k, x, side):
        near = basis[k, :, x + 2 * side, 8:16].reshape(2, 2, 2, E, LANES)
        return vx[:, side, x][:, None, None] * near

    def z_ends(k, x, group):
        halo = jnp.where(lax.rem(lane, 2) == 0, z_halo[k, group, 0], z_halo[k, group, 1])
        first = pltpu.roll(halo, lax.rem(LANES - 2 * x, LANES), 1)
        return [first] + [pltpu.roll(halo, LANES - 2 * (n * 8 + x), 1) for n in range(1, 8)]

    def flow_yz(k, x, group, closed=False):
        center = basis[k, :, x + 1, 8:16]
        total = -STEP * center.reshape(2, 2, 2, E, LANES)
        ends = [zero] * 8 if closed else z_ends(k, x, group)
        for side in range(2):
            near = basis[k, :, x + 1, 7 + 2 * side:15 + 2 * side].reshape(2, 2, 2, E, LANES)
            total = total + vy[:, side, x][None, :, None] * near
            edge = lane == (0, 127)[side]
            moved = [
                jnp.where(edge, ends[n], pltpu.roll(center[n], (1, 127)[side], 1)) for n in range(8)
            ]
            near = jnp.stack(moved).reshape(2, 2, 2, E, LANES)
            total = total + vz[:, side, x][None, None] * near
        return total

    def update(k, x, flow):
        center = center_of(k, x)
        support = mk[:, x].astype(jnp.float32).reshape(2, 2, 2, E, LANES)
        change = support * flow
        change_sum = jnp.sum(change, axis=(0, 1, 2))
        fresh = center + change - center * change_sum
        basis[k + 1, :, x + 1, 8:16] = fresh.reshape(8, E, LANES)

    def pack_z(k, x, tiles):
        up, down = tiles
        for s in range(8):
            place = 2 * (s * 8 + x)
            before = lax.rem(place + 127, LANES)
            value = basis[k, s, x + 1, 8:16]
            up = jnp.where(lane == place, pltpu.roll(value, place + 1, 1), up)
            down = jnp.where(lane == before, pltpu.roll(value, before, 1), down)
        return up, down

    def copies(k):
        ref = basis.at[k]
        y_target = basis.at[k % SWEEPS]
        own = pl.ds(8, E)
        sems = [(p_send.at[k, i], p_recv.at[k, i]) for i in range(12)]
        x = [
            Copy(ref.at[:, 8, own], ref.at[:, 0, own], *sems[0], (("gx", 1),)),
            Copy(ref.at[:, 1, own], ref.at[:, 9, own], *sems[1], (("gx", -1),)),
        ] if k == 2 else []
        yz = []
        for group in range(2):
            part_yz = []
            for n, planes in enumerate((pl.ds(2, 6),) if group == 0 else (pl.ds(1, 1), pl.ds(8, 1))):
                at_sem = 2 + 2 * group + 2 * n
                for side, (a, b, d) in enumerate(((15, 7, 1), (8, 16, -1))):
                    part_yz.append(Copy(
                        ref.at[:, planes, pl.ds(a, 1)], y_target.at[:, planes, pl.ds(b, 1)],
                        *sems[at_sem + side], (("gy", d),),
                    ))
            for side, d in ((0, 1), (1, -1)):
                part_yz.append(Copy(
                    z_send.at[k, group, side], z_halo.at[k, group, side],
                    *sems[8 + 2 * group + side], (("gz", d),),
                ))
            yz.append(part_yz)
        return x, yz[0], yz[1]

    def inner_flow(k, x, group=0):
        return flow_yz(k, x, group) + flow_x(k, x, 0) + flow_x(k, x, 1)

    def pack_outer(k):
        tiles = (zero, zero)
        for x in (0, 7):
            tiles = pack_z(k, x, tiles)
        z_send[k, 1, 0], z_send[k, 1, 1] = tiles

    arriving_x, arriving_inner, arriving_outer = copies(1)
    for c in k_yz:
        c.wait_recv()
    for side in range(2):
        for n, tile in enumerate(prepare(7 * side, (1 - side,))):
            a_send[side, n] = tile
    start(h_copies[2:4])

    def first_inner(x, tiles):
        total, t_y, t_z = prepare(x, (0, 1))
        first_values(lambda n: mk[n, x], x + 1, par_x, STEP / total, None, t_y, t_z)
        return pack_z(1, x, tiles)

    tiles = lax.fori_loop(1, 7, first_inner, (zero, zero), unroll=True)
    z_send[1, 0, 0], z_send[1, 0, 1] = tiles
    start(arriving_inner)
    for c in k_x:
        c.wait_recv()
    for side in range(2):
        x = 7 * side
        t_x = harmonic(kx[8 * side], kx[8 * side + 1])
        near_sum[x] = a_send[side, 0] + t_x
        first_values(
            lambda n: mk[n, x], x + 1, par_x, STEP / near_sum[x], t_x, a_send[side, 1], a_send[side, 2]
        )
    pack_outer(1)
    start(arriving_outer)

    def weigh(x, carry):
        weights(x)
        return carry

    lax.fori_loop(0, E, weigh, 0, unroll=True)
    for k in range(1, SWEEPS):
        next_x, next_inner, next_outer = copies(k + 1)
        for c in arriving_inner:
            c.wait_recv()

        def inner(x, tiles):
            update(k, x, inner_flow(k, x))
            return pack_z(k + 1, x, tiles)

        tiles = lax.fori_loop(1, 7, inner, (zero, zero), unroll=True)
        z_send[k + 1, 0, 0], z_send[k + 1, 0, 1] = tiles
        start(next_inner)
        for c in arriving_outer:
            c.wait_recv()
        for x, side in ((0, 1), (7, 0)):
            part[k, 1 - side] = (flow_yz(k, x, 1) + flow_x(k, x, side)).reshape(8, E, LANES)
        if k >= 2:
            start(h_copies[2 * k:2 * k + 2])
        for c in (h_copies[:4], arriving_x, h_copies[4:6])[k - 1]:
            c.wait_recv()
        for side in range(2):
            if k == 1:
                first_halo(side)
            if k == 3:
                next_halo(2, side)
        for x, side in ((0, 0), (7, 1)):
            update(k, x, part[k, side].reshape(2, 2, 2, E, LANES) + flow_x(k, x, side))
        if k == 1:
            start(next_x)
        pack_outer(k + 1)
        start(next_outer)
        arriving_x, arriving_inner, arriving_outer = next_x, next_inner, next_outer

    out = pltpu.make_async_copy(
        basis.at[SWEEPS, :, pl.ds(1, E), pl.ds(8, E)], out_p, out_sem.at[0]
    )
    out.start()

    def split_z(values):
        pair = values.reshape(4, 2, E, LANES)
        return (
            jnp.where(even, pair[:, 0], pair[:, 1]),
            jnp.where(even, pair[:, 1], pair[:, 0]),
        )

    def split_basis(x, carry):
        own, beside = split_z(center_of(SWEEPS, x))
        pz[:, 0, x] = own
        pz[:, 1, x] = beside
        return carry

    lax.fori_loop(0, E, split_basis, 0, unroll=True)
    def image(x, flow):
        own, beside = split_z(flow * negdiag[x])
        iz[:, 0, x] = own
        iz[:, 1, x] = beside

    def closed_image(x, carry):
        image(x, flow_yz(SWEEPS, x, 0, True) + flow_x(SWEEPS, x, 0) + flow_x(SWEEPS, x, 1))
        return carry

    lax.fori_loop(1, 7, closed_image, 0, unroll=True)
    for x, side in ((0, 1), (7, 0)):
        image(x, flow_yz(SWEEPS, x, 0, True) + flow_x(SWEEPS, x, side))

    def pair_of(a_x, a_y):
        return lax.rem(a_x + par_x, 2) * 2 + lax.rem(a_y + par_y, 2)

    def contract(i, carry):
        half, a_x, a_y = i // 4, lax.rem(i // 2, 2), lax.rem(i, 2)
        for a_z in range(2):
            for e in range(8):
                u_xy = pair_of(a_x + e // 4, a_y + e // 2 % 2)
                total = None
                for j in range(4):
                    x = 4 * half + j
                    term = pz[pair_of(a_x, a_y), a_z, x] * iz[u_xy, (a_z + e) % 2, x]
                    total = term if total is None else total + term
                sums[pl.ds(pl.multiple_of((i * 2 + a_z) * 64, 64) + e * 8, E)] = total
        return carry

    lax.fori_loop(0, 8, contract, 0, unroll=2)

    def y_halves(ref, count):
        results = []
        for y_half in range(2):
            total = ref[pl.ds(4 * y_half, count * 8, stride=8)]
            for y in range(1, 4):
                total = total + ref[pl.ds(4 * y_half + y, count * 8, stride=8)]
            results.append(total.reshape(count, E, LANES))
        return results

    def halves(ref, count):
        results = []
        for total in y_halves(ref, count):
            total = total + pltpu.roll(total, 127, 2)
            total = total + pltpu.roll(total, 126, 2)
            results.append(total.reshape(count // 2, 2, E, LANES))
        return results

    low = (lax.rem(lane, E) == 0) & (lane != 0)
    high = (lax.rem(lane, E) == 4) & (lane != 124)

    def merge_z(pair):
        own, beside = pair[:, 0], pair[:, 1]
        own = own + jnp.where(low, pltpu.roll(beside, 4, 2), 0.0)
        return own + jnp.where(high, pltpu.roll(beside, 124, 2), 0.0)

    def pack_rows(entries):
        up, down = zero, zero
        for place, beside in entries:
            up = jnp.where(lane == place, pltpu.roll(beside, place + 4, 1), up)
            moved = pltpu.roll(beside, place, 1) if place else beside
            down = jnp.where(lane == place, moved, down)
        return up, down

    row_copies = []

    def move_rows(src, dst, moves):
        n = len(row_copies)
        row_copies.append(Copy(src, dst, r_send.at[n], r_recv.at[n], tuple(m for m in moves if m[1])))

    quarter = halves(sums, 16)
    entries = []
    for i in range(8):
        half, a_x, a_y = i // 4, i // 2 % 2, i % 2
        for y_half in range(2):
            place = (a_x * 2 + a_y) * 32 + (half ^ a_x) * 2 + (y_half ^ a_y)
            entries.append((place, quarter[y_half][i, 1]))
    zr_send[0], zr_send[1] = pack_rows(entries)
    order = [(m_x, m_y) for m_x in (1, -1, 0) for m_y in (1, -1, 0)]
    for side, m_z in ((0, 1), (1, -1)):
        for m_x, m_y in order:
            move_rows(
                zr_send.at[side], zr_halo.at[side, m_x + 1, m_y + 1],
                (("gx", m_x), ("gy", m_y), ("gz", m_z)),
            )
    start(row_copies)
    for y_half in range(2):
        merged = merge_z(quarter[y_half])
        for i in range(8):
            rows[i // 2 % 2, i % 2, i // 4, y_half] = merged[i]
    first = len(row_copies)
    for side, d in ((0, 1), (1, -1)):
        for side_y, d_y in ((0, 1), (1, -1)):
            move_rows(
                rows.at[1, 1, 1 - side, 1 - side_y], rows_d.at[side, side_y], (("gx", d), ("gy", d_y))
            )
    for side, d in ((0, 1), (1, -1)):
        move_rows(rows.at[1, 0, 1 - side], rows_x.at[side], (("gx", d),))
        move_rows(rows.at[0, 1, :, 1 - side], rows_y.at[side], (("gy", d),))
    start(row_copies[first:])
    first = len(row_copies)

    flat = basis.reshape((SWEEPS + 1) * 8 * 240, LANES)
    flat_t = t_yz.reshape(E * 4 * E, LANES)
    def z_faces(planes):
        for x in planes:
            ends = jnp.stack(z_ends(SWEEPS, x, 1 if x in (0, 7) else 0))
            for n, tiles in enumerate(split_z(ends)):
                z_near[:, n, x] = tiles
                z_near_w[:, n, x] = tiles * z_weight(x)

    def z_weight(x):
        return -jnp.where(lane == 0, t_yz[x, 2], jnp.where(lane == 127, t_yz[x, 3], 0.0))

    def contract_z(first_planes, i, carry):
        half, a_x, a_y = i // 4, lax.rem(i // 2, 2), lax.rem(i, 2)
        s_xy = pair_of(a_x, a_y)
        planes = [1 + 3 * half + j for j in range(3)] if first_planes else [7 * half]
        for e in range(8):
            u_xy = pair_of(a_x + e // 4, a_y + e // 2 % 2)
            place = pl.ds(pl.multiple_of(i * 64, 64) + e * 8, E)
            total = None if first_planes else z_sums[place]
            for x in planes:
                term = pz[s_xy, 0, x] * z_near_w[u_xy, e % 2, x] + z_near[s_xy, 0, x] * z_own_w[u_xy, e % 2, x]
                total = term if total is None else total + term
            z_sums[place] = total
        return carry

    for x in range(E):
        for n in range(2):
            z_own_w[:, n, x] = pz[:, n, x] * z_weight(x)
    for c in arriving_inner:
        c.wait_recv()
    z_faces(range(1, 7))
    lax.fori_loop(0, 8, functools.partial(contract_z, True), 0, unroll=2)
    for c in arriving_outer:
        c.wait_recv()
    for side in range(2):
        weight = -flat_t[pl.ds(side * 15, E, stride=32)]
        for n, (k, y_row) in enumerate(((SWEEPS, 8 + 7 * side), (0, 7 + 9 * side))):
            tiles = jnp.stack([flat[pl.ds((k * 8 + m) * 240 + 24 + y_row, E, stride=24)] for m in range(8)])
            own, beside = split_z(tiles)
            y_faces[side, n, 0, :, 0] = own
            y_faces[side, n, 0, :, 1] = beside
            y_faces[side, n, 1, :, 0] = own * weight
            y_faces[side, n, 1, :, 1] = beside * weight

    def contract_y(i, carry):
        side, a_x = i // 2, lax.rem(i, 2)
        s_xy = pair_of(a_x, 0)
        for a_z in range(2):
            for e in range(8):
                u_xy = pair_of(a_x + e // 4, e // 2 % 2)
                u_z = (a_z + e) % 2
                total = y_faces[side, 0, 0, s_xy, a_z] * y_faces[side, 1, 1, u_xy, u_z]
                total = total + y_faces[side, 1, 0, s_xy, a_z] * y_faces[side, 0, 1, u_xy, u_z]
                y_sums[pl.ds(pl.multiple_of((i * 2 + a_z) * 64, 64) + e * 8, E)] = total
        return carry

    lax.fori_loop(0, 4, contract_y, 0, unroll=True)
    y_quarter = halves(y_sums, 8)
    entries = []
    for i in range(4):
        side, a_x = i // 2, i % 2
        for x_half in range(2):
            entries.append((a_x * 64 + (x_half ^ a_x) * 2 + side, y_quarter[x_half][i, 1]))
    zg_send[0], zg_send[1] = pack_rows(entries)
    for side, m_z in ((0, 1), (1, -1)):
        for m_x in (1, -1, 0):
            move_rows(zg_send.at[side], zg_halo.at[side, m_x + 1], (("gx", m_x), ("gz", m_z)))
    start(row_copies[first:])
    first = len(row_copies)

    z_faces((0, 7))
    lax.fori_loop(0, 8, functools.partial(contract_z, False), 0, unroll=2)
    z_quarter = y_halves(z_sums, 8)
    y_merged = [merge_z(part_of) for part_of in y_quarter]
    for y_half in range(2):
        tiles = jnp.where(lane == 0, z_quarter[y_half], 0.0)
        tiles = tiles + jnp.where(lane == 124, pltpu.roll(z_quarter[y_half], 125, 2), 0.0)
        for i in range(8):
            half, a_x, a_y = i // 4, i // 2 % 2, i % 2
            tile = tiles[i] if a_y else tiles[i] + y_merged[half][y_half * 2 + a_x]
            rows2[a_x, a_y, half, y_half] = tile
    for side, d in ((0, 1), (1, -1)):
        for side_y, d_y in ((0, 1), (1, -1)):
            move_rows(
                rows2.at[1, 1, 1 - side, 1 - side_y], rows2_d.at[side, side_y], (("gx", d), ("gy", d_y))
            )
    for side, d in ((0, 1), (1, -1)):
        move_rows(rows2.at[1, 0, 1 - side], rows2_x.at[side], (("gx", d),))
        move_rows(rows2.at[0, 1, :, 1 - side], rows2_y.at[side], (("gy", d),))
    start(row_copies[first:])
    first = len(row_copies)

    for c in h_copies[6:]:
        c.wait_recv()
    for side in range(2):
        next_halo(3, side)
        x = 7 * side
        weight = vx[0, side, x] * negdiag[x]
        for n, plane in enumerate((x + 1, 9 * side)):
            own, beside = split_z(basis[SWEEPS, :, plane, 8:16])
            faces[side, n, 0, :, 0] = own
            faces[side, n, 0, :, 1] = beside
            faces[side, n, 1, :, 0] = own * weight
            faces[side, n, 1, :, 1] = beside * weight

    def contract_faces(i, carry):
        side, a_y = i // 2, lax.rem(i, 2)
        s_xy = pair_of(0, a_y)
        for a_z in range(2):
            for e in range(8):
                u_xy = pair_of(e // 4, a_y + e // 2 % 2)
                u_z = (a_z + e) % 2
                total = faces[side, 0, 0, s_xy, a_z] * faces[side, 1, 1, u_xy, u_z]
                total = total + faces[side, 1, 0, s_xy, a_z] * faces[side, 0, 1, u_xy, u_z]
                face_sums[pl.ds(pl.multiple_of((i * 2 + a_z) * 64, 64) + e * 8, E)] = total
        return carry

    lax.fori_loop(0, 4, contract_faces, 0, unroll=True)
    quarter = halves(face_sums, 8)
    entries = []
    for i in range(4):
        half, a_y = i // 2, i % 2
        for y_half in range(2):
            entries.append((a_y * 32 + half * 2 + (y_half ^ a_y), quarter[y_half][i, 1]))
    zf_send[0], zf_send[1] = pack_rows(entries)
    for side, m_z in ((0, 1), (1, -1)):
        for m_y in (1, -1, 0):
            move_rows(zf_send.at[side], zf_halo.at[side, m_y + 1], (("gy", m_y), ("gz", m_z)))
    start(row_copies[first:])
    first = len(row_copies)
    face_own = []
    for y_half in range(2):
        merged = merge_z(quarter[y_half])
        face_own.append((merged[0], merged[2]))
        face_rows[y_half, 0], face_rows[y_half, 1] = merged[1], merged[3]
    for side, d in ((0, 1), (1, -1)):
        move_rows(face_rows.at[1 - side], face_rows_y.at[side], (("gy", d),))
    start(row_copies[first:])

    for c in row_copies:
        c.wait_recv()
    whole = [
        [
            rows[0, 0, h, y] + rows_x[h, y] + rows_y[y, h] + rows_d[h, y] + face_own[y][h] + face_rows_y[y, h]
            + (rows2[0, 0, h, y] + rows2_x[h, y] + rows2_y[y, h] + rows2_d[h, y])
            for y in range(2)
        ]
        for h in range(2)
    ]
    for side in range(2):
        packed = zero
        for m_x, m_y in order:
            inside = lane - 32 * (2 * abs(m_x) + abs(m_y))
            takes = (inside >= 0) & (inside < 4)
            if m_x:
                takes = takes & (inside // 2 == (1 - m_x) // 2)
            if m_y:
                takes = takes & (lax.rem(inside, 2) == (1 - m_y) // 2)
            value = zr_halo[side, m_x + 1, m_y + 1]
            if m_x == 0:
                value = value + zf_halo[side, m_y + 1]
            if m_y == 0:
                value = value + zg_halo[side, m_x + 1]
            packed = packed + jnp.where(takes, value, 0.0)
        target = 124 * side
        for h in range(2):
            for y in range(2):
                total = None
                for group in range(4):
                    shift = (target - group * 32 - (h * 2 + y)) % LANES
                    moved = pltpu.roll(packed, shift, 1) if shift else packed
                    total = moved if total is None else total + moved
                whole[h][y] = whole[h][y] + jnp.where(lane == target, total, 0.0)
    tiles = jnp.stack([whole[0][0], whole[0][1], whole[1][0], whole[1][1]])

    def gather(offset):
        values = tiles
        for step, (spread, size) in enumerate(((7, 1), (28, 4))):
            result = None
            for n in range(4):
                shift = (LANES - spread * n - (0 if step else offset)) % LANES
                moved = pltpu.roll(values, shift, 2) if shift else values
                here = lax.rem(lane, 32) == n if step == 0 else lane // 4 == n
                result = moved if result is None else jnp.where(here, moved, result)
            values = result
        return values

    lows, highs = gather(0), gather(4)
    picks = {0: ((0,), 1), 1: ((0, 1), 0), 2: ((1,), 1)}
    for d_x in range(3):
        for d_y in range(3):
            (halves_x, e_x), (halves_y, e_y) = picks[d_x], picks[d_y]
            low_tile, high_tile = None, None
            for h in halves_x:
                for y in halves_y:
                    n = h * 2 + y
                    low_tile = lows[n] if low_tile is None else low_tile + lows[n]
                    high_tile = highs[n] if high_tile is None else high_tile + highs[n]
            e = e_x * 4 + e_y * 2
            out_row = (d_x * 3 + d_y) * 3
            out_c[out_row:out_row + 1, :] = low_tile[e + 1:e + 2, :16]
            out_c[out_row + 1:out_row + 2, :] = low_tile[e:e + 1, :16] + high_tile[e:e + 1, :16]
            out_c[out_row + 2:out_row + 3, :] = high_tile[e + 1:e + 2, :16]
    out.wait()
    for c in started:
        c.wait_send()


def shards(permeability, well_flags, support_mask):
    f32 = jnp.float32
    vmem = pltpu.VMEM
    dma = pltpu.SemaphoreType.DMA
    any_spec = pl.BlockSpec(memory_space=pltpu.HBM)
    prolongation, coarse = pl.pallas_call(
        kernel,
        out_shape=(
            pltpu.VMEM((8, E, E, LANES), f32),
            pltpu.VMEM((27, 16), f32),
        ),
        in_specs=[any_spec] * 3,
        out_specs=(pl.BlockSpec(memory_space=pltpu.VMEM), pl.BlockSpec(memory_space=pltpu.VMEM)),
        scratch_shapes=[
            vmem((10, E, LANES), f32),
            vmem((E, 24, LANES), f32),
            vmem((E, E, LANES), f32),
            vmem((2, E, LANES), f32),
            vmem((2, E, LANES), f32),
            vmem((E, E, LANES), jnp.int32),
            vmem((8, E, E, LANES), jnp.int32),
            vmem((SWEEPS + 1, 8, 10, 24, LANES), f32),
            vmem((SWEEPS + 1, 2, 2, E, LANES), f32),
            vmem((SWEEPS + 1, 2, 2, E, LANES), f32),
            vmem((2, 2, E, E, LANES), f32),
            vmem((2, 2, E, E, LANES), f32),
            vmem((2, 2, E, E, LANES), f32),
            vmem((E, E, LANES), f32),
            vmem((SWEEPS, 2, 8, E, LANES), f32),
            vmem((4, 2, E, E, LANES), f32),
            vmem((4, 2, E, E, LANES), f32),
            vmem((1024, LANES), f32),
            vmem((2, 2, 2, 2, E, LANES), f32),
            vmem((2, 2, E, LANES), f32),
            vmem((2, 2, E, LANES), f32),
            vmem((2, 2, E, LANES), f32),
            vmem((2, E, LANES), f32),
            vmem((2, 3, 3, E, LANES), f32),
            vmem((2, 2, 2, 4, 2, E, LANES), f32),
            vmem((512, LANES), f32),
            vmem((2, 2, E, LANES), f32),
            vmem((2, 2, E, LANES), f32),
            vmem((2, E, LANES), f32),
            vmem((2, 3, E, LANES), f32),
            vmem((2, 3, E, LANES), f32),
            vmem((2, 3, E, LANES), f32),
            vmem((2, 8, E, LANES), jnp.int32),
            vmem((2, 2, 8, E, LANES), f32),
            vmem((2, E, LANES), f32),
            vmem((E, 4, E, LANES), f32),
            vmem((E, E, LANES), f32),
            vmem((2, 2, 2, 4, 2, E, LANES), f32),
            vmem((512, LANES), f32),
            vmem((4, 2, E, E, LANES), f32),
            vmem((4, 2, E, E, LANES), f32),
            vmem((4, 2, E, E, LANES), f32),
            vmem((512, LANES), f32),
            vmem((2, 2, 2, 2, E, LANES), f32),
            vmem((2, 2, E, LANES), f32),
            vmem((2, 2, E, LANES), f32),
            vmem((2, 2, E, LANES), f32),
            vmem((2, E, LANES), f32),
            vmem((2, 3, E, LANES), f32),
            dma((5,)),
            dma((6,)),
            dma((6,)),
            dma((SWEEPS + 1, 12)),
            dma((SWEEPS + 1, 12)),
            dma((48,)),
            dma((48,)),
            dma((8,)),
            dma((8,)),
            dma((1,)),
        ],
        compiler_params=pltpu.CompilerParams(
            collective_id=0, has_side_effects=True, vmem_limit_bytes=60 * 1024 * 1024
        ),
        name="smooth_and_contract",
    )(permeability, well_flags, support_mask)
    return prolongation, coarse.reshape(3, 3, 3, 1, 1, 16)


def solution(mesh):
    placed = (P(None, "gx", "gy", "gz"), P("gx", "gy", "gz"), P(None, "gx", "gy", "gz"))
    return jax.shard_map(
        shards,
        mesh=mesh,
        in_specs=placed,
        out_specs=(P(None, "gx", "gy", "gz"), P(None, None, None, "gx", "gy", "gz")),
        check_vma=False,
    )
```

```python
import functools

import jax
import jax.numpy as jnp
from jax import lax
from jax.experimental import pallas as pl
from jax.experimental.pallas import tpu as pltpu
from jax.sharding import PartitionSpec as P

MESH = pl.DeviceIdType.MESH
AXES = ("gx", "gy", "gz")
COUNT = {"gx": 16, "gy": 4, "gz": 4}
SWEEPS = 4
STEP = 2.0 / 3.0
WELL = 0.05
E = 8
LANES = 128
ROW0 = 8


def harmonic(lower, upper):
    return 2.0 * lower * upper / (lower + upper)


def kernel(
    perm, flags, mask, out_p, out_c,
    kx, ky, kz, kz_send, kz_halo, fl, mk, basis, z_send, z_halo,
    vx, vy, vz, negdiag, part, pz, iz, sums, rows, rows_x, rows_y, rows_d, zr_send, zr_halo,
    faces, face_sums, face_rows, face_rows_y, zf_send, zf_halo, a_send, a_halo, mask_halo, part_halo, halo_vx, t_yz, near_sum,
    y_faces, y_sums, z_near, z_near_w, z_own_w, z_sums, rows2, rows2_x, rows2_y, rows2_d, zg_send, zg_halo,
    load_sem, k_send, k_recv, p_send, p_recv, r_send, r_recv, h_send, h_recv, out_sem,
):
    at = {axis: lax.axis_index(axis) for axis in AXES}
    has = {}
    for axis in AXES:
        has[axis, 1] = at[axis] < COUNT[axis] - 1
        has[axis, -1] = at[axis] > 0
    par_x, par_y = lax.rem(at["gx"], 2), lax.rem(at["gy"], 2)
    lane = lax.broadcasted_iota(jnp.int32, (E, LANES), 1)
    row = lax.broadcasted_iota(jnp.int32, (E, LANES), 0)
    even = lax.rem(lane // E, 2) == 0

    loads = [
        pltpu.make_async_copy(perm.at[0], kx.at[pl.ds(1, E)], load_sem.at[0]),
        pltpu.make_async_copy(perm.at[1], ky.at[:, pl.ds(ROW0, E)], load_sem.at[1]),
        pltpu.make_async_copy(perm.at[2], kz, load_sem.at[2]),
        pltpu.make_async_copy(flags, fl, load_sem.at[3]),
        pltpu.make_async_copy(mask, mk, load_sem.at[4]),
    ]
    for load in loads:
        load.start()

    barrier = pltpu.get_barrier_semaphore()
    expected = 0
    for axis in AXES:
        for d in (1, -1):
            @pl.when(has[axis, d])
            def _():
                pl.semaphore_signal(
                    barrier, inc=1, device_id={axis: at[axis] + d}, device_id_type=MESH
                )
            expected = expected + has[axis, d].astype(jnp.int32)

    def shift_to(axis, d):
        size = COUNT[axis]
        return lax.rem(at[axis] + d + size, size)

    class Copy:
        def __init__(self, src, dst, ssem, rsem, moves):
            self.send_if = None
            self.recv_if = None
            target = {}
            for axis, d in moves:
                target[axis] = shift_to(axis, d)
                s, r = has[axis, d], has[axis, -d]
                self.send_if = s if self.send_if is None else self.send_if & s
                self.recv_if = r if self.recv_if is None else self.recv_if & r
            self.copy = pltpu.make_async_remote_copy(
                src_ref=src, dst_ref=dst, send_sem=ssem, recv_sem=rsem,
                device_id=target, device_id_type=MESH,
            )

        def start(self):
            pl.when(self.send_if)(self.copy.start)

        def wait_recv(self):
            pl.when(self.recv_if)(self.copy.wait_recv)

        def wait_send(self):
            pl.when(self.send_if)(self.copy.wait_send)

    started = []

    def start(copies):
        for c in copies:
            c.start()
        started.extend(copies)

    zero = jnp.zeros((E, LANES), jnp.float32)
    for d, k_plane in ((-1, 0), (1, 9)):
        side = (d + 1) // 2

        @pl.when(jnp.logical_not(has["gx", d]))
        def _():
            kx[k_plane] = zero
            a_halo[side] = jnp.ones((3, E, LANES), jnp.float32)
            mask_halo[side] = jnp.zeros((8, E, LANES), jnp.int32)
            for n in range(2):
                part_halo[n, side] = jnp.zeros((8, E, LANES), jnp.float32)
            for k in range(1, SWEEPS + 1):
                basis[k, :, k_plane, 8:16] = jnp.zeros((8, E, LANES), jnp.float32)
            rows_x[side] = jnp.zeros((2, E, LANES), jnp.float32)
            rows2_x[side] = jnp.zeros((2, E, LANES), jnp.float32)

        @pl.when(jnp.logical_not(has["gy", d]))
        def _():
            y_row = 7 if d < 0 else 16
            ky[:, y_row:y_row + 1] = jnp.zeros((E, 1, LANES), jnp.float32)

            def clear(i, carry):
                basis[i // 8, lax.rem(i, 8), 1:9, y_row:y_row + 1] = jnp.zeros(
                    (E, 1, LANES), jnp.float32
                )
                return carry

            lax.fori_loop(0, 8 * SWEEPS, clear, 0)
            rows_y[side] = jnp.zeros((2, E, LANES), jnp.float32)
            rows2_y[side] = jnp.zeros((2, E, LANES), jnp.float32)
            face_rows_y[side] = jnp.zeros((2, E, LANES), jnp.float32)

        @pl.when(jnp.logical_not(has["gz", d]))
        def _():
            kz_halo[side] = zero
            for k in range(1, SWEEPS + 1):
                z_halo[k, 0, side] = zero
                z_halo[k, 1, side] = zero

        for e in (1, -1):
            @pl.when(jnp.logical_not(has["gx", d] & has["gy", e]))
            def _():
                rows_d[side, (e + 1) // 2] = zero
                rows2_d[side, (e + 1) // 2] = zero

    for m_z in (1, -1):
        side = (1 - m_z) // 2
        for m_y in (1, 0, -1):
            near = has["gz", -m_z]
            if m_y:
                near = near & has["gy", -m_y]

            @pl.when(jnp.logical_not(near))
            def _():
                zf_halo[side, m_y + 1] = zero

            for m_x in (1, 0, -1):
                there = near & has["gx", -m_x] if m_x else near

                @pl.when(jnp.logical_not(there))
                def _():
                    zr_halo[side, m_x + 1, m_y + 1] = zero

        for m_x in (1, 0, -1):
            there = has["gz", -m_z]
            if m_x:
                there = there & has["gx", -m_x]

            @pl.when(jnp.logical_not(there))
            def _():
                zg_halo[side, m_x + 1] = zero

    def close(i, carry):
        basis[SWEEPS, i, 1:9, 7:8] = jnp.zeros((E, 1, LANES), jnp.float32)
        basis[SWEEPS, i, 1:9, 16:17] = jnp.zeros((E, 1, LANES), jnp.float32)
        return carry

    lax.fori_loop(0, 8, close, 0)

    for load in loads[:3]:
        load.wait()
    for side in range(2):
        tile = zero
        for x in range(E):
            shift = (x - 127) % LANES if side == 0 else x
            moved = pltpu.roll(kz[x], shift, 1) if shift else kz[x]
            tile = jnp.where(lane == x, moved, tile)
        kz_send[side] = tile
    pl.semaphore_wait(barrier, expected)
    k_x = [
        Copy(kx.at[8], kx.at[0], k_send.at[0], k_recv.at[0], (("gx", 1),)),
        Copy(kx.at[1], kx.at[9], k_send.at[1], k_recv.at[1], (("gx", -1),)),
    ]
    k_yz = [
        Copy(ky.at[:, pl.ds(15, 1)], ky.at[:, pl.ds(7, 1)], k_send.at[2], k_recv.at[2], (("gy", 1),)),
        Copy(ky.at[:, pl.ds(8, 1)], ky.at[:, pl.ds(16, 1)], k_send.at[3], k_recv.at[3], (("gy", -1),)),
        Copy(kz_send.at[0], kz_halo.at[0], k_send.at[4], k_recv.at[4], (("gz", 1),)),
        Copy(kz_send.at[1], kz_halo.at[1], k_send.at[5], k_recv.at[5], (("gz", -1),)),
    ]
    start(k_x)
    start(k_yz)
    for load in loads[3:]:
        load.wait()
    h_copies = []
    for src, dst in (
        (lambda side: mk.at[:, 7 * side], mask_halo),
        (lambda side: a_send.at[side], a_halo),
        (lambda side: part.at[2, side], part_halo.at[0]),
        (lambda side: part.at[3, side], part_halo.at[1]),
    ):
        for side, d in ((0, -1), (1, 1)):
            n = len(h_copies)
            h_copies.append(Copy(src(side), dst.at[1 - side], h_send.at[n], h_recv.at[n], (("gx", d),)))
    start(h_copies[:2])

    def faces_yz(x):
        here = ky[x, 8:16]
        t_y = (harmonic(ky[x, 7:15], here), harmonic(here, ky[x, 9:17]))
        here = kz[x]
        before = jnp.where(
            lane == 0, pltpu.roll(kz_halo[0], LANES - x, 1), pltpu.roll(here, 1, 1)
        )
        after = jnp.where(
            lane == 127, pltpu.roll(kz_halo[1], 127 - x, 1), pltpu.roll(here, 127, 1)
        )
        return t_y, (harmonic(before, here), harmonic(here, after))

    def prepare(x, inner_x):
        t_y, t_z = faces_yz(x)
        for n in range(2):
            t_yz[x, n] = t_y[n]
            t_yz[x, 2 + n] = t_z[n]
        total = t_y[0] + t_y[1] + t_z[0] + t_z[1]
        for n in inner_x:
            total = total + harmonic(kx[x + n], kx[x + n + 1])
        total = total + WELL * fl[x].astype(jnp.float32)
        near_sum[x] = total
        place = lax.rem(lane, E)
        cross_y = jnp.where(row == 0, t_y[0], jnp.where(row == 7, t_y[1], 0.0))
        cross_z = jnp.where(place == 0, t_z[0], jnp.where(place == 7, t_z[1], 0.0))
        return total, cross_y, cross_z

    def first_values(masks, plane, own_x, scale, t_x, t_y, t_z):
        def support(b_x, b_y, own):
            n = 4 * b_x + 2 * b_y
            pair = (masks(n), masks(n + 1)) if own else (masks(n + 1), masks(n))
            return jnp.where(even, *pair).astype(jnp.float32)

        u_y = support(own_x, 1 - par_y, True) * (t_y * scale)
        u_z = support(own_x, par_y, False) * (t_z * scale)
        u_x = zero if t_x is None else support(1 - own_x, par_y, True) * (t_x * scale)

        def put(b_x, b_y, own_z, beside_z):
            n = 4 * b_x + 2 * b_y
            basis[1, n, plane, 8:16] = jnp.where(even, own_z, beside_z)
            basis[1, n + 1, plane, 8:16] = jnp.where(even, beside_z, own_z)

        put(own_x, par_y, 1.0 - (u_x + u_y + u_z), u_z)
        put(1 - own_x, par_y, u_x, zero)
        put(own_x, 1 - par_y, u_y, zero)
        put(1 - own_x, 1 - par_y, zero, zero)

    def first_halo(side):
        t_x = harmonic(kx[8 * side], kx[8 * side + 1])
        scale = STEP / (a_halo[side, 0] + t_x)
        halo_vx[side] = t_x * scale
        first_values(
            lambda n: mask_halo[side, n], 9 * side, 1 - par_x, scale, t_x, a_halo[side, 1], a_halo[side, 2]
        )

    def next_halo(k, side):
        plane = 9 * side
        flow = part_halo[k - 2, side] + halo_vx[side] * basis[k, :, 1 + 7 * side, 8:16]
        center = basis[k, :, plane, 8:16]
        change = mask_halo[side].astype(jnp.float32) * flow
        basis[k + 1, :, plane, 8:16] = center + change - center * jnp.sum(change, axis=0)

    def weights(x):
        here = kx[x + 1]
        t_x = (harmonic(kx[x], here), harmonic(here, kx[x + 2]))
        t_y, t_z = (t_yz[x, 0], t_yz[x, 1]), (t_yz[x, 2], t_yz[x, 3])
        diagonal = near_sum[x]
        negdiag[x] = -1.5 * diagonal
        scale = STEP / diagonal
        for b in range(2):
            keep_x = (par_x == b).astype(jnp.float32)
            keep_y = (par_y == b).astype(jnp.float32)
            own_z = even if b == 0 else jnp.logical_not(even)
            for side in range(2):
                inner = 4 - side
                vx[b, side, x] = t_x[side] * scale * jnp.where(x == inner, keep_x, 1.0)
                vy[b, side, x] = t_y[side] * scale * jnp.where(row == inner, keep_y, 1.0)
                cut = (lax.rem(lane, E) == inner) & jnp.logical_not(own_z)
                vz[b, side, x] = jnp.where(cut, 0.0, t_z[side] * scale)

    def center_of(k, x):
        return basis[k, :, x + 1, 8:16].reshape(2, 2, 2, E, LANES)

    def flow_x(k, x, side):
        near = basis[k, :, x + 2 * side, 8:16].reshape(2, 2, 2, E, LANES)
        return vx[:, side, x][:, None, None] * near

    def z_ends(k, x, group):
        halo = jnp.where(lax.rem(lane, 2) == 0, z_halo[k, group, 0], z_halo[k, group, 1])
        first = pltpu.roll(halo, lax.rem(LANES - 2 * x, LANES), 1)
        return [first] + [pltpu.roll(halo, LANES - 2 * (n * 8 + x), 1) for n in range(1, 8)]

    def flow_yz(k, x, group, closed=False):
        center = basis[k, :, x + 1, 8:16]
        total = -STEP * center.reshape(2, 2, 2, E, LANES)
        ends = [zero] * 8 if closed else z_ends(k, x, group)
        for side in range(2):
            near = basis[k, :, x + 1, 7 + 2 * side:15 + 2 * side].reshape(2, 2, 2, E, LANES)
            total = total + vy[:, side, x][None, :, None] * near
            edge = lane == (0, 127)[side]
            moved = [
                jnp.where(edge, ends[n], pltpu.roll(center[n], (1, 127)[side], 1)) for n in range(8)
            ]
            near = jnp.stack(moved).reshape(2, 2, 2, E, LANES)
            total = total + vz[:, side, x][None, None] * near
        return total

    def update(k, x, flow):
        center = center_of(k, x)
        support = mk[:, x].astype(jnp.float32).reshape(2, 2, 2, E, LANES)
        change = support * flow
        change_sum = jnp.sum(change, axis=(0, 1, 2))
        fresh = center + change - center * change_sum
        basis[k + 1, :, x + 1, 8:16] = fresh.reshape(8, E, LANES)

    def pack_z(k, x, tiles):
        up, down = tiles
        for s in range(8):
            place = 2 * (s * 8 + x)
            before = lax.rem(place + 127, LANES)
            value = basis[k, s, x + 1, 8:16]
            up = jnp.where(lane == place, pltpu.roll(value, place + 1, 1), up)
            down = jnp.where(lane == before, pltpu.roll(value, before, 1), down)
        return up, down

    def copies(k):
        ref = basis.at[k]
        y_target = basis.at[k % SWEEPS]
        own = pl.ds(8, E)
        sems = [(p_send.at[k, i], p_recv.at[k, i]) for i in range(12)]
        x = [
            Copy(ref.at[:, 8, own], ref.at[:, 0, own], *sems[0], (("gx", 1),)),
            Copy(ref.at[:, 1, own], ref.at[:, 9, own], *sems[1], (("gx", -1),)),
        ] if k == 2 else []
        yz = []
        for group in range(2):
            part_yz = []
            for n, planes in enumerate((pl.ds(2, 6),) if group == 0 else (pl.ds(1, 1), pl.ds(8, 1))):
                at_sem = 2 + 2 * group + 2 * n
                for side, (a, b, d) in enumerate(((15, 7, 1), (8, 16, -1))):
                    part_yz.append(Copy(
                        ref.at[:, planes, pl.ds(a, 1)], y_target.at[:, planes, pl.ds(b, 1)],
                        *sems[at_sem + side], (("gy", d),),
                    ))
            for side, d in ((0, 1), (1, -1)):
                part_yz.append(Copy(
                    z_send.at[k, group, side], z_halo.at[k, group, side],
                    *sems[8 + 2 * group + side], (("gz", d),),
                ))
            yz.append(part_yz)
        return x, yz[0], yz[1]

    def inner_flow(k, x, group=0):
        return flow_yz(k, x, group) + flow_x(k, x, 0) + flow_x(k, x, 1)

    def pack_outer(k):
        tiles = (zero, zero)
        for x in (0, 7):
            tiles = pack_z(k, x, tiles)
        z_send[k, 1, 0], z_send[k, 1, 1] = tiles

    arriving_x, arriving_inner, arriving_outer = copies(1)
    for c in k_yz:
        c.wait_recv()
    for side in range(2):
        for n, tile in enumerate(prepare(7 * side, (1 - side,))):
            a_send[side, n] = tile
    start(h_copies[2:4])

    def first_inner(x, tiles):
        total, t_y, t_z = prepare(x, (0, 1))
        first_values(lambda n: mk[n, x], x + 1, par_x, STEP / total, None, t_y, t_z)
        return pack_z(1, x, tiles)

    tiles = lax.fori_loop(1, 7, first_inner, (zero, zero), unroll=True)
    z_send[1, 0, 0], z_send[1, 0, 1] = tiles
    start(arriving_inner)
    for c in k_x:
        c.wait_recv()
    for side in range(2):
        x = 7 * side
        t_x = harmonic(kx[8 * side], kx[8 * side + 1])
        near_sum[x] = a_send[side, 0] + t_x
        first_values(
            lambda n: mk[n, x], x + 1, par_x, STEP / near_sum[x], t_x, a_send[side, 1], a_send[side, 2]
        )
    pack_outer(1)
    start(arriving_outer)

    def weigh(x, carry):
        weights(x)
        return carry

    lax.fori_loop(0, E, weigh, 0, unroll=True)
    for k in range(1, SWEEPS):
        next_x, next_inner, next_outer = copies(k + 1)
        for c in arriving_inner:
            c.wait_recv()

        def inner(x, tiles):
            update(k, x, inner_flow(k, x))
            return pack_z(k + 1, x, tiles)

        tiles = lax.fori_loop(1, 7, inner, (zero, zero), unroll=True)
        z_send[k + 1, 0, 0], z_send[k + 1, 0, 1] = tiles
        start(next_inner)
        for c in arriving_outer:
            c.wait_recv()
        for x, side in ((0, 1), (7, 0)):
            part[k, 1 - side] = (flow_yz(k, x, 1) + flow_x(k, x, side)).reshape(8, E, LANES)
        if k >= 2:
            start(h_copies[2 * k:2 * k + 2])
        for c in (h_copies[:4], arriving_x, h_copies[4:6])[k - 1]:
            c.wait_recv()
        for side in range(2):
            if k == 1:
                first_halo(side)
            if k == 3:
                next_halo(2, side)
        for x, side in ((0, 0), (7, 1)):
            update(k, x, part[k, side].reshape(2, 2, 2, E, LANES) + flow_x(k, x, side))
        pack_outer(k + 1)
        start(next_outer)
        if k == 1:
            start(next_x)
        arriving_x, arriving_inner, arriving_outer = next_x, next_inner, next_outer

    out = pltpu.make_async_copy(
        basis.at[SWEEPS, :, pl.ds(1, E), pl.ds(8, E)], out_p, out_sem.at[0]
    )
    out.start()

    def split_z(values):
        pair = values.reshape(4, 2, E, LANES)
        return (
            jnp.where(even, pair[:, 0], pair[:, 1]),
            jnp.where(even, pair[:, 1], pair[:, 0]),
        )

    def split_basis(x, carry):
        own, beside = split_z(center_of(SWEEPS, x))
        pz[:, 0, x] = own
        pz[:, 1, x] = beside
        return carry

    lax.fori_loop(0, E, split_basis, 0, unroll=True)
    def image(x, flow):
        own, beside = split_z(flow * negdiag[x])
        iz[:, 0, x] = own
        iz[:, 1, x] = beside

    def closed_image(x, carry):
        image(x, flow_yz(SWEEPS, x, 0, True) + flow_x(SWEEPS, x, 0) + flow_x(SWEEPS, x, 1))
        return carry

    lax.fori_loop(1, 7, closed_image, 0, unroll=True)
    for x, side in ((0, 1), (7, 0)):
        image(x, flow_yz(SWEEPS, x, 0, True) + flow_x(SWEEPS, x, side))

    def pair_of(a_x, a_y):
        return lax.rem(a_x + par_x, 2) * 2 + lax.rem(a_y + par_y, 2)

    def contract(i, carry):
        half, a_x, a_y = i // 4, lax.rem(i // 2, 2), lax.rem(i, 2)
        for a_z in range(2):
            for e in range(8):
                u_xy = pair_of(a_x + e // 4, a_y + e // 2 % 2)
                total = None
                for j in range(4):
                    x = 4 * half + j
                    term = pz[pair_of(a_x, a_y), a_z, x] * iz[u_xy, (a_z + e) % 2, x]
                    total = term if total is None else total + term
                sums[pl.ds(pl.multiple_of((i * 2 + a_z) * 64, 64) + e * 8, E)] = total
        return carry

    lax.fori_loop(0, 8, contract, 0, unroll=2)

    def y_halves(ref, count):
        results = []
        for y_half in range(2):
            total = ref[pl.ds(4 * y_half, count * 8, stride=8)]
            for y in range(1, 4):
                total = total + ref[pl.ds(4 * y_half + y, count * 8, stride=8)]
            results.append(total.reshape(count, E, LANES))
        return results

    def halves(ref, count):
        results = []
        for total in y_halves(ref, count):
            total = total + pltpu.roll(total, 127, 2)
            total = total + pltpu.roll(total, 126, 2)
            results.append(total.reshape(count // 2, 2, E, LANES))
        return results

    low = (lax.rem(lane, E) == 0) & (lane != 0)
    high = (lax.rem(lane, E) == 4) & (lane != 124)

    def merge_z(pair):
        own, beside = pair[:, 0], pair[:, 1]
        own = own + jnp.where(low, pltpu.roll(beside, 4, 2), 0.0)
        return own + jnp.where(high, pltpu.roll(beside, 124, 2), 0.0)

    def pack_rows(entries):
        up, down = zero, zero
        for place, beside in entries:
            up = jnp.where(lane == place, pltpu.roll(beside, place + 4, 1), up)
            moved = pltpu.roll(beside, place, 1) if place else beside
            down = jnp.where(lane == place, moved, down)
        return up, down

    row_copies = []

    def move_rows(src, dst, moves):
        n = len(row_copies)
        row_copies.append(Copy(src, dst, r_send.at[n], r_recv.at[n], tuple(m for m in moves if m[1])))

    quarter = halves(sums, 16)
    entries = []
    for i in range(8):
        half, a_x, a_y = i // 4, i // 2 % 2, i % 2
        for y_half in range(2):
            place = (a_x * 2 + a_y) * 32 + (half ^ a_x) * 2 + (y_half ^ a_y)
            entries.append((place, quarter[y_half][i, 1]))
    zr_send[0], zr_send[1] = pack_rows(entries)
    order = [(m_x, m_y) for m_x in (1, -1, 0) for m_y in (1, -1, 0)]
    for side, m_z in ((0, 1), (1, -1)):
        for m_x, m_y in order:
            move_rows(
                zr_send.at[side], zr_halo.at[side, m_x + 1, m_y + 1],
                (("gx", m_x), ("gy", m_y), ("gz", m_z)),
            )
    start(row_copies)
    for y_half in range(2):
        merged = merge_z(quarter[y_half])
        for i in range(8):
            rows[i // 2 % 2, i % 2, i // 4, y_half] = merged[i]
    first = len(row_copies)
    for side, d in ((0, 1), (1, -1)):
        for side_y, d_y in ((0, 1), (1, -1)):
            move_rows(
                rows.at[1, 1, 1 - side, 1 - side_y], rows_d.at[side, side_y], (("gx", d), ("gy", d_y))
            )
    for side, d in ((0, 1), (1, -1)):
        move_rows(rows.at[1, 0, 1 - side], rows_x.at[side], (("gx", d),))
        move_rows(rows.at[0, 1, :, 1 - side], rows_y.at[side], (("gy", d),))
    start(row_copies[first:])
    first = len(row_copies)

    flat = basis.reshape((SWEEPS + 1) * 8 * 240, LANES)
    flat_t = t_yz.reshape(E * 4 * E, LANES)
    def z_faces(planes):
        for x in planes:
            ends = jnp.stack(z_ends(SWEEPS, x, 1 if x in (0, 7) else 0))
            for n, tiles in enumerate(split_z(ends)):
                z_near[:, n, x] = tiles
                z_near_w[:, n, x] = tiles * z_weight(x)

    def z_weight(x):
        return -jnp.where(lane == 0, t_yz[x, 2], jnp.where(lane == 127, t_yz[x, 3], 0.0))

    def contract_z(first_planes, i, carry):
        half, a_x, a_y = i // 4, lax.rem(i // 2, 2), lax.rem(i, 2)
        s_xy = pair_of(a_x, a_y)
        planes = [1 + 3 * half + j for j in range(3)] if first_planes else [7 * half]
        for e in range(8):
            u_xy = pair_of(a_x + e // 4, a_y + e // 2 % 2)
            place = pl.ds(pl.multiple_of(i * 64, 64) + e * 8, E)
            total = None if first_planes else z_sums[place]
            for x in planes:
                term = pz[s_xy, 0, x] * z_near_w[u_xy, e % 2, x] + z_near[s_xy, 0, x] * z_own_w[u_xy, e % 2, x]
                total = term if total is None else total + term
            z_sums[place] = total
        return carry

    for x in range(E):
        for n in range(2):
            z_own_w[:, n, x] = pz[:, n, x] * z_weight(x)
    for c in arriving_inner:
        c.wait_recv()
    z_faces(range(1, 7))
    lax.fori_loop(0, 8, functools.partial(contract_z, True), 0, unroll=2)
    for c in arriving_outer:
        c.wait_recv()
    for side in range(2):
        weight = -flat_t[pl.ds(side * 15, E, stride=32)]
        for n, (k, y_row) in enumerate(((SWEEPS, 8 + 7 * side), (0, 7 + 9 * side))):
            tiles = jnp.stack([flat[pl.ds((k * 8 + m) * 240 + 24 + y_row, E, stride=24)] for m in range(8)])
            own, beside = split_z(tiles)
            y_faces[side, n, 0, :, 0] = own
            y_faces[side, n, 0, :, 1] = beside
            y_faces[side, n, 1, :, 0] = own * weight
            y_faces[side, n, 1, :, 1] = beside * weight

    def contract_y(i, carry):
        side, a_x = i // 2, lax.rem(i, 2)
        s_xy = pair_of(a_x, 0)
        for a_z in range(2):
            for e in range(8):
                u_xy = pair_of(a_x + e // 4, e // 2 % 2)
                u_z = (a_z + e) % 2
                total = y_faces[side, 0, 0, s_xy, a_z] * y_faces[side, 1, 1, u_xy, u_z]
                total = total + y_faces[side, 1, 0, s_xy, a_z] * y_faces[side, 0, 1, u_xy, u_z]
                y_sums[pl.ds(pl.multiple_of((i * 2 + a_z) * 64, 64) + e * 8, E)] = total
        return carry

    lax.fori_loop(0, 4, contract_y, 0, unroll=True)
    y_quarter = halves(y_sums, 8)
    entries = []
    for i in range(4):
        side, a_x = i // 2, i % 2
        for x_half in range(2):
            entries.append((a_x * 64 + (x_half ^ a_x) * 2 + side, y_quarter[x_half][i, 1]))
    zg_send[0], zg_send[1] = pack_rows(entries)
    for side, m_z in ((0, 1), (1, -1)):
        for m_x in (1, -1, 0):
            move_rows(zg_send.at[side], zg_halo.at[side, m_x + 1], (("gx", m_x), ("gz", m_z)))
    start(row_copies[first:])
    first = len(row_copies)

    z_faces((0, 7))
    lax.fori_loop(0, 8, functools.partial(contract_z, False), 0, unroll=2)
    z_quarter = y_halves(z_sums, 8)
    y_merged = [merge_z(part_of) for part_of in y_quarter]
    for y_half in range(2):
        tiles = jnp.where(lane == 0, z_quarter[y_half], 0.0)
        tiles = tiles + jnp.where(lane == 124, pltpu.roll(z_quarter[y_half], 125, 2), 0.0)
        for i in range(8):
            half, a_x, a_y = i // 4, i // 2 % 2, i % 2
            tile = tiles[i] if a_y else tiles[i] + y_merged[half][y_half * 2 + a_x]
            rows2[a_x, a_y, half, y_half] = tile
    for side, d in ((0, 1), (1, -1)):
        for side_y, d_y in ((0, 1), (1, -1)):
            move_rows(
                rows2.at[1, 1, 1 - side, 1 - side_y], rows2_d.at[side, side_y], (("gx", d), ("gy", d_y))
            )
    for side, d in ((0, 1), (1, -1)):
        move_rows(rows2.at[1, 0, 1 - side], rows2_x.at[side], (("gx", d),))
        move_rows(rows2.at[0, 1, :, 1 - side], rows2_y.at[side], (("gy", d),))
    start(row_copies[first:])
    first = len(row_copies)

    for c in h_copies[6:]:
        c.wait_recv()
    for side in range(2):
        next_halo(3, side)
        x = 7 * side
        weight = vx[0, side, x] * negdiag[x]
        for n, plane in enumerate((x + 1, 9 * side)):
            own, beside = split_z(basis[SWEEPS, :, plane, 8:16])
            faces[side, n, 0, :, 0] = own
            faces[side, n, 0, :, 1] = beside
            faces[side, n, 1, :, 0] = own * weight
            faces[side, n, 1, :, 1] = beside * weight

    def contract_faces(i, carry):
        side, a_y = i // 2, lax.rem(i, 2)
        s_xy = pair_of(0, a_y)
        for a_z in range(2):
            for e in range(8):
                u_xy = pair_of(e // 4, a_y + e // 2 % 2)
                u_z = (a_z + e) % 2
                total = faces[side, 0, 0, s_xy, a_z] * faces[side, 1, 1, u_xy, u_z]
                total = total + faces[side, 1, 0, s_xy, a_z] * faces[side, 0, 1, u_xy, u_z]
                face_sums[pl.ds(pl.multiple_of((i * 2 + a_z) * 64, 64) + e * 8, E)] = total
        return carry

    lax.fori_loop(0, 4, contract_faces, 0, unroll=True)
    quarter = halves(face_sums, 8)
    entries = []
    for i in range(4):
        half, a_y = i // 2, i % 2
        for y_half in range(2):
            entries.append((a_y * 32 + half * 2 + (y_half ^ a_y), quarter[y_half][i, 1]))
    zf_send[0], zf_send[1] = pack_rows(entries)
    for side, m_z in ((0, 1), (1, -1)):
        for m_y in (1, -1, 0):
            move_rows(zf_send.at[side], zf_halo.at[side, m_y + 1], (("gy", m_y), ("gz", m_z)))
    start(row_copies[first:])
    first = len(row_copies)
    face_own = []
    for y_half in range(2):
        merged = merge_z(quarter[y_half])
        face_own.append((merged[0], merged[2]))
        face_rows[y_half, 0], face_rows[y_half, 1] = merged[1], merged[3]
    for side, d in ((0, 1), (1, -1)):
        move_rows(face_rows.at[1 - side], face_rows_y.at[side], (("gy", d),))
    start(row_copies[first:])

    for c in row_copies:
        c.wait_recv()
    whole = [
        [
            rows[0, 0, h, y] + rows_x[h, y] + rows_y[y, h] + rows_d[h, y] + face_own[y][h] + face_rows_y[y, h]
            + (rows2[0, 0, h, y] + rows2_x[h, y] + rows2_y[y, h] + rows2_d[h, y])
            for y in range(2)
        ]
        for h in range(2)
    ]
    for side in range(2):
        packed = zero
        for m_x, m_y in order:
            inside = lane - 32 * (2 * abs(m_x) + abs(m_y))
            takes = (inside >= 0) & (inside < 4)
            if m_x:
                takes = takes & (inside // 2 == (1 - m_x) // 2)
            if m_y:
                takes = takes & (lax.rem(inside, 2) == (1 - m_y) // 2)
            value = zr_halo[side, m_x + 1, m_y + 1]
            if m_x == 0:
                value = value + zf_halo[side, m_y + 1]
            if m_y == 0:
                value = value + zg_halo[side, m_x + 1]
            packed = packed + jnp.where(takes, value, 0.0)
        target = 124 * side
        for h in range(2):
            for y in range(2):
                total = None
                for group in range(4):
                    shift = (target - group * 32 - (h * 2 + y)) % LANES
                    moved = pltpu.roll(packed, shift, 1) if shift else packed
                    total = moved if total is None else total + moved
                whole[h][y] = whole[h][y] + jnp.where(lane == target, total, 0.0)
    tiles = jnp.stack([whole[0][0], whole[0][1], whole[1][0], whole[1][1]])

    def gather(offset):
        values = tiles
        for step, (spread, size) in enumerate(((7, 1), (28, 4))):
            result = None
            for n in range(4):
                shift = (LANES - spread * n - (0 if step else offset)) % LANES
                moved = pltpu.roll(values, shift, 2) if shift else values
                here = lax.rem(lane, 32) == n if step == 0 else lane // 4 == n
                result = moved if result is None else jnp.where(here, moved, result)
            values = result
        return values

    lows, highs = gather(0), gather(4)
    picks = {0: ((0,), 1), 1: ((0, 1), 0), 2: ((1,), 1)}
    for d_x in range(3):
        for d_y in range(3):
            (halves_x, e_x), (halves_y, e_y) = picks[d_x], picks[d_y]
            low_tile, high_tile = None, None
            for h in halves_x:
                for y in halves_y:
                    n = h * 2 + y
                    low_tile = lows[n] if low_tile is None else low_tile + lows[n]
                    high_tile = highs[n] if high_tile is None else high_tile + highs[n]
            e = e_x * 4 + e_y * 2
            out_c[d_x, d_y, 0, 0, 0:1] = low_tile[e + 1:e + 2, :16]
            out_c[d_x, d_y, 1, 0, 0:1] = low_tile[e:e + 1, :16] + high_tile[e:e + 1, :16]
            out_c[d_x, d_y, 2, 0, 0:1] = high_tile[e + 1:e + 2, :16]
    out.wait()
    for c in started:
        c.wait_send()


def hand_over(p_ref, c_ref, out_p, out_c, sem):
    copies = [
        pltpu.make_async_copy(p_ref, out_p, sem.at[0]),
        pltpu.make_async_copy(c_ref, out_c, sem.at[1]),
    ]
    for copy in copies:
        copy.start()
    for copy in copies:
        copy.wait()


def shards(permeability, well_flags, support_mask):
    f32 = jnp.float32
    vmem = pltpu.VMEM
    dma = pltpu.SemaphoreType.DMA
    any_spec = pl.BlockSpec(memory_space=pltpu.HBM)
    prolongation, coarse = pl.pallas_call(
        kernel,
        out_shape=(
            pltpu.VMEM((8, E, E, LANES), f32),
            pltpu.VMEM((3, 3, 3, 1, 1, 16), f32),
        ),
        in_specs=[any_spec] * 3,
        out_specs=(pl.BlockSpec(memory_space=pltpu.VMEM), pl.BlockSpec(memory_space=pltpu.VMEM)),
        scratch_shapes=[
            vmem((10, E, LANES), f32),
            vmem((E, 24, LANES), f32),
            vmem((E, E, LANES), f32),
            vmem((2, E, LANES), f32),
            vmem((2, E, LANES), f32),
            vmem((E, E, LANES), jnp.int32),
            vmem((8, E, E, LANES), jnp.int32),
            vmem((SWEEPS + 1, 8, 10, 24, LANES), f32),
            vmem((SWEEPS + 1, 2, 2, E, LANES), f32),
            vmem((SWEEPS + 1, 2, 2, E, LANES), f32),
            vmem((2, 2, E, E, LANES), f32),
            vmem((2, 2, E, E, LANES), f32),
            vmem((2, 2, E, E, LANES), f32),
            vmem((E, E, LANES), f32),
            vmem((SWEEPS, 2, 8, E, LANES), f32),
            vmem((4, 2, E, E, LANES), f32),
            vmem((4, 2, E, E, LANES), f32),
            vmem((1024, LANES), f32),
            vmem((2, 2, 2, 2, E, LANES), f32),
            vmem((2, 2, E, LANES), f32),
            vmem((2, 2, E, LANES), f32),
            vmem((2, 2, E, LANES), f32),
            vmem((2, E, LANES), f32),
            vmem((2, 3, 3, E, LANES), f32),
            vmem((2, 2, 2, 4, 2, E, LANES), f32),
            vmem((512, LANES), f32),
            vmem((2, 2, E, LANES), f32),
            vmem((2, 2, E, LANES), f32),
            vmem((2, E, LANES), f32),
            vmem((2, 3, E, LANES), f32),
            vmem((2, 3, E, LANES), f32),
            vmem((2, 3, E, LANES), f32),
            vmem((2, 8, E, LANES), jnp.int32),
            vmem((2, 2, 8, E, LANES), f32),
            vmem((2, E, LANES), f32),
            vmem((E, 4, E, LANES), f32),
            vmem((E, E, LANES), f32),
            vmem((2, 2, 2, 4, 2, E, LANES), f32),
            vmem((512, LANES), f32),
            vmem((4, 2, E, E, LANES), f32),
            vmem((4, 2, E, E, LANES), f32),
            vmem((4, 2, E, E, LANES), f32),
            vmem((512, LANES), f32),
            vmem((2, 2, 2, 2, E, LANES), f32),
            vmem((2, 2, E, LANES), f32),
            vmem((2, 2, E, LANES), f32),
            vmem((2, 2, E, LANES), f32),
            vmem((2, E, LANES), f32),
            vmem((2, 3, E, LANES), f32),
            dma((5,)),
            dma((6,)),
            dma((6,)),
            dma((SWEEPS + 1, 12)),
            dma((SWEEPS + 1, 12)),
            dma((48,)),
            dma((48,)),
            dma((8,)),
            dma((8,)),
            dma((1,)),
        ],
        compiler_params=pltpu.CompilerParams(
            collective_id=0, has_side_effects=True, vmem_limit_bytes=60 * 1024 * 1024
        ),
        name="smooth_and_contract",
    )(permeability, well_flags, support_mask)
    hbm_spec = pl.BlockSpec(memory_space=pltpu.HBM)
    return pl.pallas_call(
        hand_over,
        out_shape=(
            jax.ShapeDtypeStruct((8, E, E, LANES), f32),
            jax.ShapeDtypeStruct((3, 3, 3, 1, 1, 16), f32),
        ),
        in_specs=[pl.BlockSpec(memory_space=pl.ANY)] * 2,
        out_specs=(hbm_spec, hbm_spec),
        scratch_shapes=[dma((2,))],
        compiler_params=pltpu.CompilerParams(vmem_limit_bytes=4 * 1024 * 1024),
        name="hand_over",
    )(prolongation, coarse)


def solution(mesh):
    placed = (P(None, "gx", "gy", "gz"), P("gx", "gy", "gz"), P(None, "gx", "gy", "gz"))
    return jax.shard_map(
        shards,
        mesh=mesh,
        in_specs=placed,
        out_specs=(P(None, "gx", "gy", "gz"), P(None, None, None, "gx", "gy", "gz")),
        check_vma=False,
    )
```
